256 devices in a mesh: coarse: 16 (over z_hi, y), fine: 16 (over z_lo, x, core).
Axes of the slice: x: 4, y: 4, z: 8 (z_hi: 4, z_lo: 2; z = z_hi * 2 + z_lo), core: 2. Of those that a mesh axis runs over, the one named last changes fastest.
Arguments:
- right_side: float32 [128, 128, 128], P('coarse', 'fine'), may hold values from -6 to 6
- coefficient_index: int32 [128, 128, 128], P('coarse', 'fine'), may hold values from 0 to 15
- material_coefficients: float32 [16], replicated, may hold values from 0.02 to 0.5
- block_cells: int32 [16, 16, 64, 128], P('coarse', 'fine'), may hold values from 0 to 8191, as said below
- block_inverses: float32 [16, 16, 64, 128, 128], P('coarse', 'fine'), as said below
- aggregate_map: int32 [128, 128, 128], P('coarse', 'fine'), may hold values from 0 to 15, as said below
- coarse_diagonal: float32 [16, 16, 16], P('coarse', 'fine'), may hold values from 0.1 to 8
Outputs:
- solution: float32 [128, 128, 128], P('coarse', 'fine')
- residual: float32 [128, 128, 128], P('coarse', 'fine')
- direction: float32 [128, 128, 128], P('coarse', 'fine')
The draws below stay inside these ranges and needn't reach their ends.
Inputs may be any that keep to these rules, and one draw needn't show every extreme that they name: `block_cells`: each device block's 64 x 128 entries list each of its local cell numbers exactly once. `block_inverses`: every 128 x 128 matrix is symmetric positive definite. A cell with third index j has aggregate_map equal to j // 8 - 1, j // 8 or j // 8 + 1.
All inputs are finite; a program needn't handle non-finite values.
Results may differ from the reference program's by a relative error of at most 0.00016.
Values sent between devices are 32-bit elements; how exact they have to be, the bound alone decides.
No kernel may reach another device: no remote copies, remote signals or barrier semaphores. Data moves between devices by JAX's collectives and lax.ppermute only.
A program may use at most 64 MiB of HBM per device.

```python
import math
import jax
import jax.numpy as jnp
from jax import lax

AGG = 8
NY = 128
BS = 128
MATERIALS = 16
ITERS = 2
SWEEPS = 4
OWNERS = 16
MEMBERS = 16
NX = 128
NZ = 128
MY = 16
NBLK = 64


def draw_right_side(key, part):
    first = jax.random.fold_in(key, 0)
    xs = jnp.arange(NX, dtype=jnp.float32)[:, None, None]
    zs = jnp.arange(NZ, dtype=jnp.float32)[None, :, None]
    scale = 0.6 + 1.2 * (xs + zs) / (NX + NZ - 2)
    rough = jnp.clip(jax.random.normal(first, (NX, NZ, NY), jnp.float32), -3.3, 3.3)
    return rough * scale


def draw_aggregate_map(key, part):
    ys = jnp.arange(NY, dtype=jnp.int32)[None, None, :]
    moves = jax.random.randint(key, (NX, NZ, NY), -3, 4, dtype=jnp.int32)
    return jnp.clip(ys + moves, 0, NY - 1) // AGG


def draw_block_cells(key, part):
    keys = jax.random.split(key, OWNERS * MEMBERS)
    cells = AGG * AGG * NY

    def one_device(single):
        return jax.random.permutation(single, cells)
    orders = jax.vmap(one_device)(keys)
    return orders.astype(jnp.int32).reshape(OWNERS, MEMBERS, NBLK, BS)


def draw_block_inverses(key, part):
    spread, lowest, highest = (0.3, 0.3, 3.0)

    def one_owner(owner):
        base = jax.random.fold_in(key, owner)
        left, right = jax.random.split(base)
        noise = jax.random.normal(left, (MEMBERS, NBLK, BS, BS), jnp.float32) * (spread / math.sqrt(2.0 * BS))
        eye = jnp.eye(BS, dtype=jnp.float32)
        symmetric = (noise + jnp.swapaxes(noise, -1, -2)) * (1.0 - eye)
        scales = jnp.exp(jax.random.uniform(right, (MEMBERS, NBLK, BS), jnp.float32, math.log(lowest), math.log(highest)))
        root = jnp.sqrt(scales)
        return (eye + symmetric) * root[..., :, None] * root[..., None, :]
    return lax.map(one_owner, jnp.arange(OWNERS, dtype=jnp.int32))


def touch_ends(values, stream_key, least, top_value):
    longest = values.shape.index(max(values.shape))
    spots = []
    for shift in (0, 1):
        where = [jax.random.randint(jax.random.fold_in(stream_key, axis), (), 0, length) for axis, length in enumerate(values.shape)]
        where[longest] = (where[longest] + shift) % values.shape[longest]
        spots.append(tuple(where))
    return values.at[spots[0]].set(least).at[spots[1]].set(top_value)


def block_scale(rng, shape, shards, least, top_value):
    loudness = 1.0
    for position, blocks in shards:
        steps = jax.random.uniform(jax.random.fold_in(jax.random.fold_in(rng, 6), position), (blocks,), jnp.float32, least / len(shards), top_value / len(shards))
        loudness = loudness * jnp.repeat(jnp.exp(steps), shape[position] // blocks).reshape((-1,) + (1,) * (len(shape) - 1 - position))
    return loudness


def setup_inputs(seed: int = 0) -> dict:
    arg_keys = jax.random.split(jax.random.key(seed), 8)
    return {
        "right_side": draw_right_side(jax.random.fold_in(arg_keys[7], 71), 0),
        "coefficient_index": touch_ends(jax.random.randint(arg_keys[1], (NX, NZ, NY), 0, MATERIALS), jax.random.fold_in(arg_keys[1], 1), 0, MATERIALS - 1).astype(jnp.int32),
        "material_coefficients": jnp.clip(jnp.exp(jax.random.uniform(arg_keys[2], (MATERIALS,), jnp.float32, math.log(0.02), math.log(0.5))), 0.02, 0.5),
        "block_cells": draw_block_cells(jax.random.fold_in(arg_keys[7], 71), 0),
        "block_inverses": draw_block_inverses(jax.random.fold_in(arg_keys[7], 71), 0),
        "aggregate_map": draw_aggregate_map(jax.random.fold_in(arg_keys[7], 71), 0),
        "coarse_diagonal": jnp.clip(jnp.exp(math.log(8.0) - 4.3820266 * jax.random.uniform(arg_keys[6], (OWNERS, MEMBERS, MY), jnp.float32) ** block_scale(arg_keys[6], (OWNERS, MEMBERS, MY), ((0, 16), (1, 16)), -0.2, 0.2)), 0.1, 8.0),
    }


omega = 0.8
restrict_scale = 0.25


def neighbours():
    result = []
    for shift_x in (-1, 0, 1):
        for shift_z in (-1, 0, 1):
            for shift_y in (-1, 0, 1):
                reach = abs(shift_x) + abs(shift_z) + abs(shift_y)
                if reach > 0:
                    result.append((shift_x, shift_z, shift_y, 0.5 ** (reach - 1)))
    return result


def window(padded, shift_x, shift_z, shift_y, shape):
    return padded[1 + shift_x:1 + shift_x + shape[0], 1 + shift_z:1 + shift_z + shape[1], 1 + shift_y:1 + shift_y + shape[2]]


def fine_operate(field, kappa):
    padded = jnp.pad(field, 1)
    kappa_wide = jnp.pad(kappa, 1)
    total = jnp.zeros(field.shape, jnp.float32)
    for shift_x, shift_z, shift_y, weight in neighbours():
        near_field = window(padded, shift_x, shift_z, shift_y, field.shape)
        near_kappa = window(kappa_wide, shift_x, shift_z, shift_y, field.shape)
        total = total + (weight * 0.5) * (kappa + near_kappa) * (field - near_field)
    return total


def to_local(field):
    return field.reshape(OWNERS, AGG, MEMBERS, AGG, NY).transpose(0, 2, 1, 3, 4).reshape(OWNERS * MEMBERS, AGG * AGG * NY)


def from_local(flat):
    return flat.reshape(OWNERS, MEMBERS, AGG, AGG, NY).transpose(0, 2, 1, 3, 4).reshape(OWNERS * AGG, MEMBERS * AGG, NY)


def block_apply(residual, block_inverses, block_cells):
    local = to_local(residual)
    orders = block_cells.reshape(OWNERS * MEMBERS, NBLK, BS)
    matrices = block_inverses.reshape(OWNERS * MEMBERS, NBLK, BS, BS)

    def one_device(items):
        vector, order, matrix = items
        picked = vector[order]
        product = jnp.einsum("bij,bj->bi", matrix, picked, precision=lax.Precision.HIGHEST)
        return jnp.zeros(vector.shape, jnp.float32).at[order.reshape(-1)].set(product.reshape(-1))

    return from_local(lax.map(one_device, (local, orders, matrices)))


def segment_numbers(aggregate_map):
    base = jnp.arange(OWNERS * MEMBERS, dtype=jnp.int32) * MY
    return to_local(aggregate_map) + base[:, None]


def coarse_operate(guess, diagonal):
    padded = jnp.pad(guess, 1)
    beside = padded[2:, 1:-1, 1:-1] + padded[:-2, 1:-1, 1:-1]
    beside = beside + padded[1:-1, 2:, 1:-1] + padded[1:-1, :-2, 1:-1]
    beside = beside + padded[1:-1, 1:-1, 2:] + padded[1:-1, 1:-1, :-2]
    return (6.0 + diagonal) * guess - beside


def precondition(residual, block_inverses, block_cells, segments, coarse_diagonal):
    smoothed = block_apply(residual, block_inverses, block_cells)
    sums = jax.ops.segment_sum(to_local(residual).reshape(-1), segments.reshape(-1), num_segments=OWNERS * MEMBERS * MY)
    source = restrict_scale * sums.reshape(OWNERS, MEMBERS, MY)
    guess = jnp.zeros(source.shape, jnp.float32)
    for sweep in range(SWEEPS):
        guess = guess + omega * (source - coarse_operate(guess, coarse_diagonal)) / (6.0 + coarse_diagonal)
    correction = from_local(guess.reshape(-1)[segments])
    return smoothed + correction


def reference(right_side, coefficient_index, material_coefficients, block_cells, block_inverses, aggregate_map, coarse_diagonal):
    kappa = material_coefficients[coefficient_index]
    segments = segment_numbers(aggregate_map)
    solution = jnp.zeros(right_side.shape, jnp.float32)
    residual = right_side
    smoothed = precondition(residual, block_inverses, block_cells, segments, coarse_diagonal)
    current = jnp.sum(residual * smoothed)
    search = smoothed
    for step in range(ITERS):
        image = fine_operate(search, kappa)
        alpha = current / jnp.sum(search * image)
        solution = solution + alpha * search
        residual = residual - alpha * image
        smoothed = precondition(residual, block_inverses, block_cells, segments, coarse_diagonal)
        following = jnp.sum(residual * smoothed)
        search = smoothed + (following / current) * search
        current = following
    return solution, residual, search
```

```python
import functools

import jax
import jax.numpy as jnp
from jax import lax
from jax.experimental import pallas as pl
from jax.experimental.pallas import tpu as pltpu
from jax.sharding import PartitionSpec as P

AGG = 8
COARSE, FINE = "coarse", "fine"
SWEEPS = 4
OMEGA = 0.8
SIDE = 16
ROWS = 64
LANES = 128
WIDE = SIDE * SIDE
F32 = jnp.float32

SLAB = 16
RIGHT, LEFT = 8, 15


def vmem():
    return pl.BlockSpec(memory_space=pltpu.VMEM)


def smem():
    return pl.BlockSpec(memory_space=pltpu.SMEM)


def anywhere():
    return pl.BlockSpec(memory_space=pl.ANY)


def params():
    return pltpu.CompilerParams(vmem_limit_bytes=24 * 1024 * 1024)


def shape(*dims, dtype=F32):
    return jax.ShapeDtypeStruct(dims, dtype)


def iota(dims, axis):
    return lax.broadcasted_iota(jnp.int32, dims, axis)


def take_lanes(values, lanes):
    numbers = lax.GatherDimensionNumbers(
        offset_dims=(),
        collapsed_slice_dims=(1,),
        start_index_map=(1,),
        operand_batching_dims=(0,),
        start_indices_batching_dims=(0,),
    )
    return lax.gather(
        values,
        lanes[..., None],
        numbers,
        slice_sizes=(1, 1),
        mode=lax.GatherScatterMode.PROMISE_IN_BOUNDS,
    )


def permute(source_ref, index_ref, target_ref):
    rows = [index_ref[8 * g : 8 * g + 8, :] // LANES for g in range(8)]
    lanes = [index_ref[8 * g : 8 * g + 8, :] % LANES for g in range(8)]

    def body(step, picked):
        for part in range(8):
            row = step * 8 + part
            source = jnp.broadcast_to(source_ref[pl.ds(row, 1), :], (8, LANES))
            picked = tuple(
                jnp.where(rows[g] == row, take_lanes(source, lanes[g]), picked[g])
                for g in range(8)
            )
        return picked

    zero = jnp.zeros((8, LANES), F32)
    picked = lax.fori_loop(0, ROWS // 8, body, (zero,) * 8)
    for g in range(8):
        target_ref[8 * g : 8 * g + 8, :] = picked[g]


def multiply_blocks(matrices_ref, picked_ref, product_ref):
    def body(group, carry):
        start = pl.multiple_of(group * 8, 8)
        columns = jnp.transpose(picked_ref[pl.ds(start, 8), :])
        rows = []
        for part in range(8):
            matrix = matrices_ref[group * 8 + part].reshape(16, 8, LANES)
            column = columns[:, part : part + 1].reshape(16, 8, 1)
            total = jnp.sum(matrix * column, axis=0)
            rows.append(jnp.sum(total, axis=0, keepdims=True))
        product_ref[pl.ds(start, 8), :] = jnp.concatenate(rows, axis=0)
        return carry

    lax.fori_loop(0, ROWS // 8, body, 0)


def invert(order_ref):
    cell_rows = iota((ROWS, LANES), 0)
    cell_lanes = iota((LANES, LANES), 0)
    slots = iota((ROWS, LANES), 1).astype(F32)

    def body(block, total):
        entry = order_ref[pl.ds(block, 1), :]
        hit = cell_rows == entry // LANES
        numbers = jnp.concatenate(
            [jnp.where(hit, block.astype(F32), 0.0), jnp.where(hit, slots, 0.0)], axis=0
        ).astype(jnp.bfloat16)
        lanes = jnp.where(cell_lanes == entry % LANES, 1.0, 0.0).astype(jnp.bfloat16)
        return total + lax.dot_general(
            numbers, lanes, (((1,), (1,)), ((), ())), preferred_element_type=F32
        )

    total = lax.fori_loop(0, ROWS, body, jnp.zeros((LANES, LANES), F32))
    return (total[:ROWS] * float(LANES) + total[ROWS:]).astype(jnp.int32)


def restrict(field, offset, member):
    total = jnp.sum(jnp.where(offset == 0, field, 0.0), axis=0, keepdims=True)
    up = jnp.sum(jnp.where(offset == 1, field, 0.0), axis=0, keepdims=True)
    down = jnp.sum(jnp.where(offset == -1, field, 0.0), axis=0, keepdims=True)
    total, up, down = (jnp.broadcast_to(x, (8, LANES)) for x in (total, up, down))
    total = total + pltpu.roll(up, AGG, 1) + pltpu.roll(down, LANES - AGG, 1)
    for distance in (1, 2, 4):
        total = total + pltpu.roll(total, LANES - distance, 1)
    lane = iota((8, LANES), 1)
    total = 0.25 * take_lanes(total, (lane % SIDE) * AGG)
    return jnp.where(lane // SIDE == member % 8, total, 0.0)


def half_rows(values, member):
    return jnp.where(iota((8, LANES), 0) == member // 8, values, 0.0)


def moved(values, distance, axis, keep):
    size = values.shape[axis]
    return jnp.where(keep, pltpu.roll(values, distance % size, axis), 0.0)


def coarse_solve(source, diagonal):
    owner, lane = iota((SIDE, WIDE), 0), iota((SIDE, WIDE), 1)
    cell = lane % SIDE
    weight = OMEGA / (6.0 + diagonal)
    guess = weight * source
    for sweep in range(SWEEPS - 1):
        beside = moved(guess, 1, 0, owner > 0) + moved(guess, -1, 0, owner < SIDE - 1)
        beside = beside + moved(guess, SIDE, 1, lane >= SIDE)
        beside = beside + moved(guess, -SIDE, 1, lane < WIDE - SIDE)
        beside = beside + moved(guess, 1, 1, cell > 0) + moved(guess, -1, 1, cell < SIDE - 1)
        guess = (1.0 - OMEGA) * guess + weight * (source + beside)
    return guess


def nearby(coarse, member, rows_ref):
    rows_ref[...] = pltpu.roll(coarse, lax.rem((SIDE + 1 - member) * SIDE, WIDE), 1)[:, :LANES]


def smooth(slabs):
    total = slabs[1:9] + 0.5 * (slabs[0:8] + slabs[2:10])
    planes = []
    lane = iota((8, LANES), 1)
    row = iota((8, LANES), 0)
    for plane in range(8):
        own, ends = total[plane, :8], total[plane, 8:]
        before = jnp.where(row == 0, ends[LEFT - 8 :, :], pltpu.roll(own, 1, 0))
        after = jnp.where(row == 7, ends[:1, :], pltpu.roll(own, 7, 0))
        own = own + 0.5 * (before + after)
        below = jnp.where(lane > 0, pltpu.roll(own, 1, 1), 0.0)
        above = jnp.where(lane < LANES - 1, pltpu.roll(own, LANES - 1, 1), 0.0)
        planes.append(own + 0.5 * (below + above))
    return jnp.stack(planes)


def position():
    return lax.axis_index(COARSE), lax.axis_index(FINE)


def put_faces(field_ref, pieces_ref, row, member):
    pieces_ref[jnp.maximum(member - 1, 0), row : row + 8, :] = field_ref[
        pl.ds(0, 8, stride=8), :
    ]
    pieces_ref[jnp.minimum(member + 1, SIDE - 1), row : row + 8, :] = field_ref[
        pl.ds(7, 8, stride=8), :
    ]


def get_faces(pieces_ref, row, member, outside):
    left = pieces_ref[jnp.maximum(member - 1, 0), row : row + 8, :]
    right = pieces_ref[jnp.minimum(member + 1, SIDE - 1), row : row + 8, :]
    left = jnp.where(member > 0, left, outside)
    right = jnp.where(member < SIDE - 1, right, outside)
    return left, right


def fill_slabs(slabs_ref, field_ref, faces_ref, ends_ref, face_row, end_row, halo_row, outside):
    owner, member = position()
    left, right = get_faces(faces_ref, face_row, member, outside)
    gap = jnp.full((8, LANES), outside, F32)
    for plane in range(8):
        slabs_ref[plane + 1, :8, :] = field_ref[8 * plane : 8 * plane + 8, :]
        slabs_ref[plane + 1, 8:, :] = gap
        slabs_ref[plane + 1, RIGHT : RIGHT + 1, :] = right[plane : plane + 1, :]
        slabs_ref[plane + 1, LEFT : LEFT + 1, :] = left[plane : plane + 1, :]
    for plane, there, inside in (
        (0, jnp.maximum(owner - 1, 0), owner > 0),
        (9, jnp.minimum(owner + 1, SIDE - 1), owner < SIDE - 1),
    ):
        slabs_ref[plane, 8:, :] = gap
        slabs_ref[plane, :8, :] = jnp.where(
            inside, ends_ref[there, end_row : end_row + 8, :], outside
        )
        halo = jnp.where(inside, ends_ref[there, halo_row : halo_row + 2, :], outside)
        slabs_ref[plane, LEFT : LEFT + 1, :] = halo[0:1, :]
        slabs_ref[plane, RIGHT : RIGHT + 1, :] = halo[1:2, :]


def add_prolonged(slabs_ref, numbers_ref, rows_ref):
    owner, member = position()
    for plane in range(10):
        if plane == 0:
            there = jnp.maximum(owner - 1, 0)
        elif plane == 9:
            there = jnp.minimum(owner + 1, SIDE - 1)
        else:
            there = owner
        row = jnp.broadcast_to(rows_ref[pl.ds(there, 1), :], (8, LANES))
        for part in (0, 8):
            number = numbers_ref[plane, part : part + 8, :]
            value = take_lanes(row, jnp.maximum(number, 0))
            slabs_ref[plane, part : part + 8, :] += jnp.where(number >= 0, value, 0.0)


def operate(field, kappa):
    own, own_kappa = field[1:9, :8], kappa[1:9, :8]
    return own_kappa * (8.0 * own - smooth(field)) + own * smooth(kappa) - smooth(
        kappa * field
    )


def offsets(aggregate):
    return aggregate - iota((ROWS, LANES), 1) // AGG


F_FIELD, F_KAPPA, F_MAP, F_SOURCE, F_DIAGONAL, F_FIRST = 0, 8, 16, 24, 26, 32
C_FIELD, C_KAPPA, C_MAP, C_HALOS, C_SOURCE, C_DIAGONAL, C_FIRST = 0, 8, 16, 24, 30, 32, 40
C_HALO_2, C_SOURCE_2, C_SECOND = 8, 10, 16


def begin(
    table_ref, side_ref, index_ref, order_ref, matrices_hbm, map_ref, diagonal_ref,
    pieces_ref, kappa_ref, places_ref, smoothed_ref, numbers_ref,
    matrices_ref, picked_ref, product_ref, arrived,
):
    owner, member = position()
    copy = pltpu.make_async_copy(matrices_hbm, matrices_ref, arrived)
    copy.start()
    index = index_ref[...]
    kappa = jnp.zeros((ROWS, LANES), F32)
    for entry in range(table_ref.shape[0]):
        kappa = jnp.where(index == entry, table_ref[entry], kappa)
    kappa_ref[...] = kappa
    places_ref[...] = invert(order_ref)
    permute(side_ref, order_ref, picked_ref)
    copy.wait()
    multiply_blocks(matrices_ref, picked_ref, product_ref)
    permute(product_ref, places_ref, smoothed_ref)
    aggregate = map_ref[...]
    numbers_ref[...] = aggregate.astype(F32)
    source = half_rows(restrict(side_ref[...], offsets(aggregate), member), member)
    lane = iota((8, LANES), 1)
    spread = jnp.concatenate([diagonal_ref[...]] * 8, axis=1)
    spread = jnp.where(lane // SIDE == member % 8, jnp.broadcast_to(spread, (8, LANES)), 0.0)
    source = source + pltpu.roll(half_rows(spread, member), 2, 0)
    for piece in range(SIDE):
        pieces_ref[piece, F_SOURCE : F_SOURCE + 8, :] = source
    put_faces(smoothed_ref, pieces_ref, F_FIELD, member)
    put_faces(kappa_ref, pieces_ref, F_KAPPA, member)
    put_faces(numbers_ref, pieces_ref, F_MAP, member)


def put_planes(field_ref, pieces_ref, row, owner):
    pieces_ref[jnp.maximum(owner - 1, 0), row : row + 8, :] = field_ref[0:8, :]
    pieces_ref[jnp.minimum(owner + 1, SIDE - 1), row : row + 8, :] = field_ref[56:64, :]


def relay_first(faces_ref, smoothed_ref, kappa_ref, numbers_ref, pieces_ref):
    owner, member = position()
    sources = jnp.sum(faces_ref[:, F_SOURCE : F_SOURCE + 8, :], axis=0)
    before, after = jnp.maximum(owner - 1, 0), jnp.minimum(owner + 1, SIDE - 1)
    for piece in range(SIDE):
        pieces_ref[piece, C_SOURCE : C_SOURCE + 4, :] = sources[0:4, :]
    put_planes(smoothed_ref, pieces_ref, C_FIELD, owner)
    put_planes(kappa_ref, pieces_ref, C_KAPPA, owner)
    put_planes(numbers_ref, pieces_ref, C_MAP, owner)
    for number, (row, outside) in enumerate(((F_FIELD, 0.0), (F_KAPPA, 0.0), (F_MAP, -1.0))):
        left, right = get_faces(faces_ref, row, member, outside)
        start = C_HALOS + 2 * number
        pieces_ref[before, start : start + 1, :] = left[0:1, :]
        pieces_ref[before, start + 1 : start + 2, :] = right[0:1, :]
        pieces_ref[after, start : start + 1, :] = left[7:8, :]
        pieces_ref[after, start + 1 : start + 2, :] = right[7:8, :]


def halves(pieces_ref, row):
    return jnp.concatenate([pieces_ref[:, row, :], pieces_ref[:, row + 1, :]], axis=1)


def first_image(
    faces_ref, ends_ref, own_ref, own_kappa_ref, numbers_ref, map_ref, order_ref, places_ref,
    matrices_hbm,
    pieces_ref, field_ref, image_ref, smoothed_ref, kappa_ref, lanes_ref, diagonal_ref,
    matrices_ref, picked_ref, product_ref, slabs_ref, rows_ref, arrived,
):
    owner, member = position()
    copy = pltpu.make_async_copy(matrices_hbm, matrices_ref, arrived)
    copy.start()
    diagonal = halves(ends_ref, C_DIAGONAL)
    diagonal_ref[...] = diagonal
    nearby(coarse_solve(halves(ends_ref, C_SOURCE), diagonal), member, rows_ref)
    fill_slabs(
        slabs_ref, numbers_ref, faces_ref, ends_ref, F_MAP, C_MAP, C_HALOS + 4, -1.0
    )
    row = iota((10, SLAB, LANES), 1)
    shift = jnp.where(row < 8, SIDE, jnp.where(row == RIGHT, 2 * SIDE, 0))
    number = slabs_ref[...]
    lanes_ref[...] = jnp.where(number >= 0.0, number.astype(jnp.int32) + shift, -1)
    fill_slabs(
        kappa_ref, own_kappa_ref, faces_ref, ends_ref, F_KAPPA, C_KAPPA, C_HALOS + 2, 0.0
    )
    fill_slabs(slabs_ref, own_ref, faces_ref, ends_ref, F_FIELD, C_FIELD, C_HALOS, 0.0)
    add_prolonged(slabs_ref, lanes_ref, rows_ref)
    field = slabs_ref[...]
    field_ref[...] = field[1:9, :8].reshape(ROWS, LANES)
    image_ref[...] = operate(field, kappa_ref[...]).reshape(ROWS, LANES)
    permute(image_ref, order_ref, picked_ref)
    copy.wait()
    multiply_blocks(matrices_ref, picked_ref, product_ref)
    permute(product_ref, places_ref, smoothed_ref)
    source = half_rows(restrict(image_ref[...], offsets(map_ref[...]), member), member)
    for piece in range(SIDE):
        pieces_ref[piece, 8:16, :] = source
    put_faces(smoothed_ref, pieces_ref, 0, member)


def relay_second(faces_ref, smoothed_ref, pieces_ref):
    owner, member = position()
    sources = jnp.sum(faces_ref[:, 8:16, :], axis=0)
    before, after = jnp.maximum(owner - 1, 0), jnp.minimum(owner + 1, SIDE - 1)
    for piece in range(SIDE):
        pieces_ref[piece, C_SOURCE_2 : C_SOURCE_2 + 2, :] = sources[0:2, :]
    put_planes(smoothed_ref, pieces_ref, 0, owner)
    left, right = get_faces(faces_ref, 0, member, 0.0)
    pieces_ref[before, C_HALO_2 : C_HALO_2 + 1, :] = left[0:1, :]
    pieces_ref[before, C_HALO_2 + 1 : C_HALO_2 + 2, :] = right[0:1, :]
    pieces_ref[after, C_HALO_2 : C_HALO_2 + 1, :] = left[7:8, :]
    pieces_ref[after, C_HALO_2 + 1 : C_HALO_2 + 2, :] = right[7:8, :]


def second_image(
    faces_ref, ends_ref, own_ref, kappa_ref, lanes_ref, map_ref, order_ref, places_ref,
    diagonal_ref, side_ref, first_ref, image_ref, matrices_hbm,
    pieces_ref, field_ref, second_ref, smoothed_ref,
    matrices_ref, picked_ref, product_ref, slabs_ref, rows_ref, arrived,
):
    owner, member = position()
    copy = pltpu.make_async_copy(matrices_hbm, matrices_ref, arrived)
    copy.start()
    nearby(coarse_solve(halves(ends_ref, C_SOURCE_2), diagonal_ref[...]), member, rows_ref)
    fill_slabs(slabs_ref, own_ref, faces_ref, ends_ref, 0, 0, C_HALO_2, 0.0)
    add_prolonged(slabs_ref, lanes_ref, rows_ref)
    slabs = slabs_ref[...]
    field = slabs[1:9, :8].reshape(ROWS, LANES)
    field_ref[...] = field
    second = operate(slabs, kappa_ref[...]).reshape(ROWS, LANES)
    second_ref[...] = second
    permute(second_ref, order_ref, picked_ref)
    copy.wait()
    multiply_blocks(matrices_ref, picked_ref, product_ref)
    permute(product_ref, places_ref, smoothed_ref)
    first = first_ref[...]
    image = image_ref[...]
    pairs = (
        side_ref[...] * first,
        first * image,
        image * field,
        second * first,
        second * field,
        second * smoothed_ref[...],
    )
    lane = iota((8, LANES), 1)
    message = restrict(second, offsets(map_ref[...]), member)
    beside = lax.rem(member + 1, 8) * SIDE
    for number, pair in enumerate(pairs):
        total = jnp.sum(jnp.sum(pair, axis=0, keepdims=True), axis=1, keepdims=True)
        message = jnp.where(lane == beside + number, total, message)
    for start in range(0, WIDE, 8):
        pieces_ref[start : start + 8, :] = message


def finish(
    pieces_ref, diagonal_ref, map_ref, side_ref, first_ref, image_ref, field_ref, second_ref,
    smoothed_ref,
    solution_ref, residual_ref, search_ref,
):
    owner, member = position()
    pieces = pieces_ref[...].reshape(SIDE, SIDE, LANES)
    place = iota((SIDE, LANES), 0) % 8
    group = iota((SIDE, LANES), 1) // SIDE
    pieces_sum = jnp.sum(pieces, axis=0)
    sums = jnp.where(group == (place + 1) % 8, pieces_sum, 0.0)
    kept = jnp.where((group == place)[None], pieces, 0.0)
    source = jnp.concatenate(
        [jnp.sum(kept[:, :8], axis=1), jnp.sum(kept[:, 8:], axis=1)], axis=1
    )
    coarse = coarse_solve(source, diagonal_ref[...])
    lane = iota((1, LANES), 1)
    sums = jnp.sum(sums, axis=0, keepdims=True)

    def total(number):
        picked = jnp.where(lane % SIDE == number, sums, 0.0)
        return jnp.sum(picked, axis=1, keepdims=True)

    def whole(array):
        return jnp.sum(jnp.sum(array, axis=0, keepdims=True), axis=1, keepdims=True)

    r_z, z_az, w_y, v_z, v_y, v_bv = (total(number) for number in range(6))
    v_u = v_bv + 4.0 * whole(source * coarse)
    alpha = r_z / z_az
    following = r_z - 2.0 * alpha * z_az + alpha * alpha * w_y
    grown = 1.0 + following / r_z
    product = grown * grown * z_az - grown * alpha * (v_z + w_y) + alpha * alpha * v_y
    again = following / product
    one = alpha + again * grown
    two = again * alpha
    last = (
        r_z - 2.0 * one * z_az + 2.0 * two * v_z + one * one * w_y
        - 2.0 * one * two * v_y + two * two * v_u
    )
    ratio = last / following
    lanes = iota((SIDE, WIDE), 1)
    rows = iota((SIDE, WIDE), 0)
    near = pltpu.roll(coarse, lax.rem((SIDE - member) * SIDE, WIDE), 1)[:, :LANES]
    row = jnp.sum(
        jnp.where(iota((SIDE, LANES), 0) == owner, near, 0.0), axis=0, keepdims=True
    )
    row = jnp.broadcast_to(row, (8, LANES))
    for g in range(8):
        at = slice(8 * g, 8 * g + 8)
        first, image, field, second = (
            ref[at, :] for ref in (first_ref, image_ref, field_ref, second_ref)
        )
        smoothed = smoothed_ref[at, :] + take_lanes(row, map_ref[at, :])
        solution_ref[at, :] = one * first - two * field
        residual_ref[at, :] = side_ref[at, :] - one * image + two * second
        search_ref[at, :] = (
            first - one * field + two * smoothed + ratio * (grown * first - alpha * field)
        )


def shards(
    right_side, coefficient_index, material_coefficients, block_cells, block_inverses,
    aggregate_map, coarse_diagonal,
):
    dims = right_side.shape
    side = right_side.reshape(ROWS, LANES)
    index = coefficient_index.reshape(ROWS, LANES)
    order = block_cells.reshape(ROWS, LANES)
    matrices = block_inverses.reshape(ROWS, LANES, LANES)
    aggregate = aggregate_map.reshape(ROWS, LANES)
    diagonal = coarse_diagonal.reshape(1, SIDE)
    local = shape(ROWS, LANES)
    block_scratch = [
        pltpu.VMEM((ROWS, LANES, LANES), F32),
        pltpu.VMEM((ROWS, LANES), F32),
        pltpu.VMEM((ROWS, LANES), F32),
    ]
    slab_scratch = [pltpu.VMEM((10, SLAB, LANES), F32), pltpu.VMEM((SIDE, LANES), F32)]
    arrived = [pltpu.SemaphoreType.DMA]

    def call(kernel, outs, ins, scratch=(), specs=None):
        return pl.pallas_call(
            kernel,
            out_shape=outs,
            in_specs=specs or [vmem()] * ins,
            out_specs=[vmem()] * len(outs),
            scratch_shapes=list(scratch),
            compiler_params=params(),
        )

    def exchange(pieces, axis):
        return lax.all_to_all(pieces, axis, 0, 0, tiled=True)

    pieces, kappa, places, smoothed, numbers = call(
        begin,
        [shape(SIDE, F_FIRST, LANES), local, shape(ROWS, LANES, dtype=jnp.int32), local, local],
        7,
        block_scratch + arrived,
        [smem()] + [vmem()] * 3 + [anywhere()] + [vmem()] * 2,
    )(material_coefficients, side, index, order, matrices, aggregate, diagonal)
    faces = exchange(pieces, FINE)
    (pieces,) = call(relay_first, [shape(SIDE, C_FIRST, LANES)], 4)(
        faces, smoothed, kappa, numbers
    )
    ends = exchange(pieces, COARSE)
    pieces, first, image, smoothed, kappa, lanes, diagonals = call(
        first_image,
        [
            shape(SIDE, SLAB, LANES), local, local, local, shape(10, SLAB, LANES),
            shape(10, SLAB, LANES, dtype=jnp.int32), shape(SIDE, WIDE),
        ],
        9,
        block_scratch + slab_scratch + arrived,
        [vmem()] * 8 + [anywhere()],
    )(faces, ends, smoothed, kappa, numbers, aggregate, order, places, matrices)
    faces = exchange(pieces, FINE)
    (pieces,) = call(relay_second, [shape(SIDE, C_SECOND, LANES)], 2)(faces, smoothed)
    ends = exchange(pieces, COARSE)
    pieces, field, second, smoothed = call(
        second_image,
        [shape(WIDE, LANES), local, local, local],
        13,
        block_scratch + slab_scratch + arrived,
        [vmem()] * 12 + [anywhere()],
    )(
        faces, ends, smoothed, kappa, lanes, aggregate, order, places, diagonals, side, first,
        image, matrices,
    )
    pieces = exchange(pieces, (COARSE, FINE))
    results = call(finish, [local, local, local], 9)(
        pieces, diagonals, aggregate, side, first, image, field, second, smoothed
    )
    return tuple(result.reshape(dims) for result in results)


def solution(mesh):
    cells = P(COARSE, FINE, None)
    in_specs = (
        cells,
        cells,
        P(),
        P(COARSE, FINE, None, None),
        P(COARSE, FINE, None, None, None),
        cells,
        cells,
    )
    return jax.shard_map(
        shards, mesh=mesh, in_specs=in_specs, out_specs=(cells,) * 3, check_vma=False
    )
```

```python
import functools

import jax
import jax.numpy as jnp
from jax import lax
from jax.experimental import pallas as pl
from jax.experimental.pallas import tpu as pltpu
from jax.sharding import PartitionSpec as P

AGG = 8
COARSE, FINE = "coarse", "fine"
SWEEPS = 4
OMEGA = 0.8
SIDE = 16
ROWS = 64
LANES = 128
WIDE = SIDE * SIDE
F32 = jnp.float32

SLAB = 16
RIGHT, LEFT = 8, 15


def vmem():
    return pl.BlockSpec(memory_space=pltpu.VMEM)


def smem():
    return pl.BlockSpec(memory_space=pltpu.SMEM)


def hbm():
    return pl.BlockSpec(memory_space=pltpu.HBM)


def params():
    return pltpu.CompilerParams(vmem_limit_bytes=24 * 1024 * 1024)


def shape(*dims, dtype=F32):
    return jax.ShapeDtypeStruct(dims, dtype)


def iota(dims, axis):
    return lax.broadcasted_iota(jnp.int32, dims, axis)


def take_lanes(values, lanes):
    numbers = lax.GatherDimensionNumbers(
        offset_dims=(),
        collapsed_slice_dims=(1,),
        start_index_map=(1,),
        operand_batching_dims=(0,),
        start_indices_batching_dims=(0,),
    )
    return lax.gather(
        values,
        lanes[..., None],
        numbers,
        slice_sizes=(1, 1),
        mode=lax.GatherScatterMode.PROMISE_IN_BOUNDS,
    )


def permute(source_ref, index_ref, target_ref):
    rows = [index_ref[8 * g : 8 * g + 8, :] // LANES for g in range(8)]
    lanes = [index_ref[8 * g : 8 * g + 8, :] % LANES for g in range(8)]

    def body(step, picked):
        for part in range(16):
            row = step * 16 + part
            source = jnp.broadcast_to(source_ref[pl.ds(row, 1), :], (8, LANES))
            picked = tuple(
                jnp.where(rows[g] == row, take_lanes(source, lanes[g]), picked[g])
                for g in range(8)
            )
        return picked

    zero = jnp.zeros((8, LANES), F32)
    picked = lax.fori_loop(0, ROWS // 16, body, (zero,) * 8)
    for g in range(8):
        target_ref[8 * g : 8 * g + 8, :] = picked[g]


def multiply_blocks(matrices_ref, picked_ref, product_ref):
    step = 32

    def body(group, carry):
        start = pl.multiple_of(group * step, step)
        columns = jnp.transpose(picked_ref[pl.ds(start, step), :])
        rows = []
        for part in range(step):
            matrix = matrices_ref[group * step + part].reshape(16, 8, LANES)
            column = columns[:, part : part + 1].reshape(16, 8, 1)
            total = jnp.sum(matrix * column, axis=0)
            rows.append(jnp.sum(total, axis=0, keepdims=True))
        product_ref[pl.ds(start, step), :] = jnp.concatenate(rows, axis=0)
        return carry

    lax.fori_loop(0, ROWS // step, body, 0)


def invert(order_ref):
    cell_rows = iota((ROWS, LANES), 0)
    cell_lanes = iota((LANES, LANES), 0)
    slots = iota((ROWS, LANES), 1).astype(F32)

    step = 8

    def body(group, total):
        numbers, lanes = [], []
        for part in range(step):
            block = group * step + part
            entry = order_ref[pl.ds(block, 1), :]
            hit = cell_rows == entry // LANES
            number = jnp.where(hit, block.astype(F32), 0.0)
            slot = jnp.where(hit, slots, 0.0)
            numbers.append(jnp.concatenate([number, slot], axis=0).astype(jnp.bfloat16))
            lane = jnp.where(cell_lanes == entry % LANES, 1.0, 0.0)
            lanes.append(lane.astype(jnp.bfloat16))
        return total + lax.dot_general(
            jnp.concatenate(numbers, axis=1),
            jnp.concatenate(lanes, axis=1),
            (((1,), (1,)), ((), ())),
            preferred_element_type=F32,
        )

    total = lax.fori_loop(0, ROWS // step, body, jnp.zeros((LANES, LANES), F32))
    return (total[:ROWS] * float(LANES) + total[ROWS:]).astype(jnp.int32)


def restrict(field, offset, member):
    total = jnp.sum(jnp.where(offset == 0, field, 0.0), axis=0, keepdims=True)
    up = jnp.sum(jnp.where(offset == 1, field, 0.0), axis=0, keepdims=True)
    down = jnp.sum(jnp.where(offset == -1, field, 0.0), axis=0, keepdims=True)
    total, up, down = (jnp.broadcast_to(x, (8, LANES)) for x in (total, up, down))
    total = total + pltpu.roll(up, AGG, 1) + pltpu.roll(down, LANES - AGG, 1)
    for distance in (1, 2, 4):
        total = total + pltpu.roll(total, LANES - distance, 1)
    lane = iota((8, LANES), 1)
    total = 0.25 * take_lanes(total, (lane % SIDE) * AGG)
    return jnp.where(lane // SIDE == member % 8, total, 0.0)


def half_rows(values, member):
    return jnp.where(iota((8, LANES), 0) == member // 8, values, 0.0)


def moved(values, distance, axis, keep):
    size = values.shape[axis]
    return jnp.where(keep, pltpu.roll(values, distance % size, axis), 0.0)


def coarse_solve(source, diagonal):
    owner, lane = iota((SIDE, WIDE), 0), iota((SIDE, WIDE), 1)
    cell = lane % SIDE
    weight = OMEGA / (6.0 + diagonal)
    guess = weight * source
    for sweep in range(SWEEPS - 1):
        beside = moved(guess, 1, 0, owner > 0) + moved(guess, -1, 0, owner < SIDE - 1)
        beside = beside + moved(guess, SIDE, 1, lane >= SIDE)
        beside = beside + moved(guess, -SIDE, 1, lane < WIDE - SIDE)
        beside = beside + moved(guess, 1, 1, cell > 0) + moved(guess, -1, 1, cell < SIDE - 1)
        guess = (1.0 - OMEGA) * guess + weight * (source + beside)
    return guess


def nearby(coarse, member, rows_ref):
    rows_ref[...] = pltpu.roll(coarse, lax.rem((SIDE + 1 - member) * SIDE, WIDE), 1)[:, :LANES]


def smooth(slabs):
    total = slabs[1:9] + 0.5 * (slabs[0:8] + slabs[2:10])
    planes = []
    lane = iota((8, LANES), 1)
    row = iota((8, LANES), 0)
    for plane in range(8):
        own, ends = total[plane, :8], total[plane, 8:]
        before = jnp.where(row == 0, ends[LEFT - 8 :, :], pltpu.roll(own, 1, 0))
        after = jnp.where(row == 7, ends[:1, :], pltpu.roll(own, 7, 0))
        own = own + 0.5 * (before + after)
        below = jnp.where(lane > 0, pltpu.roll(own, 1, 1), 0.0)
        above = jnp.where(lane < LANES - 1, pltpu.roll(own, LANES - 1, 1), 0.0)
        planes.append(own + 0.5 * (below + above))
    return jnp.stack(planes)


def position():
    return lax.axis_index(COARSE), lax.axis_index(FINE)


def put_faces(field_ref, pieces_ref, row, member):
    pieces_ref[jnp.maximum(member - 1, 0), row : row + 8, :] = field_ref[
        pl.ds(0, 8, stride=8), :
    ]
    pieces_ref[jnp.minimum(member + 1, SIDE - 1), row : row + 8, :] = field_ref[
        pl.ds(7, 8, stride=8), :
    ]


def get_faces(pieces_ref, row, member, outside):
    left = pieces_ref[jnp.maximum(member - 1, 0), row : row + 8, :]
    right = pieces_ref[jnp.minimum(member + 1, SIDE - 1), row : row + 8, :]
    left = jnp.where(member > 0, left, outside)
    right = jnp.where(member < SIDE - 1, right, outside)
    return left, right


def neighbours(ends_ref, owner):
    return (
        ends_ref.at[jnp.maximum(owner - 1, 0)],
        ends_ref.at[jnp.minimum(owner + 1, SIDE - 1)],
    )


def fill_slabs(slabs_ref, field_ref, faces_ref, ends, face_row, end_row, halo_row, outside):
    owner, member = position()
    left, right = get_faces(faces_ref, face_row, member, outside)
    gap = jnp.full((8, LANES), outside, F32)
    for plane in range(8):
        slabs_ref[plane + 1, :8, :] = field_ref[8 * plane : 8 * plane + 8, :]
        slabs_ref[plane + 1, 8:, :] = gap
        slabs_ref[plane + 1, RIGHT : RIGHT + 1, :] = right[plane : plane + 1, :]
        slabs_ref[plane + 1, LEFT : LEFT + 1, :] = left[plane : plane + 1, :]
    for plane, end_ref, inside in ((0, ends[0], owner > 0), (9, ends[1], owner < SIDE - 1)):
        slabs_ref[plane, 8:, :] = gap
        slabs_ref[plane, :8, :] = jnp.where(inside, end_ref[end_row : end_row + 8, :], outside)
        halo = jnp.where(inside, end_ref[halo_row : halo_row + 2, :], outside)
        slabs_ref[plane, LEFT : LEFT + 1, :] = halo[0:1, :]
        slabs_ref[plane, RIGHT : RIGHT + 1, :] = halo[1:2, :]


def add_prolonged(slabs_ref, numbers_ref, rows_ref):
    owner, member = position()
    for plane in range(10):
        if plane == 0:
            there = jnp.maximum(owner - 1, 0)
        elif plane == 9:
            there = jnp.minimum(owner + 1, SIDE - 1)
        else:
            there = owner
        row = jnp.broadcast_to(rows_ref[pl.ds(there, 1), :], (8, LANES))
        for part in (0, 8):
            number = numbers_ref[plane, part : part + 8, :]
            value = take_lanes(row, jnp.maximum(number, 0))
            slabs_ref[plane, part : part + 8, :] += jnp.where(number >= 0, value, 0.0)


def operate(field, kappa):
    own, own_kappa = field[1:9, :8], kappa[1:9, :8]
    return own_kappa * (8.0 * own - smooth(field)) + own * smooth(kappa) - smooth(
        kappa * field
    )


def offsets(aggregate):
    return aggregate - iota((ROWS, LANES), 1) // AGG


F_FIELD, F_KAPPA, F_MAP, F_SOURCE, F_DIAGONAL, F_FIRST = 0, 8, 16, 24, 26, 32
C_FIELD, C_KAPPA, C_MAP, C_HALOS, C_PLANES = 0, 8, 16, 24, 32
C_SOURCE, C_DIAGONAL, C_FIRST = 0, 2, 8
C_HALO_2, C_SOURCE_2, C_SECOND = 8, 10, 16


def begin(
    table_hbm, side_hbm, index_hbm, order_hbm, matrices_hbm, map_hbm, diagonal_hbm,
    pieces_ref, kappa_ref, places_ref, smoothed_ref, numbers_ref,
    table_ref, side_ref, index_ref, order_ref, map_ref, diagonal_ref, picked_ref, product_ref,
    matrices_ref, arrived,
):
    owner, member = position()
    copies = [
        pltpu.make_async_copy(source, target, arrived.at[number])
        for number, (source, target) in enumerate(
            (
                (order_hbm, order_ref),
                (side_hbm, side_ref),
                (table_hbm, table_ref),
                (index_hbm, index_ref),
                (map_hbm, map_ref),
                (diagonal_hbm, diagonal_ref),
                (matrices_hbm, matrices_ref),
            )
        )
    ]
    for copy in copies:
        copy.start()
    copies[0].wait()
    places_ref[...] = invert(order_ref)
    for copy in copies[1:-1]:
        copy.wait()
    index = index_ref[...]
    kappa = jnp.zeros((ROWS, LANES), F32)
    for entry in range(table_ref.shape[0]):
        kappa = jnp.where(index == entry, table_ref[entry], kappa)
    kappa_ref[...] = kappa
    permute(side_ref, order_ref, picked_ref)
    copies[-1].wait()
    multiply_blocks(matrices_ref, picked_ref, product_ref)
    permute(product_ref, places_ref, smoothed_ref)
    aggregate = map_ref[...]
    numbers_ref[...] = aggregate.astype(F32)
    source = half_rows(restrict(side_ref[...], offsets(aggregate), member), member)
    lane = iota((8, LANES), 1)
    spread = jnp.concatenate([diagonal_ref[...]] * 8, axis=1)
    spread = jnp.where(lane // SIDE == member % 8, jnp.broadcast_to(spread, (8, LANES)), 0.0)
    source = source + pltpu.roll(half_rows(spread, member), 2, 0)
    for piece in range(SIDE):
        pieces_ref[piece, F_SOURCE : F_SOURCE + 8, :] = source
    put_faces(smoothed_ref, pieces_ref, F_FIELD, member)
    put_faces(kappa_ref, pieces_ref, F_KAPPA, member)
    put_faces(numbers_ref, pieces_ref, F_MAP, member)


def put_planes(field_ref, before_ref, after_ref, row):
    before_ref[row : row + 8, :] = field_ref[0:8, :]
    after_ref[row : row + 8, :] = field_ref[56:64, :]


def put_halos(left, right, before_ref, after_ref, row):
    before_ref[row : row + 1, :] = left[0:1, :]
    before_ref[row + 1 : row + 2, :] = right[0:1, :]
    after_ref[row : row + 1, :] = left[7:8, :]
    after_ref[row + 1 : row + 2, :] = right[7:8, :]


def relay_first(
    faces_ref, smoothed_ref, kappa_ref, numbers_ref, pieces_ref, before_ref, after_ref
):
    owner, member = position()
    sources = jnp.sum(faces_ref[:, F_SOURCE : F_SOURCE + 8, :], axis=0)
    for piece in range(SIDE):
        pieces_ref[piece] = sources
    put_planes(smoothed_ref, before_ref, after_ref, C_FIELD)
    put_planes(kappa_ref, before_ref, after_ref, C_KAPPA)
    put_planes(numbers_ref, before_ref, after_ref, C_MAP)
    before_ref[C_HALOS:, :] = jnp.zeros((8, LANES), F32)
    after_ref[C_HALOS:, :] = jnp.zeros((8, LANES), F32)
    for number, (row, outside) in enumerate(((F_FIELD, 0.0), (F_KAPPA, 0.0), (F_MAP, -1.0))):
        left, right = get_faces(faces_ref, row, member, outside)
        put_halos(left, right, before_ref, after_ref, C_HALOS + 2 * number)


def halves(pieces_ref, row):
    return jnp.concatenate([pieces_ref[:, row, :], pieces_ref[:, row + 1, :]], axis=1)


def first_image(
    faces_ref, ends_ref, before_ref, after_ref, own_ref, own_kappa_ref, numbers_ref, map_ref, order_ref, places_ref,
    matrices_hbm,
    pieces_ref, field_ref, image_ref, smoothed_ref, kappa_ref, lanes_ref, diagonal_ref,
    picked_ref, product_ref, slabs_ref, rows_ref, matrices_ref, arrived,
):
    owner, member = position()
    copy = pltpu.make_async_copy(matrices_hbm, matrices_ref, arrived)
    copy.start()
    diagonal = halves(ends_ref, C_DIAGONAL)
    diagonal_ref[...] = diagonal
    nearby(coarse_solve(halves(ends_ref, C_SOURCE), diagonal), member, rows_ref)
    ends = before_ref, after_ref
    fill_slabs(slabs_ref, numbers_ref, faces_ref, ends, F_MAP, C_MAP, C_HALOS + 4, -1.0)
    row = iota((10, SLAB, LANES), 1)
    shift = jnp.where(row < 8, SIDE, jnp.where(row == RIGHT, 2 * SIDE, 0))
    number = slabs_ref[...]
    lanes_ref[...] = jnp.where(number >= 0.0, number.astype(jnp.int32) + shift, -1)
    fill_slabs(kappa_ref, own_kappa_ref, faces_ref, ends, F_KAPPA, C_KAPPA, C_HALOS + 2, 0.0)
    fill_slabs(slabs_ref, own_ref, faces_ref, ends, F_FIELD, C_FIELD, C_HALOS, 0.0)
    add_prolonged(slabs_ref, lanes_ref, rows_ref)
    field = slabs_ref[...]
    field_ref[...] = field[1:9, :8].reshape(ROWS, LANES)
    image_ref[...] = operate(field, kappa_ref[...]).reshape(ROWS, LANES)
    permute(image_ref, order_ref, picked_ref)
    copy.wait()
    multiply_blocks(matrices_ref, picked_ref, product_ref)
    permute(product_ref, places_ref, smoothed_ref)
    source = half_rows(restrict(image_ref[...], offsets(map_ref[...]), member), member)
    for piece in range(SIDE):
        pieces_ref[piece, 8:16, :] = source
    put_faces(smoothed_ref, pieces_ref, 0, member)


def relay_second(faces_ref, smoothed_ref, pieces_ref):
    owner, member = position()
    sources = jnp.sum(faces_ref[:, 8:16, :], axis=0)
    for piece in range(SIDE):
        pieces_ref[piece, C_SOURCE_2 : C_SOURCE_2 + 2, :] = sources[0:2, :]
    before_ref, after_ref = neighbours(pieces_ref, owner)
    put_planes(smoothed_ref, before_ref, after_ref, 0)
    left, right = get_faces(faces_ref, 0, member, 0.0)
    put_halos(left, right, before_ref, after_ref, C_HALO_2)


def second_image(
    faces_ref, ends_ref, own_ref, kappa_ref, lanes_ref, map_ref, order_ref, places_ref,
    diagonal_ref, side_ref, first_ref, image_ref, matrices_hbm,
    pieces_ref, field_ref, second_ref, smoothed_ref,
    picked_ref, product_ref, slabs_ref, rows_ref, matrices_ref, arrived,
):
    owner, member = position()
    copy = pltpu.make_async_copy(matrices_hbm, matrices_ref, arrived)
    copy.start()
    nearby(coarse_solve(halves(ends_ref, C_SOURCE_2), diagonal_ref[...]), member, rows_ref)
    fill_slabs(slabs_ref, own_ref, faces_ref, neighbours(ends_ref, owner), 0, 0, C_HALO_2, 0.0)
    add_prolonged(slabs_ref, lanes_ref, rows_ref)
    slabs = slabs_ref[...]
    field = slabs[1:9, :8].reshape(ROWS, LANES)
    field_ref[...] = field
    second = operate(slabs, kappa_ref[...]).reshape(ROWS, LANES)
    second_ref[...] = second
    permute(second_ref, order_ref, picked_ref)
    copy.wait()
    multiply_blocks(matrices_ref, picked_ref, product_ref)
    permute(product_ref, places_ref, smoothed_ref)
    first = first_ref[...]
    image = image_ref[...]
    pairs = (
        side_ref[...] * first,
        first * image,
        image * field,
        second * first,
        second * field,
        second * smoothed_ref[...],
    )
    lane = iota((8, LANES), 1)
    message = restrict(second, offsets(map_ref[...]), member)
    beside = lax.rem(member + 1, 8) * SIDE
    for number, pair in enumerate(pairs):
        total = jnp.sum(jnp.sum(pair, axis=0, keepdims=True), axis=1, keepdims=True)
        message = jnp.where(lane == beside + number, total, message)
    for start in range(0, WIDE, 8):
        pieces_ref[start : start + 8, :] = message


def finish(
    pieces_ref, diagonal_ref, map_ref, side_ref, first_ref, image_ref, field_ref, second_ref,
    smoothed_ref,
    solution_ref, residual_ref, search_ref,
):
    owner, member = position()
    pieces = pieces_ref[...].reshape(SIDE, SIDE, LANES)
    place = iota((SIDE, LANES), 0) % 8
    group = iota((SIDE, LANES), 1) // SIDE
    pieces_sum = jnp.sum(pieces, axis=0)
    sums = jnp.where(group == (place + 1) % 8, pieces_sum, 0.0)
    kept = jnp.where((group == place)[None], pieces, 0.0)
    source = jnp.concatenate(
        [jnp.sum(kept[:, :8], axis=1), jnp.sum(kept[:, 8:], axis=1)], axis=1
    )
    coarse = coarse_solve(source, diagonal_ref[...])
    lane = iota((1, LANES), 1)
    sums = jnp.sum(sums, axis=0, keepdims=True)

    def total(number):
        picked = jnp.where(lane % SIDE == number, sums, 0.0)
        return jnp.sum(picked, axis=1, keepdims=True)

    def whole(array):
        return jnp.sum(jnp.sum(array, axis=0, keepdims=True), axis=1, keepdims=True)

    r_z, z_az, w_y, v_z, v_y, v_bv = (total(number) for number in range(6))
    v_u = v_bv + 4.0 * whole(source * coarse)
    alpha = r_z / z_az
    following = r_z - 2.0 * alpha * z_az + alpha * alpha * w_y
    grown = 1.0 + following / r_z
    product = grown * grown * z_az - grown * alpha * (v_z + w_y) + alpha * alpha * v_y
    again = following / product
    one = alpha + again * grown
    two = again * alpha
    last = (
        r_z - 2.0 * one * z_az + 2.0 * two * v_z + one * one * w_y
        - 2.0 * one * two * v_y + two * two * v_u
    )
    ratio = last / following
    lanes = iota((SIDE, WIDE), 1)
    rows = iota((SIDE, WIDE), 0)
    near = pltpu.roll(coarse, lax.rem((SIDE - member) * SIDE, WIDE), 1)[:, :LANES]
    row = jnp.sum(
        jnp.where(iota((SIDE, LANES), 0) == owner, near, 0.0), axis=0, keepdims=True
    )
    row = jnp.broadcast_to(row, (8, LANES))
    for g in range(8):
        at = slice(8 * g, 8 * g + 8)
        first, image, field, second = (
            ref[at, :] for ref in (first_ref, image_ref, field_ref, second_ref)
        )
        smoothed = smoothed_ref[at, :] + take_lanes(row, map_ref[at, :])
        solution_ref[at, :] = one * first - two * field
        residual_ref[at, :] = side_ref[at, :] - one * image + two * second
        search_ref[at, :] = (
            first - one * field + two * smoothed + ratio * (grown * first - alpha * field)
        )


def shards(
    right_side, coefficient_index, material_coefficients, block_cells, block_inverses,
    aggregate_map, coarse_diagonal,
):
    dims = right_side.shape
    side = right_side.reshape(ROWS, LANES)
    index = coefficient_index.reshape(ROWS, LANES)
    order = block_cells.reshape(ROWS, LANES)
    matrices = block_inverses.reshape(ROWS, LANES, LANES)
    aggregate = aggregate_map.reshape(ROWS, LANES)
    diagonal = coarse_diagonal.reshape(1, SIDE)
    local = shape(ROWS, LANES)
    local_int = shape(ROWS, LANES, dtype=jnp.int32)
    cells = pltpu.VMEM((ROWS, LANES), F32)
    int_cells = pltpu.VMEM((ROWS, LANES), jnp.int32)
    held = pltpu.VMEM(matrices.shape, F32)
    scratch = [
        cells, cells, pltpu.VMEM((10, SLAB, LANES), F32), pltpu.VMEM((SIDE, LANES), F32),
        held, pltpu.SemaphoreType.DMA,
    ]

    def call(kernel, outs, ins, scratch=(), specs=None):
        return pl.pallas_call(
            kernel,
            out_shape=outs,
            in_specs=specs or [vmem()] * ins,
            out_specs=[vmem()] * len(outs),
            scratch_shapes=list(scratch),
            compiler_params=params(),
        )

    def exchange(pieces, axis):
        return lax.all_to_all(pieces, axis, 0, 0, tiled=True)

    def ring(planes, step):
        return lax.ppermute(planes, COARSE, [(i, (i + step) % SIDE) for i in range(SIDE)])

    fixed = [
        pltpu.with_memory_space_constraint(array, pltpu.HBM)
        for array in (material_coefficients, side, index, order, matrices, aggregate, diagonal)
    ]
    pieces, kappa, places, smoothed, numbers = call(
        begin,
        [
            shape(SIDE, F_FIRST, LANES), local, local_int, local, local,
        ],
        7,
        [
            pltpu.SMEM(material_coefficients.shape, F32), cells, int_cells, int_cells,
            int_cells, pltpu.VMEM((1, SIDE), F32), cells, cells,
            held, pltpu.SemaphoreType.DMA((7,)),
        ],
        [hbm()] * 7,
    )(*fixed)
    faces = exchange(pieces, FINE)
    pieces, before, after = call(
        relay_first,
        [shape(SIDE, C_FIRST, LANES), shape(C_PLANES, LANES), shape(C_PLANES, LANES)],
        4,
    )(faces, smoothed, kappa, numbers)
    from_after, from_before = ring(before, -1), ring(after, 1)
    ends = exchange(pieces, COARSE)
    pieces, first, image, smoothed, kappa, lanes, diagonals = call(
        first_image,
        [
            shape(SIDE, SLAB, LANES), local, local, local, shape(10, SLAB, LANES),
            shape(10, SLAB, LANES, dtype=jnp.int32), shape(SIDE, WIDE),
        ],
        11,
        scratch,
        [vmem()] * 10 + [hbm()],
    )(
        faces, ends, from_before, from_after, smoothed, kappa, numbers, aggregate, order,
        places, fixed[4],
    )
    faces = exchange(pieces, FINE)
    (pieces,) = call(relay_second, [shape(SIDE, C_SECOND, LANES)], 2)(faces, smoothed)
    ends = exchange(pieces, COARSE)
    pieces, field, second, smoothed = call(
        second_image,
        [shape(WIDE, LANES), local, local, local],
        13,
        scratch,
        [vmem()] * 12 + [hbm()],
    )(
        faces, ends, smoothed, kappa, lanes, aggregate, order, places, diagonals, side, first,
        image, fixed[4],
    )
    pieces = exchange(pieces, (COARSE, FINE))
    results = call(finish, [local, local, local], 9)(
        pieces, diagonals, aggregate, side, first, image, field, second, smoothed
    )
    return tuple(result.reshape(dims) for result in results)


def solution(mesh):
    cells = P(COARSE, FINE, None)
    in_specs = (
        cells,
        cells,
        P(),
        P(COARSE, FINE, None, None),
        P(COARSE, FINE, None, None, None),
        cells,
        cells,
    )
    return jax.shard_map(
        shards, mesh=mesh, in_specs=in_specs, out_specs=(cells,) * 3, check_vma=False
    )
```

```python
import functools

import jax
import jax.numpy as jnp
from jax import lax
from jax.experimental import pallas as pl
from jax.experimental.pallas import tpu as pltpu
from jax.sharding import PartitionSpec as P

AGG = 8
COARSE, FINE = "coarse", "fine"
SWEEPS = 4
OMEGA = 0.8
SIDE = 16
ROWS = 64
LANES = 128
WIDE = SIDE * SIDE
F32, BF16 = jnp.float32, jnp.bfloat16
GROUP = 8

SLAB = 16
RIGHT, LEFT = 8, 15


def vmem():
    return pl.BlockSpec(memory_space=pltpu.VMEM)


def smem():
    return pl.BlockSpec(memory_space=pltpu.SMEM)


def hbm():
    return pl.BlockSpec(memory_space=pltpu.HBM)


def params():
    return pltpu.CompilerParams(vmem_limit_bytes=24 * 1024 * 1024)


def shape(*dims, dtype=F32):
    return jax.ShapeDtypeStruct(dims, dtype)


def iota(dims, axis):
    return lax.broadcasted_iota(jnp.int32, dims, axis)


def take_lanes(values, lanes):
    numbers = lax.GatherDimensionNumbers(
        offset_dims=(),
        collapsed_slice_dims=(1,),
        start_index_map=(1,),
        operand_batching_dims=(0,),
        start_indices_batching_dims=(0,),
    )
    return lax.gather(
        values,
        lanes[..., None],
        numbers,
        slice_sizes=(1, 1),
        mode=lax.GatherScatterMode.PROMISE_IN_BOUNDS,
    )


def split(values):
    high = values.astype(BF16)
    return high, (values - high.astype(F32)).astype(BF16)


def matmul(left, right, left_dim, right_dim):
    dims = (((left_dim,), (right_dim,)), ((), ()))
    return lax.dot_general(left, right, dims, preferred_element_type=F32)


def lane_hits(order_ref, group):
    lane = iota((LANES, LANES), 0)
    return jnp.concatenate(
        [
            jnp.where(lane == order_ref[b : b + 1, :] % LANES, 1.0, 0.0).astype(BF16)
            for b in range(group * GROUP, group * GROUP + GROUP)
        ],
        axis=1,
    )


def row_hit(order_ref, block):
    return iota((ROWS, LANES), 0) == order_ref[block : block + 1, :] // LANES


def column_sum(values):
    total = jnp.sum(values.reshape(-1, 8, LANES), axis=0)
    return jnp.sum(total, axis=0, keepdims=True)


def pick(source_ref, order_ref, picked_ref):
    source = jnp.concatenate(split(source_ref[...]), axis=0)
    for group in range(ROWS // GROUP):
        start = group * GROUP
        found = matmul(source, lane_hits(order_ref, group), 1, 0)
        found = found[:ROWS] + found[ROWS:]
        rows = []
        for part in range(GROUP):
            column = found[:, LANES * part : LANES * (part + 1)]
            rows.append(column_sum(jnp.where(row_hit(order_ref, start + part), column, 0.0)))
        picked_ref[start : start + GROUP, :] = jnp.concatenate(rows, axis=0)


def multiply_blocks(matrices_ref, picked_ref, product_ref):
    wide = (2 * GROUP, GROUP * LANES)
    spread = jnp.where(iota(wide, 0) % GROUP == iota(wide, 1) // LANES, 1.0, 0.0).astype(BF16)
    for start in range(0, ROWS, GROUP):
        high, low = split(picked_ref[start : start + GROUP, :])
        both = jnp.concatenate([high.astype(F32), low.astype(F32)], axis=0)
        columns = matmul(jnp.transpose(both).astype(BF16), spread, 1, 0)
        rows = [
            column_sum(
                matrices_ref[start + part] * columns[:, LANES * part : LANES * (part + 1)]
            )
            for part in range(GROUP)
        ]
        product_ref[start : start + GROUP, :] = jnp.concatenate(rows, axis=0)


def put_back(product_ref, order_ref, target_ref):
    total = jnp.zeros((2 * ROWS, LANES), F32)
    for group in range(ROWS // GROUP):
        start = group * GROUP
        halves_of = [part.astype(F32) for part in split(product_ref[start : start + GROUP, :])]
        hits = [row_hit(order_ref, start + part) for part in range(GROUP)]
        values = [
            jnp.concatenate(
                [
                    jnp.where(hits[part], half[part : part + 1, :], 0.0).astype(BF16)
                    for part in range(GROUP)
                ],
                axis=1,
            )
            for half in halves_of
        ]
        total = total + matmul(
            jnp.concatenate(values, axis=0), lane_hits(order_ref, group), 1, 1
        )
    target_ref[...] = total[:ROWS] + total[ROWS:]


def restrict(field, offset, member):
    total = jnp.sum(jnp.where(offset == 0, field, 0.0), axis=0, keepdims=True)
    up = jnp.sum(jnp.where(offset == 1, field, 0.0), axis=0, keepdims=True)
    down = jnp.sum(jnp.where(offset == -1, field, 0.0), axis=0, keepdims=True)
    total, up, down = (jnp.broadcast_to(x, (8, LANES)) for x in (total, up, down))
    total = total + pltpu.roll(up, AGG, 1) + pltpu.roll(down, LANES - AGG, 1)
    for distance in (1, 2, 4):
        total = total + pltpu.roll(total, LANES - distance, 1)
    lane = iota((8, LANES), 1)
    total = 0.25 * take_lanes(total, (lane % SIDE) * AGG)
    return jnp.where(lane // SIDE == member % 8, total, 0.0)


def moved(values, distance, axis, keep):
    size = values.shape[axis]
    return jnp.where(keep, pltpu.roll(values, distance % size, axis), 0.0)


def coarse_solve(source, diagonal):
    owner, lane = iota((SIDE, WIDE), 0), iota((SIDE, WIDE), 1)
    cell = lane % SIDE
    weight = OMEGA / (6.0 + diagonal)
    guess = weight * source
    for sweep in range(SWEEPS - 1):
        beside = moved(guess, 1, 0, owner > 0) + moved(guess, -1, 0, owner < SIDE - 1)
        beside = beside + moved(guess, SIDE, 1, lane >= SIDE)
        beside = beside + moved(guess, -SIDE, 1, lane < WIDE - SIDE)
        beside = beside + moved(guess, 1, 1, cell > 0) + moved(guess, -1, 1, cell < SIDE - 1)
        guess = (1.0 - OMEGA) * guess + weight * (source + beside)
    return guess


def nearby(coarse, member, rows_ref):
    rows_ref[...] = pltpu.roll(coarse, lax.rem((SIDE + 1 - member) * SIDE, WIDE), 1)[:, :LANES]


def smooth(slabs):
    total = slabs[1:9] + 0.5 * (slabs[0:8] + slabs[2:10])
    planes = []
    lane = iota((8, LANES), 1)
    row = iota((8, LANES), 0)
    for plane in range(8):
        own, ends = total[plane, :8], total[plane, 8:]
        before = jnp.where(row == 0, ends[LEFT - 8 :, :], pltpu.roll(own, 1, 0))
        after = jnp.where(row == 7, ends[:1, :], pltpu.roll(own, 7, 0))
        own = own + 0.5 * (before + after)
        below = jnp.where(lane > 0, pltpu.roll(own, 1, 1), 0.0)
        above = jnp.where(lane < LANES - 1, pltpu.roll(own, LANES - 1, 1), 0.0)
        planes.append(own + 0.5 * (below + above))
    return jnp.stack(planes)


def position():
    return lax.axis_index(COARSE), lax.axis_index(FINE)


def put_faces(field_ref, pieces_ref, rows, row, member):
    before, after = jnp.maximum(member - 1, 0), jnp.minimum(member + 1, SIDE - 1)
    pieces_ref[pl.ds(before * rows + row, 8), :] = field_ref[pl.ds(0, 8, stride=8), :]
    pieces_ref[pl.ds(after * rows + row, 8), :] = field_ref[pl.ds(7, 8, stride=8), :]


def get_faces(pieces_ref, rows, row, member, outside):
    before, after = jnp.maximum(member - 1, 0), jnp.minimum(member + 1, SIDE - 1)
    left = pieces_ref[pl.ds(before * rows + row, 8), :]
    right = pieces_ref[pl.ds(after * rows + row, 8), :]
    left = jnp.where(member > 0, left, outside)
    right = jnp.where(member < SIDE - 1, right, outside)
    return left, right


def fill_slabs(slabs_ref, field_ref, faces, pieces, outside):
    owner, member = position()
    faces_ref, face_rows, face_row = faces
    pieces_ref, rows, plane_row, halo_row = pieces
    left, right = get_faces(faces_ref, face_rows, face_row, member, outside)
    gap = jnp.full((8, LANES), outside, F32)
    for plane in range(8):
        slabs_ref[plane + 1, :8, :] = field_ref[8 * plane : 8 * plane + 8, :]
        slabs_ref[plane + 1, 8:, :] = gap
        slabs_ref[plane + 1, RIGHT : RIGHT + 1, :] = right[plane : plane + 1, :]
        slabs_ref[plane + 1, LEFT : LEFT + 1, :] = left[plane : plane + 1, :]
    for plane, there, inside in (
        (0, jnp.maximum(owner - 1, 0), owner > 0),
        (9, jnp.minimum(owner + 1, SIDE - 1), owner < SIDE - 1),
    ):
        start = there * rows
        slabs_ref[plane, 8:, :] = gap
        slabs_ref[plane, :8, :] = jnp.where(
            inside, pieces_ref[pl.ds(start + plane_row, 8), :], outside
        )
        for side, target in enumerate((LEFT, RIGHT)):
            slabs_ref[plane, target : target + 1, :] = jnp.where(
                inside, pieces_ref[pl.ds(start + halo_row + side, 1), :], outside
            )


def add_prolonged(slabs_ref, numbers_ref, rows_ref):
    owner, member = position()
    for plane in range(10):
        if plane == 0:
            there = jnp.maximum(owner - 1, 0)
        elif plane == 9:
            there = jnp.minimum(owner + 1, SIDE - 1)
        else:
            there = owner
        row = jnp.broadcast_to(rows_ref[pl.ds(there, 1), :], (8, LANES))
        for part in (0, 8):
            number = numbers_ref[plane, part : part + 8, :]
            value = take_lanes(row, jnp.maximum(number, 0))
            slabs_ref[plane, part : part + 8, :] += jnp.where(number >= 0, value, 0.0)


def operate(field, kappa):
    own, own_kappa = field[1:9, :8], kappa[1:9, :8]
    return own_kappa * (8.0 * own - smooth(field)) + own * smooth(kappa) - smooth(
        kappa * field
    )


def offsets(aggregate):
    return aggregate - iota((ROWS, LANES), 1) // AGG


F_FIELD, F_KAPPA, F_MAP, F_SOURCE, F_FIRST = 0, 8, 16, 24, 25
C_FIELD, C_KAPPA, C_MAP, C_HALOS, C_SOURCE, C_DIAGONAL, C_FIRST = 0, 8, 16, 24, 30, 32, 34
F_SOURCE_2, F_SECOND = 8, 9
C_HALO_2, C_SOURCE_2, C_SECOND = 8, 10, 12


def begin(
    table_hbm, side_hbm, index_hbm, order_hbm, matrices_hbm, map_hbm, diagonal_hbm,
    pieces_ref, kappa_ref, smoothed_ref, numbers_ref,
    table_ref, side_ref, index_ref, order_ref, map_ref, diagonal_ref, picked_ref, product_ref,
    matrices_ref, arrived,
):
    owner, member = position()
    copies = [
        pltpu.make_async_copy(source, target, arrived.at[number])
        for number, (source, target) in enumerate(
            (
                (order_hbm, order_ref),
                (side_hbm, side_ref),
                (table_hbm, table_ref),
                (index_hbm, index_ref),
                (map_hbm, map_ref),
                (diagonal_hbm, diagonal_ref),
                (matrices_hbm, matrices_ref),
            )
        )
    ]
    for copy in copies:
        copy.start()
    copies[0].wait()
    for copy in copies[1:-1]:
        copy.wait()
    index = index_ref[...]
    kappa = jnp.zeros((ROWS, LANES), F32)
    for entry in range(table_ref.shape[0]):
        kappa = jnp.where(index == entry, table_ref[entry], kappa)
    kappa_ref[...] = kappa
    pick(side_ref, order_ref, picked_ref)
    copies[-1].wait()
    multiply_blocks(matrices_ref, picked_ref, product_ref)
    put_back(product_ref, order_ref, smoothed_ref)
    aggregate = map_ref[...]
    numbers_ref[...] = aggregate.astype(F32)
    source = restrict(side_ref[...], offsets(aggregate), member)
    spread = jnp.broadcast_to(jnp.concatenate([diagonal_ref[...]] * 8, axis=1), (8, LANES))
    beside = iota((8, LANES), 1) // SIDE == (member + 1) % 8
    put_all(jnp.where(beside, spread, source), pieces_ref, F_FIRST, F_SOURCE)
    put_faces(smoothed_ref, pieces_ref, F_FIRST, F_FIELD, member)
    put_faces(kappa_ref, pieces_ref, F_FIRST, F_KAPPA, member)
    put_faces(numbers_ref, pieces_ref, F_FIRST, F_MAP, member)


def put_all(values, pieces_ref, rows, row):
    for piece in range(SIDE):
        pieces_ref[piece * rows + row : piece * rows + row + 1, :] = values[0:1, :]


def put_planes(field_ref, faces, pieces, outside):
    owner, member = position()
    left, right = get_faces(*faces, member, outside)
    pieces_ref, rows, plane_row, halo_row = pieces
    for there, plane in (
        (jnp.maximum(owner - 1, 0), 0),
        (jnp.minimum(owner + 1, SIDE - 1), 7),
    ):
        start = there * rows
        pieces_ref[pl.ds(start + plane_row, 8), :] = field_ref[8 * plane : 8 * plane + 8, :]
        for side, halo in enumerate((left, right)):
            pieces_ref[pl.ds(start + halo_row + side, 1), :] = halo[plane : plane + 1, :]


def gathered(rows, step):
    here = iota((SIDE, LANES), 0) % 8
    rows = jnp.where(iota((SIDE, LANES), 1) // SIDE == (here + step) % 8, rows, 0.0)
    parts = [jnp.sum(rows[at : at + 8], axis=0, keepdims=True) for at in (0, 8)]
    if step:
        parts = [
            pltpu.roll(jnp.broadcast_to(part, (8, LANES)), LANES - SIDE * step, 1)
            for part in parts
        ]
    return parts


def first_parts(faces_ref, pieces_ref):
    return (
        ((faces_ref, F_FIRST, F_FIELD), (pieces_ref, C_FIRST, C_FIELD, C_HALOS), 0.0),
        ((faces_ref, F_FIRST, F_KAPPA), (pieces_ref, C_FIRST, C_KAPPA, C_HALOS + 2), 0.0),
        ((faces_ref, F_FIRST, F_MAP), (pieces_ref, C_FIRST, C_MAP, C_HALOS + 4), -1.0),
    )


def second_parts(faces_ref, pieces_ref):
    return (faces_ref, F_SECOND, 0), (pieces_ref, C_SECOND, 0, C_HALO_2), 0.0


def relay_first(faces_ref, smoothed_ref, kappa_ref, numbers_ref, pieces_ref):
    rows = faces_ref[pl.ds(F_SOURCE, SIDE, stride=F_FIRST), :]
    for half in range(2):
        put_all(gathered(rows, 0)[half], pieces_ref, C_FIRST, C_SOURCE + half)
        put_all(gathered(rows, 1)[half], pieces_ref, C_FIRST, C_DIAGONAL + half)
    parts = first_parts(faces_ref, pieces_ref)
    for field_ref, part in zip((smoothed_ref, kappa_ref, numbers_ref), parts):
        put_planes(field_ref, *part)


def halves(pieces_ref, rows, row):
    return jnp.concatenate(
        [pieces_ref[pl.ds(row + half, SIDE, stride=rows), :] for half in range(2)], axis=1
    )


def first_image(
    faces_ref, ends_ref, own_ref, own_kappa_ref, numbers_ref, map_ref, order_ref,
    matrices_hbm,
    pieces_ref, field_ref, image_ref, smoothed_ref, kappa_ref, lanes_ref, diagonal_ref,
    picked_ref, product_ref, slabs_ref, rows_ref, matrices_ref, arrived,
):
    owner, member = position()
    copy = pltpu.make_async_copy(matrices_hbm, matrices_ref, arrived)
    copy.start()
    diagonal = halves(ends_ref, C_FIRST, C_DIAGONAL)
    diagonal_ref[...] = diagonal
    nearby(coarse_solve(halves(ends_ref, C_FIRST, C_SOURCE), diagonal), member, rows_ref)
    parts = first_parts(faces_ref, ends_ref)
    fill_slabs(slabs_ref, numbers_ref, *parts[2])
    row = iota((10, SLAB, LANES), 1)
    shift = jnp.where(row < 8, SIDE, jnp.where(row == RIGHT, 2 * SIDE, 0))
    number = slabs_ref[...]
    lanes_ref[...] = jnp.where(number >= 0.0, number.astype(jnp.int32) + shift, -1)
    fill_slabs(kappa_ref, own_kappa_ref, *parts[1])
    fill_slabs(slabs_ref, own_ref, *parts[0])
    add_prolonged(slabs_ref, lanes_ref, rows_ref)
    field = slabs_ref[...]
    field_ref[...] = field[1:9, :8].reshape(ROWS, LANES)
    image_ref[...] = operate(field, kappa_ref[...]).reshape(ROWS, LANES)
    pick(image_ref, order_ref, picked_ref)
    copy.wait()
    multiply_blocks(matrices_ref, picked_ref, product_ref)
    put_back(product_ref, order_ref, smoothed_ref)
    source = restrict(image_ref[...], offsets(map_ref[...]), member)
    put_all(source, pieces_ref, F_SECOND, F_SOURCE_2)
    put_faces(smoothed_ref, pieces_ref, F_SECOND, 0, member)


def relay_second(faces_ref, smoothed_ref, pieces_ref):
    rows = faces_ref[pl.ds(F_SOURCE_2, SIDE, stride=F_SECOND), :]
    for half, values in enumerate(gathered(rows, 0)):
        put_all(values, pieces_ref, C_SECOND, C_SOURCE_2 + half)
    put_planes(smoothed_ref, *second_parts(faces_ref, pieces_ref))


def second_image(
    faces_ref, ends_ref, own_ref, kappa_ref, lanes_ref, map_ref, order_ref,
    diagonal_ref, side_ref, first_ref, image_ref, matrices_hbm,
    pieces_ref, field_ref, second_ref, smoothed_ref,
    picked_ref, product_ref, slabs_ref, rows_ref, matrices_ref, arrived,
):
    owner, member = position()
    copy = pltpu.make_async_copy(matrices_hbm, matrices_ref, arrived)
    copy.start()
    nearby(coarse_solve(halves(ends_ref, C_SECOND, C_SOURCE_2), diagonal_ref[...]), member, rows_ref)
    fill_slabs(slabs_ref, own_ref, *second_parts(faces_ref, ends_ref))
    add_prolonged(slabs_ref, lanes_ref, rows_ref)
    slabs = slabs_ref[...]
    field = slabs[1:9, :8].reshape(ROWS, LANES)
    field_ref[...] = field
    second = operate(slabs, kappa_ref[...]).reshape(ROWS, LANES)
    second_ref[...] = second
    pick(second_ref, order_ref, picked_ref)
    copy.wait()
    multiply_blocks(matrices_ref, picked_ref, product_ref)
    put_back(product_ref, order_ref, smoothed_ref)
    first = first_ref[...]
    image = image_ref[...]
    pairs = (
        side_ref[...] * first,
        first * image,
        image * field,
        second * first,
        second * field,
        second * smoothed_ref[...],
    )
    lane = iota((8, LANES), 1)
    message = restrict(second, offsets(map_ref[...]), member)
    beside = lax.rem(member + 1, 8) * SIDE
    for number, pair in enumerate(pairs):
        total = jnp.sum(jnp.sum(pair, axis=0, keepdims=True), axis=1, keepdims=True)
        message = jnp.where(lane == beside + number, total, message)
    for start in range(0, WIDE, 8):
        pieces_ref[start : start + 8, :] = message


def finish(
    pieces_ref, diagonal_ref, map_ref, side_ref, first_ref, image_ref, field_ref, second_ref,
    smoothed_ref,
    solution_ref, residual_ref, search_ref,
):
    owner, member = position()
    pieces = pieces_ref[...].reshape(SIDE, SIDE, LANES)
    place = iota((SIDE, LANES), 0) % 8
    group = iota((SIDE, LANES), 1) // SIDE
    pieces_sum = jnp.sum(pieces, axis=0)
    sums = jnp.where(group == (place + 1) % 8, pieces_sum, 0.0)
    kept = jnp.where((group == place)[None], pieces, 0.0)
    source = jnp.concatenate(
        [jnp.sum(kept[:, :8], axis=1), jnp.sum(kept[:, 8:], axis=1)], axis=1
    )
    coarse = coarse_solve(source, diagonal_ref[...])
    lane = iota((1, LANES), 1)
    sums = jnp.sum(sums, axis=0, keepdims=True)

    def total(number):
        picked = jnp.where(lane % SIDE == number, sums, 0.0)
        return jnp.sum(picked, axis=1, keepdims=True)

    def whole(array):
        return jnp.sum(jnp.sum(array, axis=0, keepdims=True), axis=1, keepdims=True)

    r_z, z_az, w_y, v_z, v_y, v_bv = (total(number) for number in range(6))
    v_u = v_bv + 4.0 * whole(source * coarse)
    alpha = r_z / z_az
    following = r_z - 2.0 * alpha * z_az + alpha * alpha * w_y
    grown = 1.0 + following / r_z
    product = grown * grown * z_az - grown * alpha * (v_z + w_y) + alpha * alpha * v_y
    again = following / product
    one = alpha + again * grown
    two = again * alpha
    last = (
        r_z - 2.0 * one * z_az + 2.0 * two * v_z + one * one * w_y
        - 2.0 * one * two * v_y + two * two * v_u
    )
    ratio = last / following
    lanes = iota((SIDE, WIDE), 1)
    rows = iota((SIDE, WIDE), 0)
    near = pltpu.roll(coarse, lax.rem((SIDE - member) * SIDE, WIDE), 1)[:, :LANES]
    row = jnp.sum(
        jnp.where(iota((SIDE, LANES), 0) == owner, near, 0.0), axis=0, keepdims=True
    )
    row = jnp.broadcast_to(row, (8, LANES))
    for g in range(8):
        at = slice(8 * g, 8 * g + 8)
        first, image, field, second = (
            ref[at, :] for ref in (first_ref, image_ref, field_ref, second_ref)
        )
        smoothed = smoothed_ref[at, :] + take_lanes(row, map_ref[at, :])
        solution_ref[at, :] = one * first - two * field
        residual_ref[at, :] = side_ref[at, :] - one * image + two * second
        search_ref[at, :] = (
            first - one * field + two * smoothed + ratio * (grown * first - alpha * field)
        )


def shards(
    right_side, coefficient_index, material_coefficients, block_cells, block_inverses,
    aggregate_map, coarse_diagonal,
):
    dims = right_side.shape
    side = right_side.reshape(ROWS, LANES)
    index = coefficient_index.reshape(ROWS, LANES)
    order = block_cells.reshape(ROWS, LANES)
    matrices = block_inverses.reshape(ROWS, LANES, LANES)
    aggregate = aggregate_map.reshape(ROWS, LANES)
    diagonal = coarse_diagonal.reshape(1, SIDE)
    local = shape(ROWS, LANES)
    cells = pltpu.VMEM((ROWS, LANES), F32)
    int_cells = pltpu.VMEM((ROWS, LANES), jnp.int32)
    held = pltpu.VMEM(matrices.shape, F32)
    scratch = [
        cells, cells, pltpu.VMEM((10, SLAB, LANES), F32), pltpu.VMEM((SIDE, LANES), F32),
        held, pltpu.SemaphoreType.DMA,
    ]

    def call(kernel, outs, ins, scratch=(), specs=None):
        return pl.pallas_call(
            kernel,
            out_shape=outs,
            in_specs=specs or [vmem()] * ins,
            out_specs=[vmem()] * len(outs),
            scratch_shapes=list(scratch),
            compiler_params=params(),
        )

    def exchange(pieces, axis):
        rows = pieces.shape
        pieces = lax.all_to_all(pieces.reshape(rows[0], 1, LANES), axis, 0, 0, tiled=True)
        return pieces.reshape(rows)

    fixed = [
        pltpu.with_memory_space_constraint(array, pltpu.HBM)
        for array in (material_coefficients, side, index, order, matrices, aggregate, diagonal)
    ]
    pieces, kappa, smoothed, numbers = call(
        begin,
        [
            shape(SIDE * F_FIRST, LANES), local, local, local,
        ],
        7,
        [
            pltpu.SMEM(material_coefficients.shape, F32), cells, int_cells, int_cells,
            int_cells, pltpu.VMEM((1, SIDE), F32), cells, cells,
            held, pltpu.SemaphoreType.DMA((7,)),
        ],
        [hbm()] * 7,
    )(*fixed)
    faces = exchange(pieces, FINE)
    (pieces,) = call(relay_first, [shape(SIDE * C_FIRST, LANES)], 4)(
        faces, smoothed, kappa, numbers
    )
    ends = exchange(pieces, COARSE)
    pieces, first, image, smoothed, kappa, lanes, diagonals = call(
        first_image,
        [
            shape(SIDE * F_SECOND, LANES), local, local, local, shape(10, SLAB, LANES),
            shape(10, SLAB, LANES, dtype=jnp.int32), shape(SIDE, WIDE),
        ],
        11,
        scratch,
        [vmem()] * 7 + [hbm()],
    )(
        faces, ends, smoothed, kappa, numbers, aggregate, order, fixed[4],
    )
    faces = exchange(pieces, FINE)
    (pieces,) = call(relay_second, [shape(SIDE * C_SECOND, LANES)], 2)(faces, smoothed)
    ends = exchange(pieces, COARSE)
    pieces, field, second, smoothed = call(
        second_image,
        [shape(WIDE, LANES), local, local, local],
        13,
        scratch,
        [vmem()] * 11 + [hbm()],
    )(
        faces, ends, smoothed, kappa, lanes, aggregate, order, diagonals, side, first,
        image, fixed[4],
    )
    pieces = exchange(pieces, (COARSE, FINE))
    results = call(finish, [local, local, local], 9)(
        pieces, diagonals, aggregate, side, first, image, field, second, smoothed
    )
    return tuple(result.reshape(dims) for result in results)


def solution(mesh):
    cells = P(COARSE, FINE, None)
    in_specs = (
        cells,
        cells,
        P(),
        P(COARSE, FINE, None, None),
        P(COARSE, FINE, None, None, None),
        cells,
        cells,
    )
    return jax.shard_map(
        shards, mesh=mesh, in_specs=in_specs, out_specs=(cells,) * 3, check_vma=False
    )
```

```python
import functools

import jax
import jax.numpy as jnp
from jax import lax
from jax.experimental import pallas as pl
from jax.experimental.pallas import tpu as pltpu
from jax.sharding import PartitionSpec as P

AGG = 8
COARSE, FINE = "coarse", "fine"
SWEEPS = 4
OMEGA = 0.8
SIDE = 16
ROWS = 64
LANES = 128
WIDE = SIDE * SIDE
F32, BF16 = jnp.float32, jnp.bfloat16
GROUP = 8

SLAB = 16
RIGHT, LEFT = 8, 15


def vmem():
    return pl.BlockSpec(memory_space=pltpu.VMEM)


def smem():
    return pl.BlockSpec(memory_space=pltpu.SMEM)


def hbm():
    return pl.BlockSpec(memory_space=pltpu.HBM)


def params():
    return pltpu.CompilerParams(vmem_limit_bytes=24 * 1024 * 1024)


def shape(*dims, dtype=F32):
    return jax.ShapeDtypeStruct(dims, dtype)


def iota(dims, axis):
    return lax.broadcasted_iota(jnp.int32, dims, axis)


def take_lanes(values, lanes):
    numbers = lax.GatherDimensionNumbers(
        offset_dims=(),
        collapsed_slice_dims=(1,),
        start_index_map=(1,),
        operand_batching_dims=(0,),
        start_indices_batching_dims=(0,),
    )
    return lax.gather(
        values,
        lanes[..., None],
        numbers,
        slice_sizes=(1, 1),
        mode=lax.GatherScatterMode.PROMISE_IN_BOUNDS,
    )


def split(values):
    high = values.astype(BF16)
    return high, (values - high.astype(F32)).astype(BF16)


def matmul(left, right, left_dim, right_dim):
    dims = (((left_dim,), (right_dim,)), ((), ()))
    return lax.dot_general(left, right, dims, preferred_element_type=F32)


def lane_hits(order_ref, group):
    lane = iota((LANES, LANES), 0)
    return jnp.concatenate(
        [
            jnp.where(lane == order_ref[b : b + 1, :] % LANES, 1.0, 0.0).astype(BF16)
            for b in range(group * GROUP, group * GROUP + GROUP)
        ],
        axis=1,
    )


def row_hit(order_ref, block):
    return iota((ROWS, LANES), 0) == order_ref[block : block + 1, :] // LANES


def column_sum(values):
    total = jnp.sum(values.reshape(-1, 8, LANES), axis=0)
    return jnp.sum(total, axis=0, keepdims=True)


def pick(source_ref, order_ref, picked_ref):
    source = jnp.concatenate(split(source_ref[...]), axis=0)
    for group in range(ROWS // GROUP):
        start = group * GROUP
        found = matmul(source, lane_hits(order_ref, group), 1, 0)
        found = found[:ROWS] + found[ROWS:]
        rows = []
        for part in range(GROUP):
            column = found[:, LANES * part : LANES * (part + 1)]
            rows.append(column_sum(jnp.where(row_hit(order_ref, start + part), column, 0.0)))
        picked_ref[start : start + GROUP, :] = jnp.concatenate(rows, axis=0)


def multiply_blocks(matrices_ref, picked_ref, product_ref):
    wide = (2 * GROUP, GROUP * LANES)
    spread = jnp.where(iota(wide, 0) % GROUP == iota(wide, 1) // LANES, 1.0, 0.0).astype(BF16)
    for start in range(0, ROWS, GROUP):
        high, low = split(picked_ref[start : start + GROUP, :])
        both = jnp.concatenate([high.astype(F32), low.astype(F32)], axis=0)
        columns = matmul(jnp.transpose(both).astype(BF16), spread, 1, 0)
        rows = [
            column_sum(
                matrices_ref[start + part] * columns[:, LANES * part : LANES * (part + 1)]
            )
            for part in range(GROUP)
        ]
        product_ref[start : start + GROUP, :] = jnp.concatenate(rows, axis=0)


def put_back(product_ref, order_ref, target_ref):
    total = jnp.zeros((2 * ROWS, LANES), F32)
    for group in range(ROWS // GROUP):
        start = group * GROUP
        halves_of = [part.astype(F32) for part in split(product_ref[start : start + GROUP, :])]
        hits = [row_hit(order_ref, start + part) for part in range(GROUP)]
        values = [
            jnp.concatenate(
                [
                    jnp.where(hits[part], half[part : part + 1, :], 0.0).astype(BF16)
                    for part in range(GROUP)
                ],
                axis=1,
            )
            for half in halves_of
        ]
        total = total + matmul(
            jnp.concatenate(values, axis=0), lane_hits(order_ref, group), 1, 1
        )
    target_ref[...] = total[:ROWS] + total[ROWS:]


def restrict(field, offset, member):
    total = jnp.sum(jnp.where(offset == 0, field, 0.0), axis=0, keepdims=True)
    up = jnp.sum(jnp.where(offset == 1, field, 0.0), axis=0, keepdims=True)
    down = jnp.sum(jnp.where(offset == -1, field, 0.0), axis=0, keepdims=True)
    total, up, down = (jnp.broadcast_to(x, (8, LANES)) for x in (total, up, down))
    total = total + pltpu.roll(up, AGG, 1) + pltpu.roll(down, LANES - AGG, 1)
    for distance in (1, 2, 4):
        total = total + pltpu.roll(total, LANES - distance, 1)
    lane = iota((8, LANES), 1)
    total = 0.25 * take_lanes(total, (lane % SIDE) * AGG)
    return jnp.where(lane // SIDE == member % 8, total, 0.0)


def moved(values, distance, axis, keep):
    size = values.shape[axis]
    return jnp.where(keep, pltpu.roll(values, distance % size, axis), 0.0)


def coarse_solve(source, diagonal):
    owner, lane = iota((SIDE, WIDE), 0), iota((SIDE, WIDE), 1)
    cell = lane % SIDE
    weight = OMEGA / (6.0 + diagonal)
    guess = weight * source
    for sweep in range(SWEEPS - 1):
        beside = moved(guess, 1, 0, owner > 0) + moved(guess, -1, 0, owner < SIDE - 1)
        beside = beside + moved(guess, SIDE, 1, lane >= SIDE)
        beside = beside + moved(guess, -SIDE, 1, lane < WIDE - SIDE)
        beside = beside + moved(guess, 1, 1, cell > 0) + moved(guess, -1, 1, cell < SIDE - 1)
        guess = (1.0 - OMEGA) * guess + weight * (source + beside)
    return guess


def nearby(coarse, member, rows_ref):
    rows_ref[...] = pltpu.roll(coarse, lax.rem((SIDE + 1 - member) * SIDE, WIDE), 1)[:, :LANES]


def smooth(slabs):
    total = slabs[1:9] + 0.5 * (slabs[0:8] + slabs[2:10])
    planes = []
    lane = iota((8, LANES), 1)
    row = iota((8, LANES), 0)
    for plane in range(8):
        own, ends = total[plane, :8], total[plane, 8:]
        before = jnp.where(row == 0, ends[LEFT - 8 :, :], pltpu.roll(own, 1, 0))
        after = jnp.where(row == 7, ends[:1, :], pltpu.roll(own, 7, 0))
        own = own + 0.5 * (before + after)
        below = jnp.where(lane > 0, pltpu.roll(own, 1, 1), 0.0)
        above = jnp.where(lane < LANES - 1, pltpu.roll(own, LANES - 1, 1), 0.0)
        planes.append(own + 0.5 * (below + above))
    return jnp.stack(planes)


def position():
    return lax.axis_index(COARSE), lax.axis_index(FINE)


def put_faces(field_ref, pieces_ref, rows, row, member):
    before, after = jnp.maximum(member - 1, 0), jnp.minimum(member + 1, SIDE - 1)
    pieces_ref[pl.ds(before * rows + row, 8), :] = field_ref[pl.ds(0, 8, stride=8), :]
    pieces_ref[pl.ds(after * rows + row, 8), :] = field_ref[pl.ds(7, 8, stride=8), :]


def get_faces(pieces_ref, rows, row, member, outside):
    before, after = jnp.maximum(member - 1, 0), jnp.minimum(member + 1, SIDE - 1)
    left = pieces_ref[pl.ds(before * rows + row, 8), :]
    right = pieces_ref[pl.ds(after * rows + row, 8), :]
    left = jnp.where(member > 0, left, outside)
    right = jnp.where(member < SIDE - 1, right, outside)
    return left, right


def fill_slabs(slabs_ref, field_ref, faces, pieces, outside, planes):
    owner, member = position()
    pieces_ref, rows, halo_row = pieces
    left, right = get_faces(*faces, member, outside)
    gap = jnp.full((8, LANES), outside, F32)
    for plane in range(8):
        slabs_ref[plane + 1, :8, :] = field_ref[8 * plane : 8 * plane + 8, :]
        slabs_ref[plane + 1, 8:, :] = gap
        slabs_ref[plane + 1, RIGHT : RIGHT + 1, :] = right[plane : plane + 1, :]
        slabs_ref[plane + 1, LEFT : LEFT + 1, :] = left[plane : plane + 1, :]
    for plane, there, inside, own in (
        (0, jnp.maximum(owner - 1, 0), owner > 0, planes[0]),
        (9, jnp.minimum(owner + 1, SIDE - 1), owner < SIDE - 1, planes[1]),
    ):
        start = there * rows
        slabs_ref[plane, 8:, :] = gap
        slabs_ref[plane, :8, :] = jnp.where(inside, own, outside)
        for side, target in enumerate((LEFT, RIGHT)):
            slabs_ref[plane, target : target + 1, :] = jnp.where(
                inside, pieces_ref[pl.ds(start + halo_row + side, 1), :], outside
            )


def add_prolonged(slabs_ref, numbers_ref, rows_ref):
    owner, member = position()
    for plane in range(10):
        if plane == 0:
            there = jnp.maximum(owner - 1, 0)
        elif plane == 9:
            there = jnp.minimum(owner + 1, SIDE - 1)
        else:
            there = owner
        row = jnp.broadcast_to(rows_ref[pl.ds(there, 1), :], (8, LANES))
        for part in (0, 8):
            number = numbers_ref[plane, part : part + 8, :]
            value = take_lanes(row, jnp.maximum(number, 0))
            slabs_ref[plane, part : part + 8, :] += jnp.where(number >= 0, value, 0.0)


def operate(field, kappa):
    own, own_kappa = field[1:9, :8], kappa[1:9, :8]
    return own_kappa * (8.0 * own - smooth(field)) + own * smooth(kappa) - smooth(
        kappa * field
    )


def offsets(aggregate):
    return aggregate - iota((ROWS, LANES), 1) // AGG


F_FIELD, F_KAPPA, F_MAP, F_SOURCE, F_FIRST = 0, 8, 16, 24, 25
C_FIELD, C_HALOS, C_SOURCE, C_DIAGONAL, C_FIRST = 0, 8, 14, 16, 18
F_SOURCE_2, F_SECOND = 8, 9
C_HALO_2, C_SOURCE_2, C_SECOND = 8, 10, 12


def fetch(pairs, arrived):
    copies = [
        pltpu.make_async_copy(source, target, arrived.at[number])
        for number, (source, target) in enumerate(pairs)
    ]
    for copy in copies:
        copy.start()
    return copies


def prepare(
    table_hbm, index_hbm, map_hbm,
    kappa_ref, numbers_ref, before_ref, after_ref,
    table_ref, index_ref, map_ref, arrived,
):
    pairs = (table_hbm, table_ref), (index_hbm, index_ref), (map_hbm, map_ref)
    for copy in fetch(pairs, arrived):
        copy.wait()
    index = index_ref[...]
    kappa = jnp.zeros((ROWS, LANES), F32)
    for entry in range(table_ref.shape[0]):
        kappa = jnp.where(index == entry, table_ref[entry], kappa)
    kappa_ref[...] = kappa
    numbers = map_ref[...].astype(F32)
    numbers_ref[...] = numbers
    before_ref[:8, :], before_ref[8:, :] = kappa[:8], numbers[:8]
    after_ref[:8, :], after_ref[8:, :] = kappa[56:], numbers[56:]


def begin(
    side_hbm, order_hbm, matrices_hbm, diagonal_hbm, kappa_ref, numbers_ref,
    pieces_ref, smoothed_ref,
    side_ref, order_ref, matrices_ref, diagonal_ref, picked_ref, product_ref, arrived,
):
    owner, member = position()
    pairs = (
        (side_hbm, side_ref),
        (order_hbm, order_ref),
        (diagonal_hbm, diagonal_ref),
        (matrices_hbm, matrices_ref),
    )
    copies = fetch(pairs, arrived)
    for copy in copies[:-1]:
        copy.wait()
    pick(side_ref, order_ref, picked_ref)
    copies[-1].wait()
    multiply_blocks(matrices_ref, picked_ref, product_ref)
    put_back(product_ref, order_ref, smoothed_ref)
    aggregate = numbers_ref[...].astype(jnp.int32)
    source = restrict(side_ref[...], offsets(aggregate), member)
    spread = jnp.broadcast_to(jnp.concatenate([diagonal_ref[...]] * 8, axis=1), (8, LANES))
    beside = iota((8, LANES), 1) // SIDE == (member + 1) % 8
    put_all(jnp.where(beside, spread, source), pieces_ref, F_FIRST, F_SOURCE)
    put_faces(smoothed_ref, pieces_ref, F_FIRST, F_FIELD, member)
    put_faces(kappa_ref, pieces_ref, F_FIRST, F_KAPPA, member)
    put_faces(numbers_ref, pieces_ref, F_FIRST, F_MAP, member)


def put_all(values, pieces_ref, rows, row):
    for piece in range(SIDE):
        pieces_ref[piece * rows + row : piece * rows + row + 1, :] = values[0:1, :]


def put_halos(faces, pieces, outside):
    owner, member = position()
    left, right = get_faces(*faces, member, outside)
    pieces_ref, rows, row = pieces
    for there, plane in (
        (jnp.maximum(owner - 1, 0), 0),
        (jnp.minimum(owner + 1, SIDE - 1), 7),
    ):
        for side, halo in enumerate((left, right)):
            pieces_ref[pl.ds(there * rows + row + side, 1), :] = halo[plane : plane + 1, :]


def put_planes(field_ref, pieces_ref, rows):
    owner, member = position()
    before, after = jnp.maximum(owner - 1, 0), jnp.minimum(owner + 1, SIDE - 1)
    pieces_ref[pl.ds(before * rows, 8), :] = field_ref[:8, :]
    pieces_ref[pl.ds(after * rows, 8), :] = field_ref[56:, :]


def get_planes(pieces_ref, rows):
    owner, member = position()
    before, after = jnp.maximum(owner - 1, 0), jnp.minimum(owner + 1, SIDE - 1)
    return pieces_ref[pl.ds(before * rows, 8), :], pieces_ref[pl.ds(after * rows, 8), :]


def gathered(rows, step):
    here = iota((SIDE, LANES), 0) % 8
    rows = jnp.where(iota((SIDE, LANES), 1) // SIDE == (here + step) % 8, rows, 0.0)
    parts = [jnp.sum(rows[at : at + 8], axis=0, keepdims=True) for at in (0, 8)]
    if step:
        parts = [
            pltpu.roll(jnp.broadcast_to(part, (8, LANES)), LANES - SIDE * step, 1)
            for part in parts
        ]
    return parts


def first_parts(faces_ref, pieces_ref):
    return (
        ((faces_ref, F_FIRST, F_FIELD), (pieces_ref, C_FIRST, C_HALOS), 0.0),
        ((faces_ref, F_FIRST, F_KAPPA), (pieces_ref, C_FIRST, C_HALOS + 2), 0.0),
        ((faces_ref, F_FIRST, F_MAP), (pieces_ref, C_FIRST, C_HALOS + 4), -1.0),
    )


def second_parts(faces_ref, pieces_ref):
    return (faces_ref, F_SECOND, 0), (pieces_ref, C_SECOND, C_HALO_2), 0.0


def relay_first(faces_ref, smoothed_ref, pieces_ref):
    rows = faces_ref[pl.ds(F_SOURCE, SIDE, stride=F_FIRST), :]
    for half in range(2):
        put_all(gathered(rows, 0)[half], pieces_ref, C_FIRST, C_SOURCE + half)
        put_all(gathered(rows, 1)[half], pieces_ref, C_FIRST, C_DIAGONAL + half)
    put_planes(smoothed_ref, pieces_ref, C_FIRST)
    for part in first_parts(faces_ref, pieces_ref):
        put_halos(*part)


def halves(pieces_ref, rows, row):
    return jnp.concatenate(
        [pieces_ref[pl.ds(row + half, SIDE, stride=rows), :] for half in range(2)], axis=1
    )


def first_image(
    faces_ref, ends_ref, before_ref, after_ref, own_ref, own_kappa_ref, numbers_ref, map_ref, order_ref,
    matrices_hbm,
    pieces_ref, field_ref, image_ref, smoothed_ref, kappa_ref, lanes_ref, diagonal_ref,
    picked_ref, product_ref, slabs_ref, rows_ref, matrices_ref, arrived,
):
    owner, member = position()
    copy = pltpu.make_async_copy(matrices_hbm, matrices_ref, arrived)
    copy.start()
    diagonal = halves(ends_ref, C_FIRST, C_DIAGONAL)
    diagonal_ref[...] = diagonal
    nearby(coarse_solve(halves(ends_ref, C_FIRST, C_SOURCE), diagonal), member, rows_ref)
    parts = first_parts(faces_ref, ends_ref)
    fill_slabs(slabs_ref, numbers_ref, *parts[2], (before_ref[8:, :], after_ref[8:, :]))
    row = iota((10, SLAB, LANES), 1)
    shift = jnp.where(row < 8, SIDE, jnp.where(row == RIGHT, 2 * SIDE, 0))
    number = slabs_ref[...]
    lanes_ref[...] = jnp.where(number >= 0.0, number.astype(jnp.int32) + shift, -1)
    fill_slabs(kappa_ref, own_kappa_ref, *parts[1], (before_ref[:8, :], after_ref[:8, :]))
    fill_slabs(slabs_ref, own_ref, *parts[0], get_planes(ends_ref, C_FIRST))
    add_prolonged(slabs_ref, lanes_ref, rows_ref)
    field = slabs_ref[...]
    field_ref[...] = field[1:9, :8].reshape(ROWS, LANES)
    image_ref[...] = operate(field, kappa_ref[...]).reshape(ROWS, LANES)
    pick(image_ref, order_ref, picked_ref)
    copy.wait()
    multiply_blocks(matrices_ref, picked_ref, product_ref)
    put_back(product_ref, order_ref, smoothed_ref)
    source = restrict(image_ref[...], offsets(map_ref[...]), member)
    put_all(source, pieces_ref, F_SECOND, F_SOURCE_2)
    put_faces(smoothed_ref, pieces_ref, F_SECOND, 0, member)


def relay_second(faces_ref, smoothed_ref, pieces_ref):
    rows = faces_ref[pl.ds(F_SOURCE_2, SIDE, stride=F_SECOND), :]
    for half, values in enumerate(gathered(rows, 0)):
        put_all(values, pieces_ref, C_SECOND, C_SOURCE_2 + half)
    put_planes(smoothed_ref, pieces_ref, C_SECOND)
    put_halos(*second_parts(faces_ref, pieces_ref))


def second_image(
    faces_ref, ends_ref, own_ref, kappa_ref, lanes_ref, map_ref, order_ref,
    diagonal_ref, side_ref, first_ref, image_ref, matrices_hbm,
    pieces_ref, field_ref, second_ref, smoothed_ref,
    picked_ref, product_ref, slabs_ref, rows_ref, matrices_ref, arrived,
):
    owner, member = position()
    copy = pltpu.make_async_copy(matrices_hbm, matrices_ref, arrived)
    copy.start()
    nearby(coarse_solve(halves(ends_ref, C_SECOND, C_SOURCE_2), diagonal_ref[...]), member, rows_ref)
    planes = get_planes(ends_ref, C_SECOND)
    fill_slabs(slabs_ref, own_ref, *second_parts(faces_ref, ends_ref), planes)
    add_prolonged(slabs_ref, lanes_ref, rows_ref)
    slabs = slabs_ref[...]
    field = slabs[1:9, :8].reshape(ROWS, LANES)
    field_ref[...] = field
    second = operate(slabs, kappa_ref[...]).reshape(ROWS, LANES)
    second_ref[...] = second
    pick(second_ref, order_ref, picked_ref)
    copy.wait()
    multiply_blocks(matrices_ref, picked_ref, product_ref)
    put_back(product_ref, order_ref, smoothed_ref)
    first = first_ref[...]
    image = image_ref[...]
    pairs = (
        side_ref[...] * first,
        first * image,
        image * field,
        second * first,
        second * field,
        second * smoothed_ref[...],
    )
    lane = iota((8, LANES), 1)
    message = restrict(second, offsets(map_ref[...]), member)
    beside = lax.rem(member + 1, 8) * SIDE
    for number, pair in enumerate(pairs):
        total = jnp.sum(jnp.sum(pair, axis=0, keepdims=True), axis=1, keepdims=True)
        message = jnp.where(lane == beside + number, total, message)
    for start in range(0, WIDE, 8):
        pieces_ref[start : start + 8, :] = message


def finish(
    pieces_ref, diagonal_ref, map_ref, side_ref, first_ref, image_ref, field_ref, second_ref,
    smoothed_ref,
    solution_ref, residual_ref, search_ref,
):
    owner, member = position()
    pieces = pieces_ref[...].reshape(SIDE, SIDE, LANES)
    place = iota((SIDE, LANES), 0) % 8
    group = iota((SIDE, LANES), 1) // SIDE
    pieces_sum = jnp.sum(pieces, axis=0)
    sums = jnp.where(group == (place + 1) % 8, pieces_sum, 0.0)
    kept = jnp.where((group == place)[None], pieces, 0.0)
    source = jnp.concatenate(
        [jnp.sum(kept[:, :8], axis=1), jnp.sum(kept[:, 8:], axis=1)], axis=1
    )
    coarse = coarse_solve(source, diagonal_ref[...])
    lane = iota((1, LANES), 1)
    sums = jnp.sum(sums, axis=0, keepdims=True)

    def total(number):
        picked = jnp.where(lane % SIDE == number, sums, 0.0)
        return jnp.sum(picked, axis=1, keepdims=True)

    def whole(array):
        return jnp.sum(jnp.sum(array, axis=0, keepdims=True), axis=1, keepdims=True)

    r_z, z_az, w_y, v_z, v_y, v_bv = (total(number) for number in range(6))
    v_u = v_bv + 4.0 * whole(source * coarse)
    alpha = r_z / z_az
    following = r_z - 2.0 * alpha * z_az + alpha * alpha * w_y
    grown = 1.0 + following / r_z
    product = grown * grown * z_az - grown * alpha * (v_z + w_y) + alpha * alpha * v_y
    again = following / product
    one = alpha + again * grown
    two = again * alpha
    last = (
        r_z - 2.0 * one * z_az + 2.0 * two * v_z + one * one * w_y
        - 2.0 * one * two * v_y + two * two * v_u
    )
    ratio = last / following
    lanes = iota((SIDE, WIDE), 1)
    rows = iota((SIDE, WIDE), 0)
    near = pltpu.roll(coarse, lax.rem((SIDE - member) * SIDE, WIDE), 1)[:, :LANES]
    row = jnp.sum(
        jnp.where(iota((SIDE, LANES), 0) == owner, near, 0.0), axis=0, keepdims=True
    )
    row = jnp.broadcast_to(row, (8, LANES))
    for g in range(8):
        at = slice(8 * g, 8 * g + 8)
        first, image, field, second = (
            ref[at, :] for ref in (first_ref, image_ref, field_ref, second_ref)
        )
        smoothed = smoothed_ref[at, :] + take_lanes(row, map_ref[at, :])
        solution_ref[at, :] = one * first - two * field
        residual_ref[at, :] = side_ref[at, :] - one * image + two * second
        search_ref[at, :] = (
            first - one * field + two * smoothed + ratio * (grown * first - alpha * field)
        )


def shards(
    right_side, coefficient_index, material_coefficients, block_cells, block_inverses,
    aggregate_map, coarse_diagonal,
):
    dims = right_side.shape
    side = right_side.reshape(ROWS, LANES)
    index = coefficient_index.reshape(ROWS, LANES)
    order = block_cells.reshape(ROWS, LANES)
    matrices = block_inverses.reshape(ROWS, LANES, LANES)
    aggregate = aggregate_map.reshape(ROWS, LANES)
    diagonal = coarse_diagonal.reshape(1, SIDE)
    local = shape(ROWS, LANES)
    cells = pltpu.VMEM((ROWS, LANES), F32)
    int_cells = pltpu.VMEM((ROWS, LANES), jnp.int32)
    held = pltpu.VMEM(matrices.shape, F32)
    scratch = [
        cells, cells, pltpu.VMEM((10, SLAB, LANES), F32), pltpu.VMEM((SIDE, LANES), F32),
        held, pltpu.SemaphoreType.DMA,
    ]

    def call(kernel, outs, ins, scratch=(), specs=None):
        return pl.pallas_call(
            kernel,
            out_shape=outs,
            in_specs=specs or [vmem()] * ins,
            out_specs=[vmem()] * len(outs),
            scratch_shapes=list(scratch),
            compiler_params=params(),
            cost_estimate=pl.CostEstimate(
                flops=2 * 10**9, bytes_accessed=8 * 10**6, transcendentals=0
            ),
        )

    def exchange(pieces, axis):
        rows = pieces.shape
        pieces = lax.all_to_all(pieces.reshape(rows[0], 1, LANES), axis, 0, 0, tiled=True)
        return pieces.reshape(rows)

    def ring(planes, step):
        return lax.ppermute(planes, COARSE, [(i, (i + step) % SIDE) for i in range(SIDE)])

    def pinned(array):
        return pltpu.with_memory_space_constraint(array, pltpu.HBM)

    matrices = pinned(matrices)
    copied = pltpu.SemaphoreType.DMA((4,))
    kappa, numbers, before, after = call(
        prepare,
        [local, local, shape(16, LANES), shape(16, LANES)],
        3,
        [pltpu.SMEM(material_coefficients.shape, F32), int_cells, int_cells, copied],
        [hbm()] * 3,
    )(pinned(material_coefficients), pinned(index), pinned(aggregate))
    after, before = ring(before, -1), ring(after, 1)
    pieces, smoothed = call(
        begin,
        [shape(SIDE * F_FIRST, LANES), local],
        6,
        [cells, int_cells, held, pltpu.VMEM((1, SIDE), F32), cells, cells, copied],
        [hbm()] * 4 + [vmem()] * 2,
    )(pinned(side), pinned(order), matrices, pinned(diagonal), kappa, numbers)
    pieces, before, after = lax.optimization_barrier((pieces, before, after))
    faces = exchange(pieces, FINE)
    (pieces,) = call(relay_first, [shape(SIDE * C_FIRST, LANES)], 2)(faces, smoothed)
    ends = exchange(pieces, COARSE)
    pieces, first, image, smoothed, kappa, lanes, diagonals = call(
        first_image,
        [
            shape(SIDE * F_SECOND, LANES), local, local, local, shape(10, SLAB, LANES),
            shape(10, SLAB, LANES, dtype=jnp.int32), shape(SIDE, WIDE),
        ],
        11,
        scratch,
        [vmem()] * 9 + [hbm()],
    )(
        faces, ends, before, after, smoothed, kappa, numbers, aggregate, order, matrices,
    )
    faces = exchange(pieces, FINE)
    (pieces,) = call(relay_second, [shape(SIDE * C_SECOND, LANES)], 2)(faces, smoothed)
    ends = exchange(pieces, COARSE)
    pieces, field, second, smoothed = call(
        second_image,
        [shape(WIDE, LANES), local, local, local],
        13,
        scratch,
        [vmem()] * 11 + [hbm()],
    )(
        faces, ends, smoothed, kappa, lanes, aggregate, order, diagonals, side, first,
        image, matrices,
    )
    pieces = exchange(pieces, (COARSE, FINE))
    results = call(finish, [local, local, local], 9)(
        pieces, diagonals, aggregate, side, first, image, field, second, smoothed
    )
    return tuple(result.reshape(dims) for result in results)


def solution(mesh):
    cells = P(COARSE, FINE, None)
    in_specs = (
        cells,
        cells,
        P(),
        P(COARSE, FINE, None, None),
        P(COARSE, FINE, None, None, None),
        cells,
        cells,
    )
    return jax.shard_map(
        shards, mesh=mesh, in_specs=in_specs, out_specs=(cells,) * 3, check_vma=False
    )
```

```python
import functools

import jax
import jax.numpy as jnp
from jax import lax
from jax.experimental import pallas as pl
from jax.experimental.pallas import tpu as pltpu
from jax.sharding import PartitionSpec as P

AGG = 8
COARSE, FINE = "coarse", "fine"
SWEEPS = 4
OMEGA = 0.8
SIDE = 16
ROWS = 64
LANES = 128
WIDE = SIDE * SIDE
F32, BF16 = jnp.float32, jnp.bfloat16
GROUP = 8

SLAB = 16
RIGHT, LEFT = 8, 15


def vmem():
    return pl.BlockSpec(memory_space=pltpu.VMEM)


def smem():
    return pl.BlockSpec(memory_space=pltpu.SMEM)


def hbm():
    return pl.BlockSpec(memory_space=pltpu.HBM)


def params():
    return pltpu.CompilerParams(vmem_limit_bytes=24 * 1024 * 1024)


def shape(*dims, dtype=F32):
    return jax.ShapeDtypeStruct(dims, dtype)


def iota(dims, axis):
    return lax.broadcasted_iota(jnp.int32, dims, axis)


def take_lanes(values, lanes):
    numbers = lax.GatherDimensionNumbers(
        offset_dims=(),
        collapsed_slice_dims=(1,),
        start_index_map=(1,),
        operand_batching_dims=(0,),
        start_indices_batching_dims=(0,),
    )
    return lax.gather(
        values,
        lanes[..., None],
        numbers,
        slice_sizes=(1, 1),
        mode=lax.GatherScatterMode.PROMISE_IN_BOUNDS,
    )


def split(values):
    high = values.astype(BF16)
    return high, (values - high.astype(F32)).astype(BF16)


def matmul(left, right, left_dim, right_dim):
    dims = (((left_dim,), (right_dim,)), ((), ()))
    return lax.dot_general(left, right, dims, preferred_element_type=F32)


def lane_hits(order_ref, group):
    lane = iota((LANES, LANES), 0)
    return jnp.concatenate(
        [
            jnp.where(lane == order_ref[b : b + 1, :] % LANES, 1.0, 0.0).astype(BF16)
            for b in range(group * GROUP, group * GROUP + GROUP)
        ],
        axis=1,
    )


def row_hit(order_ref, block):
    return iota((ROWS, LANES), 0) == order_ref[block : block + 1, :] // LANES


def column_sum(values):
    total = jnp.sum(values.reshape(-1, 8, LANES), axis=0)
    return jnp.sum(total, axis=0, keepdims=True)


def pick(source_ref, order_ref, picked_ref):
    source = jnp.concatenate(split(source_ref[...]), axis=0)
    for group in range(ROWS // GROUP):
        start = group * GROUP
        found = matmul(source, lane_hits(order_ref, group), 1, 0)
        found = found[:ROWS] + found[ROWS:]
        rows = []
        for part in range(GROUP):
            column = found[:, LANES * part : LANES * (part + 1)]
            rows.append(column_sum(jnp.where(row_hit(order_ref, start + part), column, 0.0)))
        picked_ref[start : start + GROUP, :] = jnp.concatenate(rows, axis=0)


def multiply_blocks(matrices_ref, picked_ref, product_ref, copies=()):
    wide = (2 * GROUP, GROUP * LANES)
    spread = jnp.where(iota(wide, 0) % GROUP == iota(wide, 1) // LANES, 1.0, 0.0).astype(BF16)
    for start in range(0, ROWS, GROUP):
        if copies:
            copies[start // GROUP].wait()
        high, low = split(picked_ref[start : start + GROUP, :])
        both = jnp.concatenate([high.astype(F32), low.astype(F32)], axis=0)
        columns = matmul(jnp.transpose(both).astype(BF16), spread, 1, 0)
        rows = [
            column_sum(
                matrices_ref[start + part] * columns[:, LANES * part : LANES * (part + 1)]
            )
            for part in range(GROUP)
        ]
        product_ref[start : start + GROUP, :] = jnp.concatenate(rows, axis=0)


def put_back(product_ref, order_ref, target_ref):
    total = jnp.zeros((2 * ROWS, LANES), F32)
    for group in range(ROWS // GROUP):
        start = group * GROUP
        halves_of = [part.astype(F32) for part in split(product_ref[start : start + GROUP, :])]
        hits = [row_hit(order_ref, start + part) for part in range(GROUP)]
        values = [
            jnp.concatenate(
                [
                    jnp.where(hits[part], half[part : part + 1, :], 0.0).astype(BF16)
                    for part in range(GROUP)
                ],
                axis=1,
            )
            for half in halves_of
        ]
        total = total + matmul(
            jnp.concatenate(values, axis=0), lane_hits(order_ref, group), 1, 1
        )
    target_ref[...] = total[:ROWS] + total[ROWS:]


def restrict(field, offset, member):
    total = jnp.sum(jnp.where(offset == 0, field, 0.0), axis=0, keepdims=True)
    up = jnp.sum(jnp.where(offset == 1, field, 0.0), axis=0, keepdims=True)
    down = jnp.sum(jnp.where(offset == -1, field, 0.0), axis=0, keepdims=True)
    total, up, down = (jnp.broadcast_to(x, (8, LANES)) for x in (total, up, down))
    total = total + pltpu.roll(up, AGG, 1) + pltpu.roll(down, LANES - AGG, 1)
    for distance in (1, 2, 4):
        total = total + pltpu.roll(total, LANES - distance, 1)
    lane = iota((8, LANES), 1)
    total = 0.25 * take_lanes(total, (lane % SIDE) * AGG)
    return jnp.where(lane // SIDE == member % 8, total, 0.0)


def moved(values, distance, axis, keep):
    size = values.shape[axis]
    return jnp.where(keep, pltpu.roll(values, distance % size, axis), 0.0)


def coarse_solve(source, diagonal):
    owner, lane = iota((SIDE, WIDE), 0), iota((SIDE, WIDE), 1)
    cell = lane % SIDE
    weight = OMEGA / (6.0 + diagonal)
    guess = weight * source
    for sweep in range(SWEEPS - 1):
        beside = moved(guess, 1, 0, owner > 0) + moved(guess, -1, 0, owner < SIDE - 1)
        beside = beside + moved(guess, SIDE, 1, lane >= SIDE)
        beside = beside + moved(guess, -SIDE, 1, lane < WIDE - SIDE)
        beside = beside + moved(guess, 1, 1, cell > 0) + moved(guess, -1, 1, cell < SIDE - 1)
        guess = (1.0 - OMEGA) * guess + weight * (source + beside)
    return guess


def nearby(coarse, member, rows_ref):
    rows_ref[...] = pltpu.roll(coarse, lax.rem((SIDE + 1 - member) * SIDE, WIDE), 1)[:, :LANES]


def smooth(slabs):
    total = slabs[1:9] + 0.5 * (slabs[0:8] + slabs[2:10])
    planes = []
    lane = iota((8, LANES), 1)
    row = iota((8, LANES), 0)
    for plane in range(8):
        own, ends = total[plane, :8], total[plane, 8:]
        before = jnp.where(row == 0, ends[LEFT - 8 :, :], pltpu.roll(own, 1, 0))
        after = jnp.where(row == 7, ends[:1, :], pltpu.roll(own, 7, 0))
        own = own + 0.5 * (before + after)
        below = jnp.where(lane > 0, pltpu.roll(own, 1, 1), 0.0)
        above = jnp.where(lane < LANES - 1, pltpu.roll(own, LANES - 1, 1), 0.0)
        planes.append(own + 0.5 * (below + above))
    return jnp.stack(planes)


def position():
    return lax.axis_index(COARSE), lax.axis_index(FINE)


def put_faces(field_ref, pieces_ref, rows, row, member):
    before, after = jnp.maximum(member - 1, 0), jnp.minimum(member + 1, SIDE - 1)
    pieces_ref[pl.ds(before * rows + row, 8), :] = field_ref[pl.ds(0, 8, stride=8), :]
    pieces_ref[pl.ds(after * rows + row, 8), :] = field_ref[pl.ds(7, 8, stride=8), :]


def get_faces(pieces_ref, rows, row, member, outside):
    before, after = jnp.maximum(member - 1, 0), jnp.minimum(member + 1, SIDE - 1)
    left = pieces_ref[pl.ds(before * rows + row, 8), :]
    right = pieces_ref[pl.ds(after * rows + row, 8), :]
    left = jnp.where(member > 0, left, outside)
    right = jnp.where(member < SIDE - 1, right, outside)
    return left, right


def fill_slabs(slabs_ref, field_ref, faces, pieces, outside):
    owner, member = position()
    faces_ref, face_rows, face_row = faces
    pieces_ref, rows, plane_row, halo_row = pieces
    left, right = get_faces(faces_ref, face_rows, face_row, member, outside)
    gap = jnp.full((8, LANES), outside, F32)
    for plane in range(8):
        slabs_ref[plane + 1, :8, :] = field_ref[8 * plane : 8 * plane + 8, :]
        slabs_ref[plane + 1, 8:, :] = gap
        slabs_ref[plane + 1, RIGHT : RIGHT + 1, :] = right[plane : plane + 1, :]
        slabs_ref[plane + 1, LEFT : LEFT + 1, :] = left[plane : plane + 1, :]
    for plane, there, inside in (
        (0, jnp.maximum(owner - 1, 0), owner > 0),
        (9, jnp.minimum(owner + 1, SIDE - 1), owner < SIDE - 1),
    ):
        start = there * rows
        slabs_ref[plane, 8:, :] = gap
        slabs_ref[plane, :8, :] = jnp.where(
            inside, pieces_ref[pl.ds(start + plane_row, 8), :], outside
        )
        for side, target in enumerate((LEFT, RIGHT)):
            slabs_ref[plane, target : target + 1, :] = jnp.where(
                inside, pieces_ref[pl.ds(start + halo_row + side, 1), :], outside
            )


def add_prolonged(slabs_ref, numbers_ref, rows_ref):
    owner, member = position()
    for plane in range(10):
        if plane == 0:
            there = jnp.maximum(owner - 1, 0)
        elif plane == 9:
            there = jnp.minimum(owner + 1, SIDE - 1)
        else:
            there = owner
        row = jnp.broadcast_to(rows_ref[pl.ds(there, 1), :], (8, LANES))
        for part in (0, 8):
            number = numbers_ref[plane, part : part + 8, :]
            value = take_lanes(row, jnp.maximum(number, 0))
            slabs_ref[plane, part : part + 8, :] += jnp.where(number >= 0, value, 0.0)


def operate(field, kappa):
    own, own_kappa = field[1:9, :8], kappa[1:9, :8]
    return own_kappa * (8.0 * own - smooth(field)) + own * smooth(kappa) - smooth(
        kappa * field
    )


def offsets(aggregate):
    return aggregate - iota((ROWS, LANES), 1) // AGG


F_FIELD, F_KAPPA, F_MAP, F_SOURCE, F_FIRST = 0, 8, 16, 24, 25
C_FIELD, C_KAPPA, C_MAP, C_HALOS, C_SOURCE, C_DIAGONAL, C_FIRST = 0, 8, 16, 24, 30, 32, 34
F_SOURCE_2, F_SECOND = 8, 9
C_HALO_2, C_SOURCE_2, C_SECOND = 8, 10, 12


def begin(
    table_hbm, side_hbm, index_hbm, order_hbm, matrices_hbm, map_hbm, diagonal_hbm,
    pieces_ref, kappa_ref, smoothed_ref, numbers_ref,
    table_ref, side_ref, index_ref, order_ref, map_ref, diagonal_ref, picked_ref, product_ref,
    matrices_ref, arrived,
):
    owner, member = position()
    copies = [
        pltpu.make_async_copy(source, target, arrived.at[number])
        for number, (source, target) in enumerate(
            (
                (order_hbm, order_ref),
                (side_hbm, side_ref),
                (table_hbm, table_ref),
                (index_hbm, index_ref),
                (map_hbm, map_ref),
                (diagonal_hbm, diagonal_ref),
            )
        )
    ]
    copies += [
        pltpu.make_async_copy(
            matrices_hbm.at[pl.ds(start, GROUP)],
            matrices_ref.at[pl.ds(start, GROUP)],
            arrived.at[6 + start // GROUP],
        )
        for start in range(0, ROWS, GROUP)
    ]
    for copy in copies:
        copy.start()
    copies[0].wait()
    for copy in copies[1:6]:
        copy.wait()
    index = index_ref[...]
    kappa = jnp.zeros((ROWS, LANES), F32)
    for entry in range(table_ref.shape[0]):
        kappa = jnp.where(index == entry, table_ref[entry], kappa)
    kappa_ref[...] = kappa
    pick(side_ref, order_ref, picked_ref)
    multiply_blocks(matrices_ref, picked_ref, product_ref, copies[6:])
    put_back(product_ref, order_ref, smoothed_ref)
    aggregate = map_ref[...]
    numbers_ref[...] = aggregate.astype(F32)
    source = restrict(side_ref[...], offsets(aggregate), member)
    spread = jnp.broadcast_to(jnp.concatenate([diagonal_ref[...]] * 8, axis=1), (8, LANES))
    beside = iota((8, LANES), 1) // SIDE == (member + 1) % 8
    put_all(jnp.where(beside, spread, source), pieces_ref, F_FIRST, F_SOURCE)
    put_faces(smoothed_ref, pieces_ref, F_FIRST, F_FIELD, member)
    put_faces(kappa_ref, pieces_ref, F_FIRST, F_KAPPA, member)
    put_faces(numbers_ref, pieces_ref, F_FIRST, F_MAP, member)


def put_all(values, pieces_ref, rows, row):
    for piece in range(SIDE):
        pieces_ref[piece * rows + row : piece * rows + row + 1, :] = values[0:1, :]


def put_planes(field_ref, faces, pieces, outside):
    owner, member = position()
    left, right = get_faces(*faces, member, outside)
    pieces_ref, rows, plane_row, halo_row = pieces
    for there, plane in (
        (jnp.maximum(owner - 1, 0), 0),
        (jnp.minimum(owner + 1, SIDE - 1), 7),
    ):
        start = there * rows
        pieces_ref[pl.ds(start + plane_row, 8), :] = field_ref[8 * plane : 8 * plane + 8, :]
        for side, halo in enumerate((left, right)):
            pieces_ref[pl.ds(start + halo_row + side, 1), :] = halo[plane : plane + 1, :]


def gathered(rows, step):
    here = iota((SIDE, LANES), 0) % 8
    rows = jnp.where(iota((SIDE, LANES), 1) // SIDE == (here + step) % 8, rows, 0.0)
    parts = [jnp.sum(rows[at : at + 8], axis=0, keepdims=True) for at in (0, 8)]
    if step:
        parts = [
            pltpu.roll(jnp.broadcast_to(part, (8, LANES)), LANES - SIDE * step, 1)
            for part in parts
        ]
    return parts


def first_parts(faces_ref, pieces_ref):
    return (
        ((faces_ref, F_FIRST, F_FIELD), (pieces_ref, C_FIRST, C_FIELD, C_HALOS), 0.0),
        ((faces_ref, F_FIRST, F_KAPPA), (pieces_ref, C_FIRST, C_KAPPA, C_HALOS + 2), 0.0),
        ((faces_ref, F_FIRST, F_MAP), (pieces_ref, C_FIRST, C_MAP, C_HALOS + 4), -1.0),
    )


def second_parts(faces_ref, pieces_ref):
    return (faces_ref, F_SECOND, 0), (pieces_ref, C_SECOND, 0, C_HALO_2), 0.0


def relay_first(faces_ref, smoothed_ref, kappa_ref, numbers_ref, pieces_ref):
    rows = faces_ref[pl.ds(F_SOURCE, SIDE, stride=F_FIRST), :]
    for half in range(2):
        put_all(gathered(rows, 0)[half], pieces_ref, C_FIRST, C_SOURCE + half)
        put_all(gathered(rows, 1)[half], pieces_ref, C_FIRST, C_DIAGONAL + half)
    parts = first_parts(faces_ref, pieces_ref)
    for field_ref, part in zip((smoothed_ref, kappa_ref, numbers_ref), parts):
        put_planes(field_ref, *part)


def halves(pieces_ref, rows, row):
    return jnp.concatenate(
        [pieces_ref[pl.ds(row + half, SIDE, stride=rows), :] for half in range(2)], axis=1
    )


def first_image(
    faces_ref, ends_ref, own_ref, own_kappa_ref, numbers_ref, map_ref, order_ref,
    matrices_hbm,
    pieces_ref, field_ref, image_ref, smoothed_ref, kappa_ref, lanes_ref, diagonal_ref,
    picked_ref, product_ref, slabs_ref, rows_ref, matrices_ref, arrived,
):
    owner, member = position()
    copy = pltpu.make_async_copy(matrices_hbm, matrices_ref, arrived)
    copy.start()
    diagonal = halves(ends_ref, C_FIRST, C_DIAGONAL)
    diagonal_ref[...] = diagonal
    nearby(coarse_solve(halves(ends_ref, C_FIRST, C_SOURCE), diagonal), member, rows_ref)
    parts = first_parts(faces_ref, ends_ref)
    fill_slabs(slabs_ref, numbers_ref, *parts[2])
    row = iota((10, SLAB, LANES), 1)
    shift = jnp.where(row < 8, SIDE, jnp.where(row == RIGHT, 2 * SIDE, 0))
    number = slabs_ref[...]
    lanes_ref[...] = jnp.where(number >= 0.0, number.astype(jnp.int32) + shift, -1)
    fill_slabs(kappa_ref, own_kappa_ref, *parts[1])
    fill_slabs(slabs_ref, own_ref, *parts[0])
    add_prolonged(slabs_ref, lanes_ref, rows_ref)
    field = slabs_ref[...]
    field_ref[...] = field[1:9, :8].reshape(ROWS, LANES)
    image_ref[...] = operate(field, kappa_ref[...]).reshape(ROWS, LANES)
    pick(image_ref, order_ref, picked_ref)
    copy.wait()
    multiply_blocks(matrices_ref, picked_ref, product_ref)
    put_back(product_ref, order_ref, smoothed_ref)
    source = restrict(image_ref[...], offsets(map_ref[...]), member)
    put_all(source, pieces_ref, F_SECOND, F_SOURCE_2)
    put_faces(smoothed_ref, pieces_ref, F_SECOND, 0, member)


def relay_second(faces_ref, smoothed_ref, pieces_ref):
    rows = faces_ref[pl.ds(F_SOURCE_2, SIDE, stride=F_SECOND), :]
    for half, values in enumerate(gathered(rows, 0)):
        put_all(values, pieces_ref, C_SECOND, C_SOURCE_2 + half)
    put_planes(smoothed_ref, *second_parts(faces_ref, pieces_ref))


def second_image(
    faces_ref, ends_ref, own_ref, kappa_ref, lanes_ref, map_ref, order_ref,
    diagonal_ref, side_ref, first_ref, image_ref, matrices_hbm,
    pieces_ref, field_ref, second_ref, product_ref,
    picked_ref, slabs_ref, rows_ref, matrices_ref, arrived,
):
    owner, member = position()
    copy = pltpu.make_async_copy(matrices_hbm, matrices_ref, arrived)
    copy.start()
    nearby(coarse_solve(halves(ends_ref, C_SECOND, C_SOURCE_2), diagonal_ref[...]), member, rows_ref)
    fill_slabs(slabs_ref, own_ref, *second_parts(faces_ref, ends_ref))
    add_prolonged(slabs_ref, lanes_ref, rows_ref)
    slabs = slabs_ref[...]
    field = slabs[1:9, :8].reshape(ROWS, LANES)
    field_ref[...] = field
    second = operate(slabs, kappa_ref[...]).reshape(ROWS, LANES)
    second_ref[...] = second
    pick(second_ref, order_ref, picked_ref)
    copy.wait()
    multiply_blocks(matrices_ref, picked_ref, product_ref)
    first = first_ref[...]
    image = image_ref[...]
    pairs = (
        side_ref[...] * first,
        first * image,
        image * field,
        second * first,
        second * field,
        picked_ref[...] * product_ref[...],
    )
    lane = iota((8, LANES), 1)
    message = restrict(second, offsets(map_ref[...]), member)
    beside = lax.rem(member + 1, 8) * SIDE
    for number, pair in enumerate(pairs):
        total = jnp.sum(jnp.sum(pair, axis=0, keepdims=True), axis=1, keepdims=True)
        message = jnp.where(lane == beside + number, total, message)
    for start in range(0, WIDE, 8):
        pieces_ref[start : start + 8, :] = message


def finish(
    pieces_ref, diagonal_ref, map_ref, side_ref, first_ref, image_ref, field_ref, second_ref,
    smoothed_ref,
    solution_ref, residual_ref, search_ref,
):
    owner, member = position()
    pieces = pieces_ref[...].reshape(SIDE, SIDE, LANES)
    place = iota((SIDE, LANES), 0) % 8
    group = iota((SIDE, LANES), 1) // SIDE
    pieces_sum = jnp.sum(pieces, axis=0)
    sums = jnp.where(group == (place + 1) % 8, pieces_sum, 0.0)
    kept = jnp.where((group == place)[None], pieces, 0.0)
    source = jnp.concatenate(
        [jnp.sum(kept[:, :8], axis=1), jnp.sum(kept[:, 8:], axis=1)], axis=1
    )
    coarse = coarse_solve(source, diagonal_ref[...])
    lane = iota((1, LANES), 1)
    sums = jnp.sum(sums, axis=0, keepdims=True)

    def total(number):
        picked = jnp.where(lane % SIDE == number, sums, 0.0)
        return jnp.sum(picked, axis=1, keepdims=True)

    def whole(array):
        return jnp.sum(jnp.sum(array, axis=0, keepdims=True), axis=1, keepdims=True)

    r_z, z_az, w_y, v_z, v_y, v_bv = (total(number) for number in range(6))
    v_u = v_bv + 4.0 * whole(source * coarse)
    alpha = r_z / z_az
    following = r_z - 2.0 * alpha * z_az + alpha * alpha * w_y
    grown = 1.0 + following / r_z
    product = grown * grown * z_az - grown * alpha * (v_z + w_y) + alpha * alpha * v_y
    again = following / product
    one = alpha + again * grown
    two = again * alpha
    last = (
        r_z - 2.0 * one * z_az + 2.0 * two * v_z + one * one * w_y
        - 2.0 * one * two * v_y + two * two * v_u
    )
    ratio = last / following
    lanes = iota((SIDE, WIDE), 1)
    rows = iota((SIDE, WIDE), 0)
    near = pltpu.roll(coarse, lax.rem((SIDE - member) * SIDE, WIDE), 1)[:, :LANES]
    row = jnp.sum(
        jnp.where(iota((SIDE, LANES), 0) == owner, near, 0.0), axis=0, keepdims=True
    )
    row = jnp.broadcast_to(row, (8, LANES))
    for g in range(8):
        at = slice(8 * g, 8 * g + 8)
        first, image, field, second = (
            ref[at, :] for ref in (first_ref, image_ref, field_ref, second_ref)
        )
        smoothed = smoothed_ref[at, :] + take_lanes(row, map_ref[at, :])
        solution_ref[at, :] = one * first - two * field
        residual_ref[at, :] = side_ref[at, :] - one * image + two * second
        search_ref[at, :] = (
            first - one * field + two * smoothed + ratio * (grown * first - alpha * field)
        )


def shards(
    right_side, coefficient_index, material_coefficients, block_cells, block_inverses,
    aggregate_map, coarse_diagonal,
):
    dims = right_side.shape
    side = right_side.reshape(ROWS, LANES)
    index = coefficient_index.reshape(ROWS, LANES)
    order = block_cells.reshape(ROWS, LANES)
    matrices = block_inverses.reshape(ROWS, LANES, LANES)
    aggregate = aggregate_map.reshape(ROWS, LANES)
    diagonal = coarse_diagonal.reshape(1, SIDE)
    local = shape(ROWS, LANES)
    cells = pltpu.VMEM((ROWS, LANES), F32)
    int_cells = pltpu.VMEM((ROWS, LANES), jnp.int32)
    held = pltpu.VMEM(matrices.shape, F32)
    scratch = [
        cells, cells, pltpu.VMEM((10, SLAB, LANES), F32), pltpu.VMEM((SIDE, LANES), F32),
        held, pltpu.SemaphoreType.DMA,
    ]

    def call(kernel, outs, ins, scratch=(), specs=None):
        return pl.pallas_call(
            kernel,
            out_shape=outs,
            in_specs=specs or [vmem()] * ins,
            out_specs=[vmem()] * len(outs),
            scratch_shapes=list(scratch),
            compiler_params=params(),
            cost_estimate=pl.CostEstimate(
                flops=10**9, bytes_accessed=4 * 10**6, transcendentals=0
            ),
        )

    def exchange(pieces, axis):
        rows = pieces.shape
        pieces = lax.all_to_all(pieces.reshape(rows[0], 1, LANES), axis, 0, 0, tiled=True)
        return pieces.reshape(rows)

    fixed = [
        pltpu.with_memory_space_constraint(array, pltpu.HBM)
        for array in (material_coefficients, side, index, order, matrices, aggregate, diagonal)
    ]
    pieces, kappa, smoothed, numbers = call(
        begin,
        [
            shape(SIDE * F_FIRST, LANES), local, local, local,
        ],
        7,
        [
            pltpu.SMEM(material_coefficients.shape, F32), cells, int_cells, int_cells,
            int_cells, pltpu.VMEM((1, SIDE), F32), cells, cells,
            held, pltpu.SemaphoreType.DMA((6 + ROWS // GROUP,)),
        ],
        [hbm()] * 7,
    )(*fixed)
    faces = exchange(pieces, FINE)
    (pieces,) = call(relay_first, [shape(SIDE * C_FIRST, LANES)], 4)(
        faces, smoothed, kappa, numbers
    )
    ends = exchange(pieces, COARSE)
    pieces, first, image, smoothed, kappa, lanes, diagonals = call(
        first_image,
        [
            shape(SIDE * F_SECOND, LANES), local, local, local, shape(10, SLAB, LANES),
            shape(10, SLAB, LANES, dtype=jnp.int32), shape(SIDE, WIDE),
        ],
        11,
        scratch,
        [vmem()] * 7 + [hbm()],
    )(
        faces, ends, smoothed, kappa, numbers, aggregate, order, fixed[4],
    )
    faces = exchange(pieces, FINE)
    (pieces,) = call(relay_second, [shape(SIDE * C_SECOND, LANES)], 2)(faces, smoothed)
    ends = exchange(pieces, COARSE)
    pieces, field, second, product = call(
        second_image,
        [shape(WIDE, LANES), local, local, local],
        13,
        scratch[:1] + scratch[2:],
        [vmem()] * 11 + [hbm()],
    )(
        faces, ends, smoothed, kappa, lanes, aggregate, order, diagonals, side, first,
        image, fixed[4],
    )
    pieces = exchange(pieces, (COARSE, FINE))
    (smoothed,) = call(put_back, [local], 2)(product, order)
    results = call(finish, [local, local, local], 9)(
        pieces, diagonals, aggregate, side, first, image, field, second, smoothed
    )
    return tuple(result.reshape(dims) for result in results)


def solution(mesh):
    cells = P(COARSE, FINE, None)
    in_specs = (
        cells,
        cells,
        P(),
        P(COARSE, FINE, None, None),
        P(COARSE, FINE, None, None, None),
        cells,
        cells,
    )
    return jax.shard_map(
        shards, mesh=mesh, in_specs=in_specs, out_specs=(cells,) * 3, check_vma=False
    )
```

```python
import functools

import jax
import jax.numpy as jnp
from jax import lax
from jax.experimental import pallas as pl
from jax.experimental.pallas import tpu as pltpu
from jax.sharding import PartitionSpec as P

AGG = 8
COARSE, FINE = "coarse", "fine"
SWEEPS = 4
OMEGA = 0.8
SIDE = 16
ROWS = 64
LANES = 128
WIDE = SIDE * SIDE
F32, BF16 = jnp.float32, jnp.bfloat16
GROUP = 8

SLAB = 16
RIGHT, LEFT = 8, 15


def vmem():
    return pl.BlockSpec(memory_space=pltpu.VMEM)


def smem():
    return pl.BlockSpec(memory_space=pltpu.SMEM)


def hbm():
    return pl.BlockSpec(memory_space=pltpu.HBM)


def params():
    return pltpu.CompilerParams(vmem_limit_bytes=24 * 1024 * 1024)


def shape(*dims, dtype=F32):
    return jax.ShapeDtypeStruct(dims, dtype)


def iota(dims, axis):
    return lax.broadcasted_iota(jnp.int32, dims, axis)


def take_lanes(values, lanes):
    numbers = lax.GatherDimensionNumbers(
        offset_dims=(),
        collapsed_slice_dims=(1,),
        start_index_map=(1,),
        operand_batching_dims=(0,),
        start_indices_batching_dims=(0,),
    )
    return lax.gather(
        values,
        lanes[..., None],
        numbers,
        slice_sizes=(1, 1),
        mode=lax.GatherScatterMode.PROMISE_IN_BOUNDS,
    )


def split(values):
    high = values.astype(BF16)
    return high, (values - high.astype(F32)).astype(BF16)


def matmul(left, right, left_dim, right_dim):
    dims = (((left_dim,), (right_dim,)), ((), ()))
    return lax.dot_general(left, right, dims, preferred_element_type=F32)


def lane_hits(order_ref, group):
    lane = iota((LANES, LANES), 0)
    return jnp.concatenate(
        [
            jnp.where(lane == order_ref[b : b + 1, :] % LANES, 1.0, 0.0).astype(BF16)
            for b in range(group * GROUP, group * GROUP + GROUP)
        ],
        axis=1,
    )


def row_hit(order_ref, block):
    return iota((ROWS, LANES), 0) == order_ref[block : block + 1, :] // LANES


def column_sum(values):
    total = jnp.sum(values.reshape(-1, 8, LANES), axis=0)
    return jnp.sum(total, axis=0, keepdims=True)


def pick(source_ref, order_ref, picked_ref):
    source = jnp.concatenate(split(source_ref[...]), axis=0)
    for group in range(ROWS // GROUP):
        start = group * GROUP
        found = matmul(source, lane_hits(order_ref, group), 1, 0)
        found = found[:ROWS] + found[ROWS:]
        rows = []
        for part in range(GROUP):
            column = found[:, LANES * part : LANES * (part + 1)]
            rows.append(column_sum(jnp.where(row_hit(order_ref, start + part), column, 0.0)))
        picked_ref[start : start + GROUP, :] = jnp.concatenate(rows, axis=0)


def multiply_blocks(matrices_ref, picked_ref, product_ref):
    wide = (2 * GROUP, GROUP * LANES)
    spread = jnp.where(iota(wide, 0) % GROUP == iota(wide, 1) // LANES, 1.0, 0.0).astype(BF16)
    for start in range(0, ROWS, GROUP):
        high, low = split(picked_ref[start : start + GROUP, :])
        both = jnp.concatenate([high.astype(F32), low.astype(F32)], axis=0)
        columns = matmul(jnp.transpose(both).astype(BF16), spread, 1, 0)
        rows = [
            column_sum(
                matrices_ref[start + part] * columns[:, LANES * part : LANES * (part + 1)]
            )
            for part in range(GROUP)
        ]
        product_ref[start : start + GROUP, :] = jnp.concatenate(rows, axis=0)


def put_back(product_ref, order_ref, target_ref):
    total = jnp.zeros((2 * ROWS, LANES), F32)
    for group in range(ROWS // GROUP):
        start = group * GROUP
        halves_of = [part.astype(F32) for part in split(product_ref[start : start + GROUP, :])]
        hits = [row_hit(order_ref, start + part) for part in range(GROUP)]
        values = [
            jnp.concatenate(
                [
                    jnp.where(hits[part], half[part : part + 1, :], 0.0).astype(BF16)
                    for part in range(GROUP)
                ],
                axis=1,
            )
            for half in halves_of
        ]
        total = total + matmul(
            jnp.concatenate(values, axis=0), lane_hits(order_ref, group), 1, 1
        )
    target_ref[...] = total[:ROWS] + total[ROWS:]


def restrict(field, offset, member):
    total = jnp.sum(jnp.where(offset == 0, field, 0.0), axis=0, keepdims=True)
    up = jnp.sum(jnp.where(offset == 1, field, 0.0), axis=0, keepdims=True)
    down = jnp.sum(jnp.where(offset == -1, field, 0.0), axis=0, keepdims=True)
    total, up, down = (jnp.broadcast_to(x, (8, LANES)) for x in (total, up, down))
    total = total + pltpu.roll(up, AGG, 1) + pltpu.roll(down, LANES - AGG, 1)
    for distance in (1, 2, 4):
        total = total + pltpu.roll(total, LANES - distance, 1)
    lane = iota((8, LANES), 1)
    total = 0.25 * take_lanes(total, (lane % SIDE) * AGG)
    return jnp.where(lane // SIDE == member % 8, total, 0.0)


def moved(values, distance, axis, keep):
    size = values.shape[axis]
    return jnp.where(keep, pltpu.roll(values, distance % size, axis), 0.0)


def coarse_solve(source, diagonal):
    owner, lane = iota((SIDE, WIDE), 0), iota((SIDE, WIDE), 1)
    cell = lane % SIDE
    weight = OMEGA / (6.0 + diagonal)
    guess = weight * source
    for sweep in range(SWEEPS - 1):
        beside = moved(guess, 1, 0, owner > 0) + moved(guess, -1, 0, owner < SIDE - 1)
        beside = beside + moved(guess, SIDE, 1, lane >= SIDE)
        beside = beside + moved(guess, -SIDE, 1, lane < WIDE - SIDE)
        beside = beside + moved(guess, 1, 1, cell > 0) + moved(guess, -1, 1, cell < SIDE - 1)
        guess = (1.0 - OMEGA) * guess + weight * (source + beside)
    return guess


def nearby(coarse, member, rows_ref):
    rows_ref[...] = pltpu.roll(coarse, lax.rem((SIDE + 1 - member) * SIDE, WIDE), 1)[:, :LANES]


def smooth(slabs):
    total = slabs[1:9] + 0.5 * (slabs[0:8] + slabs[2:10])
    planes = []
    lane = iota((8, LANES), 1)
    row = iota((8, LANES), 0)
    for plane in range(8):
        own, ends = total[plane, :8], total[plane, 8:]
        before = jnp.where(row == 0, ends[LEFT - 8 :, :], pltpu.roll(own, 1, 0))
        after = jnp.where(row == 7, ends[:1, :], pltpu.roll(own, 7, 0))
        own = own + 0.5 * (before + after)
        below = jnp.where(lane > 0, pltpu.roll(own, 1, 1), 0.0)
        above = jnp.where(lane < LANES - 1, pltpu.roll(own, LANES - 1, 1), 0.0)
        planes.append(own + 0.5 * (below + above))
    return jnp.stack(planes)


def position():
    return lax.axis_index(COARSE), lax.axis_index(FINE)


def put_faces(field_ref, pieces_ref, rows, row, member):
    before, after = jnp.maximum(member - 1, 0), jnp.minimum(member + 1, SIDE - 1)
    pieces_ref[pl.ds(before * rows + row, 8), :] = field_ref[pl.ds(0, 8, stride=8), :]
    pieces_ref[pl.ds(after * rows + row, 8), :] = field_ref[pl.ds(7, 8, stride=8), :]


def get_faces(pieces_ref, rows, row, member, outside):
    before, after = jnp.maximum(member - 1, 0), jnp.minimum(member + 1, SIDE - 1)
    left = pieces_ref[pl.ds(before * rows + row, 8), :]
    right = pieces_ref[pl.ds(after * rows + row, 8), :]
    left = jnp.where(member > 0, left, outside)
    right = jnp.where(member < SIDE - 1, right, outside)
    return left, right


def fill_slabs(slabs_ref, field_ref, faces, pieces, outside):
    owner, member = position()
    faces_ref, face_rows, face_row = faces
    pieces_ref, rows, plane_row, halo_row = pieces
    left, right = get_faces(faces_ref, face_rows, face_row, member, outside)
    gap = jnp.full((8, LANES), outside, F32)
    for plane in range(8):
        slabs_ref[plane + 1, :8, :] = field_ref[8 * plane : 8 * plane + 8, :]
        slabs_ref[plane + 1, 8:, :] = gap
        slabs_ref[plane + 1, RIGHT : RIGHT + 1, :] = right[plane : plane + 1, :]
        slabs_ref[plane + 1, LEFT : LEFT + 1, :] = left[plane : plane + 1, :]
    for plane, there, inside in (
        (0, jnp.maximum(owner - 1, 0), owner > 0),
        (9, jnp.minimum(owner + 1, SIDE - 1), owner < SIDE - 1),
    ):
        start = there * rows
        slabs_ref[plane, 8:, :] = gap
        slabs_ref[plane, :8, :] = jnp.where(
            inside, pieces_ref[pl.ds(start + plane_row, 8), :], outside
        )
        for side, target in enumerate((LEFT, RIGHT)):
            slabs_ref[plane, target : target + 1, :] = jnp.where(
                inside, pieces_ref[pl.ds(start + halo_row + side, 1), :], outside
            )


def add_prolonged(slabs_ref, numbers_ref, rows_ref):
    owner, member = position()
    for plane in range(10):
        if plane == 0:
            there = jnp.maximum(owner - 1, 0)
        elif plane == 9:
            there = jnp.minimum(owner + 1, SIDE - 1)
        else:
            there = owner
        row = jnp.broadcast_to(rows_ref[pl.ds(there, 1), :], (8, LANES))
        for part in (0, 8):
            number = numbers_ref[plane, part : part + 8, :]
            value = take_lanes(row, jnp.maximum(number, 0))
            slabs_ref[plane, part : part + 8, :] += jnp.where(number >= 0, value, 0.0)


def operate(field, kappa):
    own, own_kappa = field[1:9, :8], kappa[1:9, :8]
    return own_kappa * (8.0 * own - smooth(field)) + own * smooth(kappa) - smooth(
        kappa * field
    )


def offsets(aggregate):
    return aggregate - iota((ROWS, LANES), 1) // AGG


F_FIELD, F_KAPPA, F_MAP, F_SOURCE, F_FIRST = 0, 8, 16, 24, 25
C_FIELD, C_KAPPA, C_MAP, C_HALOS, C_SOURCE, C_DIAGONAL, C_FIRST = 0, 8, 16, 24, 30, 32, 34
F_SOURCE_2, F_SECOND = 8, 9
C_HALO_2, C_SOURCE_2, C_SECOND = 8, 10, 12


def begin(
    table_hbm, side_hbm, index_hbm, order_hbm, matrices_hbm, map_hbm, diagonal_hbm,
    pieces_ref, kappa_ref, smoothed_ref, numbers_ref,
    table_ref, side_ref, index_ref, order_ref, map_ref, diagonal_ref, picked_ref, product_ref,
    matrices_ref, arrived,
):
    owner, member = position()
    copies = [
        pltpu.make_async_copy(source, target, arrived.at[number])
        for number, (source, target) in enumerate(
            (
                (order_hbm, order_ref),
                (side_hbm, side_ref),
                (table_hbm, table_ref),
                (index_hbm, index_ref),
                (map_hbm, map_ref),
                (diagonal_hbm, diagonal_ref),
                (matrices_hbm, matrices_ref),
            )
        )
    ]
    for copy in copies:
        copy.start()
    copies[0].wait()
    for copy in copies[1:-1]:
        copy.wait()
    index = index_ref[...]
    kappa = jnp.zeros((ROWS, LANES), F32)
    for entry in range(table_ref.shape[0]):
        kappa = jnp.where(index == entry, table_ref[entry], kappa)
    kappa_ref[...] = kappa
    pick(side_ref, order_ref, picked_ref)
    copies[-1].wait()
    multiply_blocks(matrices_ref, picked_ref, product_ref)
    put_back(product_ref, order_ref, smoothed_ref)
    aggregate = map_ref[...]
    numbers_ref[...] = aggregate.astype(F32)
    source = restrict(side_ref[...], offsets(aggregate), member)
    spread = jnp.broadcast_to(jnp.concatenate([diagonal_ref[...]] * 8, axis=1), (8, LANES))
    beside = iota((8, LANES), 1) // SIDE == (member + 1) % 8
    put_all(jnp.where(beside, spread, source), pieces_ref, F_FIRST, F_SOURCE)
    put_faces(smoothed_ref, pieces_ref, F_FIRST, F_FIELD, member)
    put_faces(kappa_ref, pieces_ref, F_FIRST, F_KAPPA, member)
    put_faces(numbers_ref, pieces_ref, F_FIRST, F_MAP, member)


def put_all(values, pieces_ref, rows, row):
    for piece in range(SIDE):
        pieces_ref[piece * rows + row : piece * rows + row + 1, :] = values[0:1, :]


def put_planes(field_ref, faces, pieces, outside):
    owner, member = position()
    left, right = get_faces(*faces, member, outside)
    pieces_ref, rows, plane_row, halo_row = pieces
    for there, plane in (
        (jnp.maximum(owner - 1, 0), 0),
        (jnp.minimum(owner + 1, SIDE - 1), 7),
    ):
        start = there * rows
        pieces_ref[pl.ds(start + plane_row, 8), :] = field_ref[8 * plane : 8 * plane + 8, :]
        for side, halo in enumerate((left, right)):
            pieces_ref[pl.ds(start + halo_row + side, 1), :] = halo[plane : plane + 1, :]


def gathered(rows, step):
    here = iota((SIDE, LANES), 0) % 8
    rows = jnp.where(iota((SIDE, LANES), 1) // SIDE == (here + step) % 8, rows, 0.0)
    parts = [jnp.sum(rows[at : at + 8], axis=0, keepdims=True) for at in (0, 8)]
    if step:
        parts = [
            pltpu.roll(jnp.broadcast_to(part, (8, LANES)), LANES - SIDE * step, 1)
            for part in parts
        ]
    return parts


def first_parts(faces_ref, pieces_ref):
    return (
        ((faces_ref, F_FIRST, F_FIELD), (pieces_ref, C_FIRST, C_FIELD, C_HALOS), 0.0),
        ((faces_ref, F_FIRST, F_KAPPA), (pieces_ref, C_FIRST, C_KAPPA, C_HALOS + 2), 0.0),
        ((faces_ref, F_FIRST, F_MAP), (pieces_ref, C_FIRST, C_MAP, C_HALOS + 4), -1.0),
    )


def second_parts(faces_ref, pieces_ref):
    return (faces_ref, F_SECOND, 0), (pieces_ref, C_SECOND, 0, C_HALO_2), 0.0


def relay_first(faces_ref, smoothed_ref, kappa_ref, numbers_ref, pieces_ref):
    rows = faces_ref[pl.ds(F_SOURCE, SIDE, stride=F_FIRST), :]
    for half in range(2):
        put_all(gathered(rows, 0)[half], pieces_ref, C_FIRST, C_SOURCE + half)
        put_all(gathered(rows, 1)[half], pieces_ref, C_FIRST, C_DIAGONAL + half)
    parts = first_parts(faces_ref, pieces_ref)
    for field_ref, part in zip((smoothed_ref, kappa_ref, numbers_ref), parts):
        put_planes(field_ref, *part)


def halves(pieces_ref, rows, row):
    return jnp.concatenate(
        [pieces_ref[pl.ds(row + half, SIDE, stride=rows), :] for half in range(2)], axis=1
    )


def first_image(
    faces_ref, ends_ref, own_ref, own_kappa_ref, numbers_ref, map_ref, order_ref,
    matrices_hbm,
    pieces_ref, field_ref, image_ref, smoothed_ref, kappa_ref, lanes_ref, diagonal_ref,
    picked_ref, product_ref, slabs_ref, rows_ref, matrices_ref, arrived,
):
    owner, member = position()
    copy = pltpu.make_async_copy(matrices_hbm, matrices_ref, arrived)
    copy.start()
    diagonal = halves(ends_ref, C_FIRST, C_DIAGONAL)
    diagonal_ref[...] = diagonal
    nearby(coarse_solve(halves(ends_ref, C_FIRST, C_SOURCE), diagonal), member, rows_ref)
    parts = first_parts(faces_ref, ends_ref)
    fill_slabs(slabs_ref, numbers_ref, *parts[2])
    row = iota((10, SLAB, LANES), 1)
    shift = jnp.where(row < 8, SIDE, jnp.where(row == RIGHT, 2 * SIDE, 0))
    number = slabs_ref[...]
    lanes_ref[...] = jnp.where(number >= 0.0, number.astype(jnp.int32) + shift, -1)
    fill_slabs(kappa_ref, own_kappa_ref, *parts[1])
    fill_slabs(slabs_ref, own_ref, *parts[0])
    add_prolonged(slabs_ref, lanes_ref, rows_ref)
    field = slabs_ref[...]
    field_ref[...] = field[1:9, :8].reshape(ROWS, LANES)
    image_ref[...] = operate(field, kappa_ref[...]).reshape(ROWS, LANES)
    copy.wait()
    pick(image_ref, order_ref, picked_ref)
    multiply_blocks(matrices_ref, picked_ref, product_ref)
    put_back(product_ref, order_ref, smoothed_ref)
    source = restrict(image_ref[...], offsets(map_ref[...]), member)
    put_all(source, pieces_ref, F_SECOND, F_SOURCE_2)
    put_faces(smoothed_ref, pieces_ref, F_SECOND, 0, member)


def relay_second(faces_ref, smoothed_ref, pieces_ref):
    rows = faces_ref[pl.ds(F_SOURCE_2, SIDE, stride=F_SECOND), :]
    for half, values in enumerate(gathered(rows, 0)):
        put_all(values, pieces_ref, C_SECOND, C_SOURCE_2 + half)
    put_planes(smoothed_ref, *second_parts(faces_ref, pieces_ref))


def second_image(
    faces_ref, ends_ref, own_ref, kappa_ref, lanes_ref, map_ref, order_ref,
    diagonal_ref, side_ref, first_ref, image_ref, matrices_hbm,
    pieces_ref, field_ref, second_ref, product_ref,
    picked_ref, slabs_ref, rows_ref, matrices_ref, arrived,
):
    owner, member = position()
    copy = pltpu.make_async_copy(matrices_hbm, matrices_ref, arrived)
    copy.start()
    nearby(coarse_solve(halves(ends_ref, C_SECOND, C_SOURCE_2), diagonal_ref[...]), member, rows_ref)
    fill_slabs(slabs_ref, own_ref, *second_parts(faces_ref, ends_ref))
    add_prolonged(slabs_ref, lanes_ref, rows_ref)
    slabs = slabs_ref[...]
    field = slabs[1:9, :8].reshape(ROWS, LANES)
    field_ref[...] = field
    second = operate(slabs, kappa_ref[...]).reshape(ROWS, LANES)
    second_ref[...] = second
    copy.wait()
    pick(second_ref, order_ref, picked_ref)
    multiply_blocks(matrices_ref, picked_ref, product_ref)
    first = first_ref[...]
    image = image_ref[...]
    pairs = (
        side_ref[...] * first,
        first * image,
        image * field,
        second * first,
        second * field,
        picked_ref[...] * product_ref[...],
    )
    lane = iota((8, LANES), 1)
    message = restrict(second, offsets(map_ref[...]), member)
    beside = lax.rem(member + 1, 8) * SIDE
    for number, pair in enumerate(pairs):
        total = jnp.sum(jnp.sum(pair, axis=0, keepdims=True), axis=1, keepdims=True)
        message = jnp.where(lane == beside + number, total, message)
    for start in range(0, WIDE, 8):
        pieces_ref[start : start + 8, :] = message


def finish(
    pieces_ref, diagonal_ref, map_ref, side_ref, first_ref, image_ref, field_ref, second_ref,
    smoothed_ref,
    solution_ref, residual_ref, search_ref,
):
    owner, member = position()
    pieces = pieces_ref[...].reshape(SIDE, SIDE, LANES)
    place = iota((SIDE, LANES), 0) % 8
    group = iota((SIDE, LANES), 1) // SIDE
    pieces_sum = jnp.sum(pieces, axis=0)
    sums = jnp.where(group == (place + 1) % 8, pieces_sum, 0.0)
    kept = jnp.where((group == place)[None], pieces, 0.0)
    source = jnp.concatenate(
        [jnp.sum(kept[:, :8], axis=1), jnp.sum(kept[:, 8:], axis=1)], axis=1
    )
    coarse = coarse_solve(source, diagonal_ref[...])
    lane = iota((1, LANES), 1)
    sums = jnp.sum(sums, axis=0, keepdims=True)

    def total(number):
        picked = jnp.where(lane % SIDE == number, sums, 0.0)
        return jnp.sum(picked, axis=1, keepdims=True)

    def whole(array):
        return jnp.sum(jnp.sum(array, axis=0, keepdims=True), axis=1, keepdims=True)

    r_z, z_az, w_y, v_z, v_y, v_bv = (total(number) for number in range(6))
    v_u = v_bv + 4.0 * whole(source * coarse)
    alpha = r_z / z_az
    following = r_z - 2.0 * alpha * z_az + alpha * alpha * w_y
    grown = 1.0 + following / r_z
    product = grown * grown * z_az - grown * alpha * (v_z + w_y) + alpha * alpha * v_y
    again = following / product
    one = alpha + again * grown
    two = again * alpha
    last = (
        r_z - 2.0 * one * z_az + 2.0 * two * v_z + one * one * w_y
        - 2.0 * one * two * v_y + two * two * v_u
    )
    ratio = last / following
    lanes = iota((SIDE, WIDE), 1)
    rows = iota((SIDE, WIDE), 0)
    near = pltpu.roll(coarse, lax.rem((SIDE - member) * SIDE, WIDE), 1)[:, :LANES]
    row = jnp.sum(
        jnp.where(iota((SIDE, LANES), 0) == owner, near, 0.0), axis=0, keepdims=True
    )
    row = jnp.broadcast_to(row, (8, LANES))
    for g in range(8):
        at = slice(8 * g, 8 * g + 8)
        first, image, field, second = (
            ref[at, :] for ref in (first_ref, image_ref, field_ref, second_ref)
        )
        smoothed = smoothed_ref[at, :] + take_lanes(row, map_ref[at, :])
        solution_ref[at, :] = one * first - two * field
        residual_ref[at, :] = side_ref[at, :] - one * image + two * second
        search_ref[at, :] = (
            first - one * field + two * smoothed + ratio * (grown * first - alpha * field)
        )


def shards(
    right_side, coefficient_index, material_coefficients, block_cells, block_inverses,
    aggregate_map, coarse_diagonal,
):
    dims = right_side.shape
    side = right_side.reshape(ROWS, LANES)
    index = coefficient_index.reshape(ROWS, LANES)
    order = block_cells.reshape(ROWS, LANES)
    matrices = block_inverses.reshape(ROWS, LANES, LANES)
    aggregate = aggregate_map.reshape(ROWS, LANES)
    diagonal = coarse_diagonal.reshape(1, SIDE)
    local = shape(ROWS, LANES)
    cells = pltpu.VMEM((ROWS, LANES), F32)
    int_cells = pltpu.VMEM((ROWS, LANES), jnp.int32)
    held = pltpu.VMEM(matrices.shape, F32)
    scratch = [
        cells, cells, pltpu.VMEM((10, SLAB, LANES), F32), pltpu.VMEM((SIDE, LANES), F32),
        held, pltpu.SemaphoreType.DMA,
    ]

    def call(kernel, outs, ins, scratch=(), specs=None):
        return pl.pallas_call(
            kernel,
            out_shape=outs,
            in_specs=specs or [vmem()] * ins,
            out_specs=[vmem()] * len(outs),
            scratch_shapes=list(scratch),
            compiler_params=params(),
            cost_estimate=pl.CostEstimate(
                flops=10**9, bytes_accessed=4 * 10**6, transcendentals=0
            ),
        )

    def exchange(pieces, axis):
        rows = pieces.shape
        pieces = lax.all_to_all(pieces.reshape(rows[0], 1, LANES), axis, 0, 0, tiled=True)
        return pieces.reshape(rows)

    fixed = [
        pltpu.with_memory_space_constraint(array, pltpu.HBM)
        for array in (material_coefficients, side, index, order, matrices, aggregate, diagonal)
    ]
    pieces, kappa, smoothed, numbers = call(
        begin,
        [
            shape(SIDE * F_FIRST, LANES), local, local, local,
        ],
        7,
        [
            pltpu.SMEM(material_coefficients.shape, F32), cells, int_cells, int_cells,
            int_cells, pltpu.VMEM((1, SIDE), F32), cells, cells,
            held, pltpu.SemaphoreType.DMA((7,)),
        ],
        [hbm()] * 7,
    )(*fixed)
    faces = exchange(pieces, FINE)
    (pieces,) = call(relay_first, [shape(SIDE * C_FIRST, LANES)], 4)(
        faces, smoothed, kappa, numbers
    )
    ends = exchange(pieces, COARSE)
    pieces, first, image, smoothed, kappa, lanes, diagonals = call(
        first_image,
        [
            shape(SIDE * F_SECOND, LANES), local, local, local, shape(10, SLAB, LANES),
            shape(10, SLAB, LANES, dtype=jnp.int32), shape(SIDE, WIDE),
        ],
        11,
        scratch,
        [vmem()] * 7 + [hbm()],
    )(
        faces, ends, smoothed, kappa, numbers, aggregate, order, fixed[4],
    )
    faces = exchange(pieces, FINE)
    (pieces,) = call(relay_second, [shape(SIDE * C_SECOND, LANES)], 2)(faces, smoothed)
    ends = exchange(pieces, COARSE)
    pieces, field, second, product = call(
        second_image,
        [shape(WIDE, LANES), local, local, local],
        13,
        scratch[:1] + scratch[2:],
        [vmem()] * 11 + [hbm()],
    )(
        faces, ends, smoothed, kappa, lanes, aggregate, order, diagonals, side, first,
        image, fixed[4],
    )
    pieces = exchange(pieces, (COARSE, FINE))
    (smoothed,) = call(put_back, [local], 2)(product, order)
    results = call(finish, [local, local, local], 9)(
        pieces, diagonals, aggregate, side, first, image, field, second, smoothed
    )
    return tuple(result.reshape(dims) for result in results)


def solution(mesh):
    cells = P(COARSE, FINE, None)
    in_specs = (
        cells,
        cells,
        P(),
        P(COARSE, FINE, None, None),
        P(COARSE, FINE, None, None, None),
        cells,
        cells,
    )
    return jax.shard_map(
        shards, mesh=mesh, in_specs=in_specs, out_specs=(cells,) * 3, check_vma=False
    )
```

```python
import functools

import jax
import jax.numpy as jnp
from jax import lax
from jax.experimental import pallas as pl
from jax.experimental.pallas import tpu as pltpu
from jax.sharding import PartitionSpec as P

AGG = 8
COARSE, FINE = "coarse", "fine"
SWEEPS = 4
OMEGA = 0.8
SIDE = 16
ROWS = 64
LANES = 128
WIDE = SIDE * SIDE
F32, BF16 = jnp.float32, jnp.bfloat16
GROUP = 8

SLAB = 16
RIGHT, LEFT = 8, 15


def vmem():
    return pl.BlockSpec(memory_space=pltpu.VMEM)


def smem():
    return pl.BlockSpec(memory_space=pltpu.SMEM)


def hbm():
    return pl.BlockSpec(memory_space=pltpu.HBM)


def params():
    return pltpu.CompilerParams(vmem_limit_bytes=24 * 1024 * 1024)


def shape(*dims, dtype=F32):
    return jax.ShapeDtypeStruct(dims, dtype)


def iota(dims, axis):
    return lax.broadcasted_iota(jnp.int32, dims, axis)


def take_lanes(values, lanes):
    numbers = lax.GatherDimensionNumbers(
        offset_dims=(),
        collapsed_slice_dims=(1,),
        start_index_map=(1,),
        operand_batching_dims=(0,),
        start_indices_batching_dims=(0,),
    )
    return lax.gather(
        values,
        lanes[..., None],
        numbers,
        slice_sizes=(1, 1),
        mode=lax.GatherScatterMode.PROMISE_IN_BOUNDS,
    )


def split(values):
    high = values.astype(BF16)
    return high, (values - high.astype(F32)).astype(BF16)


def matmul(left, right, left_dim, right_dim):
    dims = (((left_dim,), (right_dim,)), ((), ()))
    return lax.dot_general(left, right, dims, preferred_element_type=F32)


def lane_hits(order_ref, group):
    lane = iota((LANES, LANES), 0)
    return jnp.concatenate(
        [
            jnp.where(lane == order_ref[b : b + 1, :] % LANES, 1.0, 0.0).astype(BF16)
            for b in range(group * GROUP, group * GROUP + GROUP)
        ],
        axis=1,
    )


def row_hit(order_ref, block):
    return iota((ROWS, LANES), 0) == order_ref[block : block + 1, :] // LANES


def column_sum(values):
    total = jnp.sum(values.reshape(-1, 8, LANES), axis=0)
    return jnp.sum(total, axis=0, keepdims=True)


def pick(source_ref, order_ref, picked_ref):
    source = jnp.concatenate(split(source_ref[...]), axis=0)
    for group in range(ROWS // GROUP):
        start = group * GROUP
        found = matmul(source, lane_hits(order_ref, group), 1, 0)
        found = found[:ROWS] + found[ROWS:]
        rows = []
        for part in range(GROUP):
            column = found[:, LANES * part : LANES * (part + 1)]
            rows.append(column_sum(jnp.where(row_hit(order_ref, start + part), column, 0.0)))
        picked_ref[start : start + GROUP, :] = jnp.concatenate(rows, axis=0)


def multiply_blocks(matrices_ref, picked_ref, product_ref):
    wide = (2 * GROUP, GROUP * LANES)
    spread = jnp.where(iota(wide, 0) % GROUP == iota(wide, 1) // LANES, 1.0, 0.0).astype(BF16)
    for start in range(0, ROWS, GROUP):
        high, low = split(picked_ref[start : start + GROUP, :])
        both = jnp.concatenate([high.astype(F32), low.astype(F32)], axis=0)
        columns = matmul(jnp.transpose(both).astype(BF16), spread, 1, 0)
        rows = [
            column_sum(
                matrices_ref[start + part] * columns[:, LANES * part : LANES * (part + 1)]
            )
            for part in range(GROUP)
        ]
        product_ref[start : start + GROUP, :] = jnp.concatenate(rows, axis=0)


def put_back(product_ref, order_ref, target_ref):
    total = jnp.zeros((2 * ROWS, LANES), F32)
    for group in range(ROWS // GROUP):
        start = group * GROUP
        halves_of = [part.astype(F32) for part in split(product_ref[start : start + GROUP, :])]
        hits = [row_hit(order_ref, start + part) for part in range(GROUP)]
        values = [
            jnp.concatenate(
                [
                    jnp.where(hits[part], half[part : part + 1, :], 0.0).astype(BF16)
                    for part in range(GROUP)
                ],
                axis=1,
            )
            for half in halves_of
        ]
        total = total + matmul(
            jnp.concatenate(values, axis=0), lane_hits(order_ref, group), 1, 1
        )
    target_ref[...] = total[:ROWS] + total[ROWS:]


def restrict(field, offset, member):
    total = jnp.sum(jnp.where(offset == 0, field, 0.0), axis=0, keepdims=True)
    up = jnp.sum(jnp.where(offset == 1, field, 0.0), axis=0, keepdims=True)
    down = jnp.sum(jnp.where(offset == -1, field, 0.0), axis=0, keepdims=True)
    total, up, down = (jnp.broadcast_to(x, (8, LANES)) for x in (total, up, down))
    total = total + pltpu.roll(up, AGG, 1) + pltpu.roll(down, LANES - AGG, 1)
    for distance in (1, 2, 4):
        total = total + pltpu.roll(total, LANES - distance, 1)
    lane = iota((8, LANES), 1)
    total = 0.25 * take_lanes(total, (lane % SIDE) * AGG)
    return jnp.where(lane // SIDE == member % 8, total, 0.0)


def moved(values, distance, axis, keep):
    size = values.shape[axis]
    return jnp.where(keep, pltpu.roll(values, distance % size, axis), 0.0)


def coarse_solve(source, diagonal):
    owner, lane = iota((SIDE, WIDE), 0), iota((SIDE, WIDE), 1)
    cell = lane % SIDE
    weight = OMEGA / (6.0 + diagonal)
    guess = weight * source
    for sweep in range(SWEEPS - 1):
        beside = moved(guess, 1, 0, owner > 0) + moved(guess, -1, 0, owner < SIDE - 1)
        beside = beside + moved(guess, SIDE, 1, lane >= SIDE)
        beside = beside + moved(guess, -SIDE, 1, lane < WIDE - SIDE)
        beside = beside + moved(guess, 1, 1, cell > 0) + moved(guess, -1, 1, cell < SIDE - 1)
        guess = (1.0 - OMEGA) * guess + weight * (source + beside)
    return guess


def nearby(coarse, member, rows_ref):
    rows_ref[...] = pltpu.roll(coarse, lax.rem((SIDE + 1 - member) * SIDE, WIDE), 1)[:, :LANES]


def smooth(slabs):
    total = slabs[1:9] + 0.5 * (slabs[0:8] + slabs[2:10])
    planes = []
    lane = iota((8, LANES), 1)
    row = iota((8, LANES), 0)
    for plane in range(8):
        own, ends = total[plane, :8], total[plane, 8:]
        before = jnp.where(row == 0, ends[LEFT - 8 :, :], pltpu.roll(own, 1, 0))
        after = jnp.where(row == 7, ends[:1, :], pltpu.roll(own, 7, 0))
        own = own + 0.5 * (before + after)
        below = jnp.where(lane > 0, pltpu.roll(own, 1, 1), 0.0)
        above = jnp.where(lane < LANES - 1, pltpu.roll(own, LANES - 1, 1), 0.0)
        planes.append(own + 0.5 * (below + above))
    return jnp.stack(planes)


def position():
    return lax.axis_index(COARSE), lax.axis_index(FINE)


def put_faces(field_ref, pieces_ref, rows, row, member):
    before, after = jnp.maximum(member - 1, 0), jnp.minimum(member + 1, SIDE - 1)
    pieces_ref[pl.ds(before * rows + row, 8), :] = field_ref[pl.ds(0, 8, stride=8), :]
    pieces_ref[pl.ds(after * rows + row, 8), :] = field_ref[pl.ds(7, 8, stride=8), :]


def get_faces(pieces_ref, rows, row, member, outside):
    before, after = jnp.maximum(member - 1, 0), jnp.minimum(member + 1, SIDE - 1)
    left = pieces_ref[pl.ds(before * rows + row, 8), :]
    right = pieces_ref[pl.ds(after * rows + row, 8), :]
    left = jnp.where(member > 0, left, outside)
    right = jnp.where(member < SIDE - 1, right, outside)
    return left, right


def fill_slabs(slabs_ref, field_ref, faces, pieces, outside):
    owner, member = position()
    faces_ref, face_rows, face_row = faces
    pieces_ref, rows, plane_row, halo_row = pieces
    left, right = get_faces(faces_ref, face_rows, face_row, member, outside)
    gap = jnp.full((8, LANES), outside, F32)
    for plane in range(8):
        slabs_ref[plane + 1, :8, :] = field_ref[8 * plane : 8 * plane + 8, :]
        slabs_ref[plane + 1, 8:, :] = gap
        slabs_ref[plane + 1, RIGHT : RIGHT + 1, :] = right[plane : plane + 1, :]
        slabs_ref[plane + 1, LEFT : LEFT + 1, :] = left[plane : plane + 1, :]
    for plane, there, inside in (
        (0, jnp.maximum(owner - 1, 0), owner > 0),
        (9, jnp.minimum(owner + 1, SIDE - 1), owner < SIDE - 1),
    ):
        start = there * rows
        slabs_ref[plane, 8:, :] = gap
        slabs_ref[plane, :8, :] = jnp.where(
            inside, pieces_ref[pl.ds(start + plane_row, 8), :], outside
        )
        for side, target in enumerate((LEFT, RIGHT)):
            slabs_ref[plane, target : target + 1, :] = jnp.where(
                inside, pieces_ref[pl.ds(start + halo_row + side, 1), :], outside
            )


def add_prolonged(slabs_ref, numbers_ref, rows_ref):
    owner, member = position()
    for plane in range(10):
        if plane == 0:
            there = jnp.maximum(owner - 1, 0)
        elif plane == 9:
            there = jnp.minimum(owner + 1, SIDE - 1)
        else:
            there = owner
        row = jnp.broadcast_to(rows_ref[pl.ds(there, 1), :], (8, LANES))
        for part in (0, 8):
            number = numbers_ref[plane, part : part + 8, :]
            value = take_lanes(row, jnp.maximum(number, 0))
            slabs_ref[plane, part : part + 8, :] += jnp.where(number >= 0, value, 0.0)


def operate(field, kappa):
    own, own_kappa = field[1:9, :8], kappa[1:9, :8]
    return own_kappa * (8.0 * own - smooth(field)) + own * smooth(kappa) - smooth(
        kappa * field
    )


def offsets(aggregate):
    return aggregate - iota((ROWS, LANES), 1) // AGG


F_FIELD, F_KAPPA, F_MAP, F_SOURCE, F_FIRST = 0, 8, 16, 24, 25
C_FIELD, C_KAPPA, C_MAP, C_HALOS, C_SOURCE, C_DIAGONAL, C_FIRST = 0, 8, 16, 24, 30, 32, 34
F_SOURCE_2, F_SECOND = 8, 9
C_HALO_2, C_SOURCE_2, C_SECOND = 8, 10, 12


def begin(
    table_hbm, side_hbm, index_hbm, order_hbm, matrices_hbm, map_hbm, diagonal_hbm,
    pieces_ref, kappa_ref, smoothed_ref, numbers_ref, matrices_ref,
    table_ref, side_ref, index_ref, order_ref, map_ref, diagonal_ref, picked_ref, product_ref,
    arrived,
):
    owner, member = position()
    copies = [
        pltpu.make_async_copy(source, target, arrived.at[number])
        for number, (source, target) in enumerate(
            (
                (order_hbm, order_ref),
                (side_hbm, side_ref),
                (table_hbm, table_ref),
                (index_hbm, index_ref),
                (map_hbm, map_ref),
                (diagonal_hbm, diagonal_ref),
                (matrices_hbm, matrices_ref),
            )
        )
    ]
    for copy in copies:
        copy.start()
    copies[0].wait()
    for copy in copies[1:-1]:
        copy.wait()
    index = index_ref[...]
    kappa = jnp.zeros((ROWS, LANES), F32)
    for entry in range(table_ref.shape[0]):
        kappa = jnp.where(index == entry, table_ref[entry], kappa)
    kappa_ref[...] = kappa
    pick(side_ref, order_ref, picked_ref)
    copies[-1].wait()
    multiply_blocks(matrices_ref, picked_ref, product_ref)
    put_back(product_ref, order_ref, smoothed_ref)
    aggregate = map_ref[...]
    numbers_ref[...] = aggregate.astype(F32)
    source = restrict(side_ref[...], offsets(aggregate), member)
    spread = jnp.broadcast_to(jnp.concatenate([diagonal_ref[...]] * 8, axis=1), (8, LANES))
    beside = iota((8, LANES), 1) // SIDE == (member + 1) % 8
    put_all(jnp.where(beside, spread, source), pieces_ref, F_FIRST, F_SOURCE)
    put_faces(smoothed_ref, pieces_ref, F_FIRST, F_FIELD, member)
    put_faces(kappa_ref, pieces_ref, F_FIRST, F_KAPPA, member)
    put_faces(numbers_ref, pieces_ref, F_FIRST, F_MAP, member)


def put_all(values, pieces_ref, rows, row):
    for piece in range(SIDE):
        pieces_ref[piece * rows + row : piece * rows + row + 1, :] = values[0:1, :]


def put_planes(field_ref, faces, pieces, outside):
    owner, member = position()
    left, right = get_faces(*faces, member, outside)
    pieces_ref, rows, plane_row, halo_row = pieces
    for there, plane in (
        (jnp.maximum(owner - 1, 0), 0),
        (jnp.minimum(owner + 1, SIDE - 1), 7),
    ):
        start = there * rows
        pieces_ref[pl.ds(start + plane_row, 8), :] = field_ref[8 * plane : 8 * plane + 8, :]
        for side, halo in enumerate((left, right)):
            pieces_ref[pl.ds(start + halo_row + side, 1), :] = halo[plane : plane + 1, :]


def gathered(rows, step):
    here = iota((SIDE, LANES), 0) % 8
    rows = jnp.where(iota((SIDE, LANES), 1) // SIDE == (here + step) % 8, rows, 0.0)
    parts = [jnp.sum(rows[at : at + 8], axis=0, keepdims=True) for at in (0, 8)]
    if step:
        parts = [
            pltpu.roll(jnp.broadcast_to(part, (8, LANES)), LANES - SIDE * step, 1)
            for part in parts
        ]
    return parts


def first_parts(faces_ref, pieces_ref):
    return (
        ((faces_ref, F_FIRST, F_FIELD), (pieces_ref, C_FIRST, C_FIELD, C_HALOS), 0.0),
        ((faces_ref, F_FIRST, F_KAPPA), (pieces_ref, C_FIRST, C_KAPPA, C_HALOS + 2), 0.0),
        ((faces_ref, F_FIRST, F_MAP), (pieces_ref, C_FIRST, C_MAP, C_HALOS + 4), -1.0),
    )


def second_parts(faces_ref, pieces_ref):
    return (faces_ref, F_SECOND, 0), (pieces_ref, C_SECOND, 0, C_HALO_2), 0.0


def relay_first(faces_ref, smoothed_ref, kappa_ref, numbers_ref, pieces_ref):
    rows = faces_ref[pl.ds(F_SOURCE, SIDE, stride=F_FIRST), :]
    for half in range(2):
        put_all(gathered(rows, 0)[half], pieces_ref, C_FIRST, C_SOURCE + half)
        put_all(gathered(rows, 1)[half], pieces_ref, C_FIRST, C_DIAGONAL + half)
    parts = first_parts(faces_ref, pieces_ref)
    for field_ref, part in zip((smoothed_ref, kappa_ref, numbers_ref), parts):
        put_planes(field_ref, *part)


def halves(pieces_ref, rows, row):
    return jnp.concatenate(
        [pieces_ref[pl.ds(row + half, SIDE, stride=rows), :] for half in range(2)], axis=1
    )


def first_image(
    faces_ref, ends_ref, own_ref, own_kappa_ref, numbers_ref, map_ref, order_ref,
    matrices_ref,
    pieces_ref, field_ref, image_ref, smoothed_ref, kappa_ref, lanes_ref, diagonal_ref,
    picked_ref, product_ref, slabs_ref, rows_ref,
):
    owner, member = position()
    diagonal = halves(ends_ref, C_FIRST, C_DIAGONAL)
    diagonal_ref[...] = diagonal
    nearby(coarse_solve(halves(ends_ref, C_FIRST, C_SOURCE), diagonal), member, rows_ref)
    parts = first_parts(faces_ref, ends_ref)
    fill_slabs(slabs_ref, numbers_ref, *parts[2])
    row = iota((10, SLAB, LANES), 1)
    shift = jnp.where(row < 8, SIDE, jnp.where(row == RIGHT, 2 * SIDE, 0))
    number = slabs_ref[...]
    lanes_ref[...] = jnp.where(number >= 0.0, number.astype(jnp.int32) + shift, -1)
    fill_slabs(kappa_ref, own_kappa_ref, *parts[1])
    fill_slabs(slabs_ref, own_ref, *parts[0])
    add_prolonged(slabs_ref, lanes_ref, rows_ref)
    field = slabs_ref[...]
    field_ref[...] = field[1:9, :8].reshape(ROWS, LANES)
    image_ref[...] = operate(field, kappa_ref[...]).reshape(ROWS, LANES)
    pick(image_ref, order_ref, picked_ref)
    multiply_blocks(matrices_ref, picked_ref, product_ref)
    put_back(product_ref, order_ref, smoothed_ref)
    source = restrict(image_ref[...], offsets(map_ref[...]), member)
    put_all(source, pieces_ref, F_SECOND, F_SOURCE_2)
    put_faces(smoothed_ref, pieces_ref, F_SECOND, 0, member)


def relay_second(faces_ref, smoothed_ref, pieces_ref):
    rows = faces_ref[pl.ds(F_SOURCE_2, SIDE, stride=F_SECOND), :]
    for half, values in enumerate(gathered(rows, 0)):
        put_all(values, pieces_ref, C_SECOND, C_SOURCE_2 + half)
    put_planes(smoothed_ref, *second_parts(faces_ref, pieces_ref))


def second_image(
    faces_ref, ends_ref, own_ref, kappa_ref, lanes_ref, map_ref, order_ref,
    diagonal_ref, side_ref, first_ref, image_ref, matrices_ref,
    pieces_ref, field_ref, second_ref, product_ref,
    picked_ref, slabs_ref, rows_ref,
):
    owner, member = position()
    nearby(coarse_solve(halves(ends_ref, C_SECOND, C_SOURCE_2), diagonal_ref[...]), member, rows_ref)
    fill_slabs(slabs_ref, own_ref, *second_parts(faces_ref, ends_ref))
    add_prolonged(slabs_ref, lanes_ref, rows_ref)
    slabs = slabs_ref[...]
    field = slabs[1:9, :8].reshape(ROWS, LANES)
    field_ref[...] = field
    second = operate(slabs, kappa_ref[...]).reshape(ROWS, LANES)
    second_ref[...] = second
    pick(second_ref, order_ref, picked_ref)
    multiply_blocks(matrices_ref, picked_ref, product_ref)
    first = first_ref[...]
    image = image_ref[...]
    pairs = (
        side_ref[...] * first,
        first * image,
        image * field,
        second * first,
        second * field,
        picked_ref[...] * product_ref[...],
    )
    lane = iota((8, LANES), 1)
    message = restrict(second, offsets(map_ref[...]), member)
    beside = lax.rem(member + 1, 8) * SIDE
    for number, pair in enumerate(pairs):
        total = jnp.sum(jnp.sum(pair, axis=0, keepdims=True), axis=1, keepdims=True)
        message = jnp.where(lane == beside + number, total, message)
    for start in range(0, WIDE, 8):
        pieces_ref[start : start + 8, :] = message


def finish(
    pieces_ref, diagonal_ref, map_ref, side_ref, first_ref, image_ref, field_ref, second_ref,
    smoothed_ref,
    solution_ref, residual_ref, search_ref,
):
    owner, member = position()
    pieces = pieces_ref[...].reshape(SIDE, SIDE, LANES)
    place = iota((SIDE, LANES), 0) % 8
    group = iota((SIDE, LANES), 1) // SIDE
    pieces_sum = jnp.sum(pieces, axis=0)
    sums = jnp.where(group == (place + 1) % 8, pieces_sum, 0.0)
    kept = jnp.where((group == place)[None], pieces, 0.0)
    source = jnp.concatenate(
        [jnp.sum(kept[:, :8], axis=1), jnp.sum(kept[:, 8:], axis=1)], axis=1
    )
    coarse = coarse_solve(source, diagonal_ref[...])
    lane = iota((1, LANES), 1)
    sums = jnp.sum(sums, axis=0, keepdims=True)

    def total(number):
        picked = jnp.where(lane % SIDE == number, sums, 0.0)
        return jnp.sum(picked, axis=1, keepdims=True)

    def whole(array):
        return jnp.sum(jnp.sum(array, axis=0, keepdims=True), axis=1, keepdims=True)

    r_z, z_az, w_y, v_z, v_y, v_bv = (total(number) for number in range(6))
    v_u = v_bv + 4.0 * whole(source * coarse)
    alpha = r_z / z_az
    following = r_z - 2.0 * alpha * z_az + alpha * alpha * w_y
    grown = 1.0 + following / r_z
    product = grown * grown * z_az - grown * alpha * (v_z + w_y) + alpha * alpha * v_y
    again = following / product
    one = alpha + again * grown
    two = again * alpha
    last = (
        r_z - 2.0 * one * z_az + 2.0 * two * v_z + one * one * w_y
        - 2.0 * one * two * v_y + two * two * v_u
    )
    ratio = last / following
    lanes = iota((SIDE, WIDE), 1)
    rows = iota((SIDE, WIDE), 0)
    near = pltpu.roll(coarse, lax.rem((SIDE - member) * SIDE, WIDE), 1)[:, :LANES]
    row = jnp.sum(
        jnp.where(iota((SIDE, LANES), 0) == owner, near, 0.0), axis=0, keepdims=True
    )
    row = jnp.broadcast_to(row, (8, LANES))
    for g in range(8):
        at = slice(8 * g, 8 * g + 8)
        first, image, field, second = (
            ref[at, :] for ref in (first_ref, image_ref, field_ref, second_ref)
        )
        smoothed = smoothed_ref[at, :] + take_lanes(row, map_ref[at, :])
        solution_ref[at, :] = one * first - two * field
        residual_ref[at, :] = side_ref[at, :] - one * image + two * second
        search_ref[at, :] = (
            first - one * field + two * smoothed + ratio * (grown * first - alpha * field)
        )


def shards(
    right_side, coefficient_index, material_coefficients, block_cells, block_inverses,
    aggregate_map, coarse_diagonal,
):
    dims = right_side.shape
    side = right_side.reshape(ROWS, LANES)
    index = coefficient_index.reshape(ROWS, LANES)
    order = block_cells.reshape(ROWS, LANES)
    matrices = block_inverses.reshape(ROWS, LANES, LANES)
    aggregate = aggregate_map.reshape(ROWS, LANES)
    diagonal = coarse_diagonal.reshape(1, SIDE)
    local = shape(ROWS, LANES)
    cells = pltpu.VMEM((ROWS, LANES), F32)
    int_cells = pltpu.VMEM((ROWS, LANES), jnp.int32)
    scratch = [
        cells, cells, pltpu.VMEM((10, SLAB, LANES), F32), pltpu.VMEM((SIDE, LANES), F32),
    ]

    def call(kernel, outs, ins, scratch=(), specs=None):
        return pl.pallas_call(
            kernel,
            out_shape=outs,
            in_specs=specs or [vmem()] * ins,
            out_specs=[vmem()] * len(outs),
            scratch_shapes=list(scratch),
            compiler_params=params(),
            cost_estimate=pl.CostEstimate(
                flops=10**9, bytes_accessed=4 * 10**6, transcendentals=0
            ),
        )

    def exchange(pieces, axis):
        rows = pieces.shape
        pieces = lax.all_to_all(pieces.reshape(rows[0], 1, LANES), axis, 0, 0, tiled=True)
        return pieces.reshape(rows)

    fixed = [
        pltpu.with_memory_space_constraint(array, pltpu.HBM)
        for array in (material_coefficients, side, index, order, matrices, aggregate, diagonal)
    ]
    pieces, kappa, smoothed, numbers, matrices = call(
        begin,
        [
            shape(SIDE * F_FIRST, LANES), local, local, local, pltpu.VMEM(matrices.shape, F32),
        ],
        7,
        [
            pltpu.SMEM(material_coefficients.shape, F32), cells, int_cells, int_cells,
            int_cells, pltpu.VMEM((1, SIDE), F32), cells, cells,
            pltpu.SemaphoreType.DMA((7,)),
        ],
        [hbm()] * 7,
    )(*fixed)
    matrices = pltpu.with_memory_space_constraint(matrices, pltpu.VMEM)
    faces = exchange(pieces, FINE)
    (pieces,) = call(relay_first, [shape(SIDE * C_FIRST, LANES)], 4)(
        faces, smoothed, kappa, numbers
    )
    ends = exchange(pieces, COARSE)
    pieces, first, image, smoothed, kappa, lanes, diagonals = call(
        first_image,
        [
            shape(SIDE * F_SECOND, LANES), local, local, local, shape(10, SLAB, LANES),
            shape(10, SLAB, LANES, dtype=jnp.int32), shape(SIDE, WIDE),
        ],
        8,
        scratch,
    )(
        faces, ends, smoothed, kappa, numbers, aggregate, order, matrices,
    )
    faces = exchange(pieces, FINE)
    (pieces,) = call(relay_second, [shape(SIDE * C_SECOND, LANES)], 2)(faces, smoothed)
    ends = exchange(pieces, COARSE)
    pieces, field, second, product = call(
        second_image,
        [shape(WIDE, LANES), local, local, local],
        12,
        scratch[:1] + scratch[2:],
    )(
        faces, ends, smoothed, kappa, lanes, aggregate, order, diagonals, side, first,
        image, matrices,
    )
    pieces = exchange(pieces, (COARSE, FINE))
    (smoothed,) = call(put_back, [local], 2)(product, order)
    results = call(finish, [local, local, local], 9)(
        pieces, diagonals, aggregate, side, first, image, field, second, smoothed
    )
    return tuple(result.reshape(dims) for result in results)


def solution(mesh):
    cells = P(COARSE, FINE, None)
    in_specs = (
        cells,
        cells,
        P(),
        P(COARSE, FINE, None, None),
        P(COARSE, FINE, None, None, None),
        cells,
        cells,
    )
    return jax.shard_map(
        shards, mesh=mesh, in_specs=in_specs, out_specs=(cells,) * 3, check_vma=False
    )
```

```python
import functools

import jax
import jax.numpy as jnp
from jax import lax
from jax.experimental import pallas as pl
from jax.experimental.pallas import tpu as pltpu
from jax.sharding import PartitionSpec as P

AGG = 8
COARSE, FINE = "coarse", "fine"
SWEEPS = 4
OMEGA = 0.8
SIDE = 16
ROWS = 64
LANES = 128
WIDE = SIDE * SIDE
F32, BF16 = jnp.float32, jnp.bfloat16
GROUP = 8

SLAB = 16
RIGHT, LEFT = 8, 15


def vmem():
    return pl.BlockSpec(memory_space=pltpu.VMEM)


def smem():
    return pl.BlockSpec(memory_space=pltpu.SMEM)


def hbm():
    return pl.BlockSpec(memory_space=pltpu.HBM)


def params():
    return pltpu.CompilerParams(vmem_limit_bytes=24 * 1024 * 1024)


def shape(*dims, dtype=F32):
    return jax.ShapeDtypeStruct(dims, dtype)


def iota(dims, axis):
    return lax.broadcasted_iota(jnp.int32, dims, axis)


def take_lanes(values, lanes):
    numbers = lax.GatherDimensionNumbers(
        offset_dims=(),
        collapsed_slice_dims=(1,),
        start_index_map=(1,),
        operand_batching_dims=(0,),
        start_indices_batching_dims=(0,),
    )
    return lax.gather(
        values,
        lanes[..., None],
        numbers,
        slice_sizes=(1, 1),
        mode=lax.GatherScatterMode.PROMISE_IN_BOUNDS,
    )


def split(values):
    high = values.astype(BF16)
    return high, (values - high.astype(F32)).astype(BF16)


def matmul(left, right, left_dim, right_dim):
    dims = (((left_dim,), (right_dim,)), ((), ()))
    return lax.dot_general(left, right, dims, preferred_element_type=F32)


def lane_hits(order_ref, group):
    lane = iota((LANES, LANES), 0)
    return jnp.concatenate(
        [
            jnp.where(lane == order_ref[b : b + 1, :] % LANES, 1.0, 0.0).astype(BF16)
            for b in range(group * GROUP, group * GROUP + GROUP)
        ],
        axis=1,
    )


def row_hit(order_ref, block):
    return iota((ROWS, LANES), 0) == order_ref[block : block + 1, :] // LANES


def column_sum(values):
    total = jnp.sum(values.reshape(-1, 8, LANES), axis=0)
    return jnp.sum(total, axis=0, keepdims=True)


def pick(source_ref, order_ref, picked_ref):
    source = jnp.concatenate(split(source_ref[...]), axis=0)
    for group in range(ROWS // GROUP):
        start = group * GROUP
        found = matmul(source, lane_hits(order_ref, group), 1, 0)
        found = found[:ROWS] + found[ROWS:]
        rows = []
        for part in range(GROUP):
            column = found[:, LANES * part : LANES * (part + 1)]
            rows.append(column_sum(jnp.where(row_hit(order_ref, start + part), column, 0.0)))
        picked_ref[start : start + GROUP, :] = jnp.concatenate(rows, axis=0)


def multiply_blocks(matrices_ref, picked_ref, product_ref):
    wide = (2 * GROUP, GROUP * LANES)
    spread = jnp.where(iota(wide, 0) % GROUP == iota(wide, 1) // LANES, 1.0, 0.0).astype(BF16)
    for start in range(0, ROWS, GROUP):
        high, low = split(picked_ref[start : start + GROUP, :])
        both = jnp.concatenate([high.astype(F32), low.astype(F32)], axis=0)
        columns = matmul(jnp.transpose(both).astype(BF16), spread, 1, 0)
        rows = [
            column_sum(
                matrices_ref[start + part] * columns[:, LANES * part : LANES * (part + 1)]
            )
            for part in range(GROUP)
        ]
        product_ref[start : start + GROUP, :] = jnp.concatenate(rows, axis=0)


def put_back(product_ref, order_ref, target_ref):
    total = jnp.zeros((2 * ROWS, LANES), F32)
    for group in range(ROWS // GROUP):
        start = group * GROUP
        halves_of = [part.astype(F32) for part in split(product_ref[start : start + GROUP, :])]
        hits = [row_hit(order_ref, start + part) for part in range(GROUP)]
        values = [
            jnp.concatenate(
                [
                    jnp.where(hits[part], half[part : part + 1, :], 0.0).astype(BF16)
                    for part in range(GROUP)
                ],
                axis=1,
            )
            for half in halves_of
        ]
        total = total + matmul(
            jnp.concatenate(values, axis=0), lane_hits(order_ref, group), 1, 1
        )
    target_ref[...] = total[:ROWS] + total[ROWS:]


def restrict(field, offset, member):
    total = jnp.sum(jnp.where(offset == 0, field, 0.0), axis=0, keepdims=True)
    up = jnp.sum(jnp.where(offset == 1, field, 0.0), axis=0, keepdims=True)
    down = jnp.sum(jnp.where(offset == -1, field, 0.0), axis=0, keepdims=True)
    total, up, down = (jnp.broadcast_to(x, (8, LANES)) for x in (total, up, down))
    total = total + pltpu.roll(up, AGG, 1) + pltpu.roll(down, LANES - AGG, 1)
    for distance in (1, 2, 4):
        total = total + pltpu.roll(total, LANES - distance, 1)
    lane = iota((8, LANES), 1)
    total = 0.25 * take_lanes(total, (lane % SIDE) * AGG)
    return jnp.where(lane // SIDE == member % 8, total, 0.0)


def moved(values, distance, axis, keep):
    size = values.shape[axis]
    return jnp.where(keep, pltpu.roll(values, distance % size, axis), 0.0)


def coarse_solve(source, diagonal):
    owner, lane = iota((SIDE, WIDE), 0), iota((SIDE, WIDE), 1)
    cell = lane % SIDE
    weight = OMEGA / (6.0 + diagonal)
    guess = weight * source
    for sweep in range(SWEEPS - 1):
        beside = moved(guess, 1, 0, owner > 0) + moved(guess, -1, 0, owner < SIDE - 1)
        beside = beside + moved(guess, SIDE, 1, lane >= SIDE)
        beside = beside + moved(guess, -SIDE, 1, lane < WIDE - SIDE)
        beside = beside + moved(guess, 1, 1, cell > 0) + moved(guess, -1, 1, cell < SIDE - 1)
        guess = (1.0 - OMEGA) * guess + weight * (source + beside)
    return guess


def nearby(coarse, member, rows_ref):
    rows_ref[...] = pltpu.roll(coarse, lax.rem((SIDE + 1 - member) * SIDE, WIDE), 1)[:, :LANES]


def smooth(slabs):
    total = slabs[1:9] + 0.5 * (slabs[0:8] + slabs[2:10])
    planes = []
    lane = iota((8, LANES), 1)
    row = iota((8, LANES), 0)
    for plane in range(8):
        own, ends = total[plane, :8], total[plane, 8:]
        before = jnp.where(row == 0, ends[LEFT - 8 :, :], pltpu.roll(own, 1, 0))
        after = jnp.where(row == 7, ends[:1, :], pltpu.roll(own, 7, 0))
        own = own + 0.5 * (before + after)
        below = jnp.where(lane > 0, pltpu.roll(own, 1, 1), 0.0)
        above = jnp.where(lane < LANES - 1, pltpu.roll(own, LANES - 1, 1), 0.0)
        planes.append(own + 0.5 * (below + above))
    return jnp.stack(planes)


def position():
    return lax.axis_index(COARSE), lax.axis_index(FINE)


def put_faces(field_ref, pieces_ref, rows, row, member):
    before, after = jnp.maximum(member - 1, 0), jnp.minimum(member + 1, SIDE - 1)
    pieces_ref[pl.ds(before * rows + row, 8), :] = field_ref[pl.ds(0, 8, stride=8), :]
    pieces_ref[pl.ds(after * rows + row, 8), :] = field_ref[pl.ds(7, 8, stride=8), :]


def within(left, right, member, outside):
    left = jnp.where(member > 0, left, outside)
    right = jnp.where(member < SIDE - 1, right, outside)
    return left, right


def get_faces(pieces_ref, rows, row, member, outside):
    before, after = jnp.maximum(member - 1, 0), jnp.minimum(member + 1, SIDE - 1)
    left = pieces_ref[pl.ds(before * rows + row, 8), :]
    right = pieces_ref[pl.ds(after * rows + row, 8), :]
    return within(left, right, member, outside)


def fill_slabs(slabs_ref, field_ref, faces, ends, outside):
    owner, member = position()
    left, right = faces
    gap = jnp.full((8, LANES), outside, F32)
    for plane in range(8):
        slabs_ref[plane + 1, :8, :] = field_ref[8 * plane : 8 * plane + 8, :]
        slabs_ref[plane + 1, 8:, :] = gap
        slabs_ref[plane + 1, RIGHT : RIGHT + 1, :] = right[plane : plane + 1, :]
        slabs_ref[plane + 1, LEFT : LEFT + 1, :] = left[plane : plane + 1, :]
    for plane, inside, (own, *halos) in (
        (0, owner > 0, ends[0]),
        (9, owner < SIDE - 1, ends[1]),
    ):
        slabs_ref[plane, 8:, :] = gap
        slabs_ref[plane, :8, :] = jnp.where(inside, own, outside)
        for target, halo in zip((LEFT, RIGHT), halos):
            slabs_ref[plane, target : target + 1, :] = jnp.where(inside, halo, outside)


def add_prolonged(slabs_ref, numbers_ref, rows_ref):
    owner, member = position()
    for plane in range(10):
        if plane == 0:
            there = jnp.maximum(owner - 1, 0)
        elif plane == 9:
            there = jnp.minimum(owner + 1, SIDE - 1)
        else:
            there = owner
        row = jnp.broadcast_to(rows_ref[pl.ds(there, 1), :], (8, LANES))
        for part in (0, 8):
            number = numbers_ref[plane, part : part + 8, :]
            value = take_lanes(row, jnp.maximum(number, 0))
            slabs_ref[plane, part : part + 8, :] += jnp.where(number >= 0, value, 0.0)


def operate(field, kappa):
    own, own_kappa = field[1:9, :8], kappa[1:9, :8]
    return own_kappa * (8.0 * own - smooth(field)) + own * smooth(kappa) - smooth(
        kappa * field
    )


def offsets(aggregate):
    return aggregate - iota((ROWS, LANES), 1) // AGG


FIELD, KAPPA, MAP, FACE_ROWS, PLANE_ROWS = 0, 8, 16, 24, 32
OUTSIDE = (0.0, 0.0, -1.0)
F_SOURCE_2, F_SECOND = 8, 9
C_HALO_2, C_SOURCE_2, C_SECOND = 8, 10, 12


def begin(
    table_hbm, side_hbm, index_hbm, order_hbm, matrices_hbm, map_hbm, diagonal_hbm,
    pieces_ref, left_ref, right_ref, kappa_ref, smoothed_ref, numbers_ref,
    table_ref, side_ref, index_ref, order_ref, map_ref, diagonal_ref, picked_ref, product_ref,
    matrices_ref, arrived,
):
    owner, member = position()
    copies = [
        pltpu.make_async_copy(source, target, arrived.at[number])
        for number, (source, target) in enumerate(
            (
                (order_hbm, order_ref),
                (side_hbm, side_ref),
                (table_hbm, table_ref),
                (index_hbm, index_ref),
                (map_hbm, map_ref),
                (diagonal_hbm, diagonal_ref),
                (matrices_hbm, matrices_ref),
            )
        )
    ]
    for copy in copies:
        copy.start()
    copies[0].wait()
    for copy in copies[1:-1]:
        copy.wait()
    index = index_ref[...]
    kappa = jnp.zeros((ROWS, LANES), F32)
    for entry in range(table_ref.shape[0]):
        kappa = jnp.where(index == entry, table_ref[entry], kappa)
    kappa_ref[...] = kappa
    pick(side_ref, order_ref, picked_ref)
    copies[-1].wait()
    multiply_blocks(matrices_ref, picked_ref, product_ref)
    put_back(product_ref, order_ref, smoothed_ref)
    aggregate = map_ref[...]
    numbers_ref[...] = aggregate.astype(F32)
    source = restrict(side_ref[...], offsets(aggregate), member)
    spread = jnp.broadcast_to(jnp.concatenate([diagonal_ref[...]] * 8, axis=1), (8, LANES))
    beside = iota((8, LANES), 1) // SIDE == (member + 1) % 8
    message = jnp.where(beside, spread, source)
    for start in range(0, WIDE, 8):
        pieces_ref[start : start + 8, :] = message
    for row, field_ref in ((FIELD, smoothed_ref), (KAPPA, kappa_ref), (MAP, numbers_ref)):
        left_ref[row : row + 8, :] = field_ref[pl.ds(0, 8, stride=8), :]
        right_ref[row : row + 8, :] = field_ref[pl.ds(7, 8, stride=8), :]


def put_all(values, pieces_ref, rows, row):
    for piece in range(SIDE):
        pieces_ref[piece * rows + row : piece * rows + row + 1, :] = values[0:1, :]


def put_planes(field_ref, faces, pieces, outside):
    owner, member = position()
    left, right = get_faces(*faces, member, outside)
    pieces_ref, rows, plane_row, halo_row = pieces
    for there, plane in (
        (jnp.maximum(owner - 1, 0), 0),
        (jnp.minimum(owner + 1, SIDE - 1), 7),
    ):
        start = there * rows
        pieces_ref[pl.ds(start + plane_row, 8), :] = field_ref[8 * plane : 8 * plane + 8, :]
        for side, halo in enumerate((left, right)):
            pieces_ref[pl.ds(start + halo_row + side, 1), :] = halo[plane : plane + 1, :]


def gathered(rows):
    place = iota((SIDE, LANES), 0) % 8
    rows = jnp.where(iota((SIDE, LANES), 1) // SIDE == place, rows, 0.0)
    return [jnp.sum(rows[at : at + 8], axis=0, keepdims=True) for at in (0, 8)]


def coarse_rows(pieces_ref, step):
    pieces = pieces_ref[...].reshape(SIDE, SIDE, LANES)
    place = (iota((SIDE, LANES), 0) + step) % 8
    kept = jnp.where((iota((SIDE, LANES), 1) // SIDE == place)[None], pieces, 0.0)
    halves_of = [jnp.sum(kept[:, :8], axis=1), jnp.sum(kept[:, 8:], axis=1)]
    if step:
        halves_of = [pltpu.roll(half, LANES - SIDE * step, 1) for half in halves_of]
    return jnp.concatenate(halves_of, axis=1)


def first_faces(left_ref, right_ref, row, member, outside):
    return within(left_ref[row : row + 8, :], right_ref[row : row + 8, :], member, outside)


def relay_first(
    left_ref, right_ref, smoothed_ref, kappa_ref, numbers_ref, before_ref, after_ref
):
    owner, member = position()
    fields = (smoothed_ref, kappa_ref, numbers_ref)
    for target_ref, plane in ((before_ref, 0), (after_ref, 7)):
        target_ref[FACE_ROWS:, :] = jnp.zeros((8, LANES), F32)
        for number, field_ref in enumerate(fields):
            row = 8 * number
            faces = first_faces(left_ref, right_ref, row, member, OUTSIDE[number])
            target_ref[row : row + 8, :] = field_ref[8 * plane : 8 * plane + 8, :]
            for side, face in enumerate(faces):
                halo = FACE_ROWS + 2 * number + side
                target_ref[halo : halo + 1, :] = face[plane : plane + 1, :]


def fill_first(slabs_ref, field_ref, left_ref, right_ref, before_ref, after_ref, number):
    owner, member = position()
    row, outside = 8 * number, OUTSIDE[number]
    halo = FACE_ROWS + 2 * number
    ends = [
        (end[row : row + 8, :], end[halo : halo + 1, :], end[halo + 1 : halo + 2, :])
        for end in (before_ref, after_ref)
    ]
    faces = first_faces(left_ref, right_ref, row, member, outside)
    fill_slabs(slabs_ref, field_ref, faces, ends, outside)


def fill_second(slabs_ref, field_ref, faces_ref, pieces_ref):
    owner, member = position()
    ends = []
    for there in (jnp.maximum(owner - 1, 0), jnp.minimum(owner + 1, SIDE - 1)):
        start = there * C_SECOND
        ends.append(
            (
                pieces_ref[pl.ds(start, 8), :],
                pieces_ref[pl.ds(start + C_HALO_2, 1), :],
                pieces_ref[pl.ds(start + C_HALO_2 + 1, 1), :],
            )
        )
    faces = get_faces(faces_ref, F_SECOND, 0, member, 0.0)
    fill_slabs(slabs_ref, field_ref, faces, ends, 0.0)


def halves(pieces_ref, rows, row):
    return jnp.concatenate(
        [pieces_ref[pl.ds(row + half, SIDE, stride=rows), :] for half in range(2)], axis=1
    )


def first_image(
    rows_of_all_ref, left_ref, right_ref, before_ref, after_ref,
    own_ref, own_kappa_ref, numbers_ref, map_ref, order_ref, matrices_hbm,
    pieces_ref, field_ref, image_ref, smoothed_ref, kappa_ref, lanes_ref, diagonal_ref,
    matrices_ref,
    picked_ref, product_ref, slabs_ref, rows_ref, arrived,
):
    owner, member = position()
    copy = pltpu.make_async_copy(matrices_hbm, matrices_ref, arrived)
    copy.start()
    diagonal = coarse_rows(rows_of_all_ref, 1)
    diagonal_ref[...] = diagonal
    nearby(coarse_solve(coarse_rows(rows_of_all_ref, 0), diagonal), member, rows_ref)
    around = left_ref, right_ref, before_ref, after_ref
    fill_first(slabs_ref, numbers_ref, *around, 2)
    row = iota((10, SLAB, LANES), 1)
    shift = jnp.where(row < 8, SIDE, jnp.where(row == RIGHT, 2 * SIDE, 0))
    number = slabs_ref[...]
    lanes_ref[...] = jnp.where(number >= 0.0, number.astype(jnp.int32) + shift, -1)
    fill_first(kappa_ref, own_kappa_ref, *around, 1)
    fill_first(slabs_ref, own_ref, *around, 0)
    add_prolonged(slabs_ref, lanes_ref, rows_ref)
    field = slabs_ref[...]
    field_ref[...] = field[1:9, :8].reshape(ROWS, LANES)
    image_ref[...] = operate(field, kappa_ref[...]).reshape(ROWS, LANES)
    pick(image_ref, order_ref, picked_ref)
    copy.wait()
    multiply_blocks(matrices_ref, picked_ref, product_ref)
    put_back(product_ref, order_ref, smoothed_ref)
    source = restrict(image_ref[...], offsets(map_ref[...]), member)
    put_all(source, pieces_ref, F_SECOND, F_SOURCE_2)
    put_faces(smoothed_ref, pieces_ref, F_SECOND, 0, member)


def relay_second(faces_ref, smoothed_ref, pieces_ref):
    rows = faces_ref[pl.ds(F_SOURCE_2, SIDE, stride=F_SECOND), :]
    for half, values in enumerate(gathered(rows)):
        put_all(values, pieces_ref, C_SECOND, C_SOURCE_2 + half)
    faces, pieces = (faces_ref, F_SECOND, 0), (pieces_ref, C_SECOND, 0, C_HALO_2)
    put_planes(smoothed_ref, faces, pieces, 0.0)


def second_image(
    faces_ref, ends_ref, own_ref, kappa_ref, lanes_ref, map_ref, order_ref,
    diagonal_ref, side_ref, first_ref, image_ref, matrices_ref,
    pieces_ref, field_ref, second_ref, product_ref,
    picked_ref, slabs_ref, rows_ref,
):
    owner, member = position()
    source = halves(ends_ref, C_SECOND, C_SOURCE_2)
    nearby(coarse_solve(source, diagonal_ref[...]), member, rows_ref)
    fill_second(slabs_ref, own_ref, faces_ref, ends_ref)
    add_prolonged(slabs_ref, lanes_ref, rows_ref)
    slabs = slabs_ref[...]
    field = slabs[1:9, :8].reshape(ROWS, LANES)
    field_ref[...] = field
    second = operate(slabs, kappa_ref[...]).reshape(ROWS, LANES)
    second_ref[...] = second
    pick(second_ref, order_ref, picked_ref)
    multiply_blocks(matrices_ref, picked_ref, product_ref)
    first = first_ref[...]
    image = image_ref[...]
    pairs = (
        side_ref[...] * first,
        first * image,
        image * field,
        second * first,
        second * field,
        picked_ref[...] * product_ref[...],
    )
    lane = iota((8, LANES), 1)
    message = restrict(second, offsets(map_ref[...]), member)
    beside = lax.rem(member + 1, 8) * SIDE
    for number, pair in enumerate(pairs):
        total = jnp.sum(jnp.sum(pair, axis=0, keepdims=True), axis=1, keepdims=True)
        message = jnp.where(lane == beside + number, total, message)
    for start in range(0, WIDE, 8):
        pieces_ref[start : start + 8, :] = message


def finish(
    pieces_ref, diagonal_ref, map_ref, side_ref, first_ref, image_ref, field_ref, second_ref,
    smoothed_ref,
    solution_ref, residual_ref, search_ref,
):
    owner, member = position()
    pieces = pieces_ref[...].reshape(SIDE, SIDE, LANES)
    place = iota((SIDE, LANES), 0) % 8
    group = iota((SIDE, LANES), 1) // SIDE
    pieces_sum = jnp.sum(pieces, axis=0)
    sums = jnp.where(group == (place + 1) % 8, pieces_sum, 0.0)
    source = coarse_rows(pieces_ref, 0)
    coarse = coarse_solve(source, diagonal_ref[...])
    lane = iota((1, LANES), 1)
    sums = jnp.sum(sums, axis=0, keepdims=True)

    def total(number):
        picked = jnp.where(lane % SIDE == number, sums, 0.0)
        return jnp.sum(picked, axis=1, keepdims=True)

    def whole(array):
        return jnp.sum(jnp.sum(array, axis=0, keepdims=True), axis=1, keepdims=True)

    r_z, z_az, w_y, v_z, v_y, v_bv = (total(number) for number in range(6))
    v_u = v_bv + 4.0 * whole(source * coarse)
    alpha = r_z / z_az
    following = r_z - 2.0 * alpha * z_az + alpha * alpha * w_y
    grown = 1.0 + following / r_z
    product = grown * grown * z_az - grown * alpha * (v_z + w_y) + alpha * alpha * v_y
    again = following / product
    one = alpha + again * grown
    two = again * alpha
    last = (
        r_z - 2.0 * one * z_az + 2.0 * two * v_z + one * one * w_y
        - 2.0 * one * two * v_y + two * two * v_u
    )
    ratio = last / following
    lanes = iota((SIDE, WIDE), 1)
    rows = iota((SIDE, WIDE), 0)
    near = pltpu.roll(coarse, lax.rem((SIDE - member) * SIDE, WIDE), 1)[:, :LANES]
    row = jnp.sum(
        jnp.where(iota((SIDE, LANES), 0) == owner, near, 0.0), axis=0, keepdims=True
    )
    row = jnp.broadcast_to(row, (8, LANES))
    for g in range(8):
        at = slice(8 * g, 8 * g + 8)
        first, image, field, second = (
            ref[at, :] for ref in (first_ref, image_ref, field_ref, second_ref)
        )
        smoothed = smoothed_ref[at, :] + take_lanes(row, map_ref[at, :])
        solution_ref[at, :] = one * first - two * field
        residual_ref[at, :] = side_ref[at, :] - one * image + two * second
        search_ref[at, :] = (
            first - one * field + two * smoothed + ratio * (grown * first - alpha * field)
        )


def shards(
    right_side, coefficient_index, material_coefficients, block_cells, block_inverses,
    aggregate_map, coarse_diagonal,
):
    dims = right_side.shape
    side = right_side.reshape(ROWS, LANES)
    index = coefficient_index.reshape(ROWS, LANES)
    order = block_cells.reshape(ROWS, LANES)
    matrices = block_inverses.reshape(ROWS, LANES, LANES)
    aggregate = aggregate_map.reshape(ROWS, LANES)
    diagonal = coarse_diagonal.reshape(1, SIDE)
    local = shape(ROWS, LANES)
    cells = pltpu.VMEM((ROWS, LANES), F32)
    int_cells = pltpu.VMEM((ROWS, LANES), jnp.int32)
    scratch = [
        cells, cells, pltpu.VMEM((10, SLAB, LANES), F32), pltpu.VMEM((SIDE, LANES), F32),
    ]

    def call(kernel, outs, ins, scratch=(), specs=None):
        return pl.pallas_call(
            kernel,
            out_shape=outs,
            in_specs=specs or [vmem()] * ins,
            out_specs=[vmem()] * len(outs),
            scratch_shapes=list(scratch),
            compiler_params=params(),
            cost_estimate=pl.CostEstimate(
                flops=10**9, bytes_accessed=4 * 10**6, transcendentals=0
            ),
        )

    def exchange(pieces, axis):
        rows = pieces.shape
        pieces = lax.all_to_all(pieces.reshape(rows[0], 1, LANES), axis, 0, 0, tiled=True)
        return pieces.reshape(rows)

    def ring(rows, axis, step):
        return lax.ppermute(rows, axis, [(i, (i + step) % SIDE) for i in range(SIDE)])

    fixed = [
        pltpu.with_memory_space_constraint(array, pltpu.HBM)
        for array in (material_coefficients, side, index, order, matrices, aggregate, diagonal)
    ]
    pieces, left, right, kappa, smoothed, numbers = call(
        begin,
        [
            shape(WIDE, LANES), shape(FACE_ROWS, LANES), shape(FACE_ROWS, LANES), local, local,
            local,
        ],
        7,
        [
            pltpu.SMEM(material_coefficients.shape, F32), cells, int_cells, int_cells,
            int_cells, pltpu.VMEM((1, SIDE), F32), cells, cells,
            pltpu.VMEM(matrices.shape, F32), pltpu.SemaphoreType.DMA((7,)),
        ],
        [hbm()] * 7,
    )(*fixed)
    right, left = ring(left, FINE, -1), ring(right, FINE, 1)
    rows = exchange(pieces, (COARSE, FINE))
    before, after = call(
        relay_first, [shape(PLANE_ROWS, LANES), shape(PLANE_ROWS, LANES)], 5
    )(left, right, smoothed, kappa, numbers)
    after, before = ring(before, COARSE, -1), ring(after, COARSE, 1)
    pieces, first, image, smoothed, kappa, lanes, diagonals, matrices = call(
        first_image,
        [
            shape(SIDE * F_SECOND, LANES), local, local, local, shape(10, SLAB, LANES),
            shape(10, SLAB, LANES, dtype=jnp.int32), shape(SIDE, WIDE),
            pltpu.VMEM(matrices.shape, F32),
        ],
        11,
        scratch + [pltpu.SemaphoreType.DMA],
        [vmem()] * 10 + [hbm()],
    )(
        rows, left, right, before, after, smoothed, kappa, numbers, aggregate, order, fixed[4]
    )
    matrices = pltpu.with_memory_space_constraint(matrices, pltpu.VMEM)
    faces = exchange(pieces, FINE)
    (pieces,) = call(relay_second, [shape(SIDE * C_SECOND, LANES)], 2)(faces, smoothed)
    ends = exchange(pieces, COARSE)
    pieces, field, second, product = call(
        second_image,
        [shape(WIDE, LANES), local, local, local],
        12,
        scratch[:1] + scratch[2:],
    )(
        faces, ends, smoothed, kappa, lanes, aggregate, order, diagonals, side, first,
        image, matrices,
    )
    pieces = exchange(pieces, (COARSE, FINE))
    (smoothed,) = call(put_back, [local], 2)(product, order)
    results = call(finish, [local, local, local], 9)(
        pieces, diagonals, aggregate, side, first, image, field, second, smoothed
    )
    return tuple(result.reshape(dims) for result in results)


def solution(mesh):
    cells = P(COARSE, FINE, None)
    in_specs = (
        cells,
        cells,
        P(),
        P(COARSE, FINE, None, None),
        P(COARSE, FINE, None, None, None),
        cells,
        cells,
    )
    return jax.shard_map(
        shards, mesh=mesh, in_specs=in_specs, out_specs=(cells,) * 3, check_vma=False
    )
```

```python
import functools

import jax
import jax.numpy as jnp
from jax import lax
from jax.experimental import pallas as pl
from jax.experimental.pallas import tpu as pltpu
from jax.sharding import PartitionSpec as P

AGG = 8
COARSE, FINE = "coarse", "fine"
SWEEPS = 4
OMEGA = 0.8
SIDE = 16
ROWS = 64
LANES = 128
WIDE = SIDE * SIDE
F32, BF16 = jnp.float32, jnp.bfloat16
GROUP = 8

SLAB = 16
RIGHT, LEFT = 8, 15


def vmem():
    return pl.BlockSpec(memory_space=pltpu.VMEM)


def smem():
    return pl.BlockSpec(memory_space=pltpu.SMEM)


def hbm():
    return pl.BlockSpec(memory_space=pltpu.HBM)


def params():
    return pltpu.CompilerParams(vmem_limit_bytes=24 * 1024 * 1024)


def shape(*dims, dtype=F32):
    return jax.ShapeDtypeStruct(dims, dtype)


def iota(dims, axis):
    return lax.broadcasted_iota(jnp.int32, dims, axis)


def take_lanes(values, lanes):
    numbers = lax.GatherDimensionNumbers(
        offset_dims=(),
        collapsed_slice_dims=(1,),
        start_index_map=(1,),
        operand_batching_dims=(0,),
        start_indices_batching_dims=(0,),
    )
    return lax.gather(
        values,
        lanes[..., None],
        numbers,
        slice_sizes=(1, 1),
        mode=lax.GatherScatterMode.PROMISE_IN_BOUNDS,
    )


def split(values):
    high = values.astype(BF16)
    return high, (values - high.astype(F32)).astype(BF16)


def matmul(left, right, left_dim, right_dim):
    dims = (((left_dim,), (right_dim,)), ((), ()))
    return lax.dot_general(left, right, dims, preferred_element_type=F32)


def lane_hits(order_ref, group):
    lane = iota((LANES, LANES), 0)
    return jnp.concatenate(
        [
            jnp.where(lane == order_ref[b : b + 1, :] % LANES, 1.0, 0.0).astype(BF16)
            for b in range(group * GROUP, group * GROUP + GROUP)
        ],
        axis=1,
    )


def row_hit(order_ref, block):
    return iota((ROWS, LANES), 0) == order_ref[block : block + 1, :] // LANES


def column_sum(values):
    total = jnp.sum(values.reshape(-1, 8, LANES), axis=0)
    return jnp.sum(total, axis=0, keepdims=True)


def pick(source_ref, order_ref, picked_ref):
    source = jnp.concatenate(split(source_ref[...]), axis=0)
    for group in range(ROWS // GROUP):
        start = group * GROUP
        found = matmul(source, lane_hits(order_ref, group), 1, 0)
        found = found[:ROWS] + found[ROWS:]
        rows = []
        for part in range(GROUP):
            column = found[:, LANES * part : LANES * (part + 1)]
            rows.append(column_sum(jnp.where(row_hit(order_ref, start + part), column, 0.0)))
        picked_ref[start : start + GROUP, :] = jnp.concatenate(rows, axis=0)


def multiply_blocks(matrices_ref, picked_ref, product_ref):
    wide = (2 * GROUP, GROUP * LANES)
    spread = jnp.where(iota(wide, 0) % GROUP == iota(wide, 1) // LANES, 1.0, 0.0).astype(BF16)
    for start in range(0, ROWS, GROUP):
        high, low = split(picked_ref[start : start + GROUP, :])
        both = jnp.concatenate([high.astype(F32), low.astype(F32)], axis=0)
        columns = matmul(jnp.transpose(both).astype(BF16), spread, 1, 0)
        rows = [
            column_sum(
                matrices_ref[start + part] * columns[:, LANES * part : LANES * (part + 1)]
            )
            for part in range(GROUP)
        ]
        product_ref[start : start + GROUP, :] = jnp.concatenate(rows, axis=0)


def put_back(product_ref, order_ref, target_ref):
    total = jnp.zeros((2 * ROWS, LANES), F32)
    for group in range(ROWS // GROUP):
        start = group * GROUP
        halves_of = [part.astype(F32) for part in split(product_ref[start : start + GROUP, :])]
        hits = [row_hit(order_ref, start + part) for part in range(GROUP)]
        values = [
            jnp.concatenate(
                [
                    jnp.where(hits[part], half[part : part + 1, :], 0.0).astype(BF16)
                    for part in range(GROUP)
                ],
                axis=1,
            )
            for half in halves_of
        ]
        total = total + matmul(
            jnp.concatenate(values, axis=0), lane_hits(order_ref, group), 1, 1
        )
    target_ref[...] = total[:ROWS] + total[ROWS:]


def restrict(field, offset, member):
    total = jnp.sum(jnp.where(offset == 0, field, 0.0), axis=0, keepdims=True)
    up = jnp.sum(jnp.where(offset == 1, field, 0.0), axis=0, keepdims=True)
    down = jnp.sum(jnp.where(offset == -1, field, 0.0), axis=0, keepdims=True)
    total, up, down = (jnp.broadcast_to(x, (8, LANES)) for x in (total, up, down))
    total = total + pltpu.roll(up, AGG, 1) + pltpu.roll(down, LANES - AGG, 1)
    for distance in (1, 2, 4):
        total = total + pltpu.roll(total, LANES - distance, 1)
    lane = iota((8, LANES), 1)
    total = 0.25 * take_lanes(total, (lane % SIDE) * AGG)
    return jnp.where(lane // SIDE == member % 8, total, 0.0)


def moved(values, distance, axis, keep):
    size = values.shape[axis]
    return jnp.where(keep, pltpu.roll(values, distance % size, axis), 0.0)


def coarse_solve(source, diagonal):
    owner, lane = iota((SIDE, WIDE), 0), iota((SIDE, WIDE), 1)
    cell = lane % SIDE
    weight = OMEGA / (6.0 + diagonal)
    guess = weight * source
    for sweep in range(SWEEPS - 1):
        beside = moved(guess, 1, 0, owner > 0) + moved(guess, -1, 0, owner < SIDE - 1)
        beside = beside + moved(guess, SIDE, 1, lane >= SIDE)
        beside = beside + moved(guess, -SIDE, 1, lane < WIDE - SIDE)
        beside = beside + moved(guess, 1, 1, cell > 0) + moved(guess, -1, 1, cell < SIDE - 1)
        guess = (1.0 - OMEGA) * guess + weight * (source + beside)
    return guess


def nearby(coarse, member, rows_ref):
    rows_ref[...] = pltpu.roll(coarse, lax.rem((SIDE + 1 - member) * SIDE, WIDE), 1)[:, :LANES]


def smooth(slabs):
    total = slabs[1:9] + 0.5 * (slabs[0:8] + slabs[2:10])
    planes = []
    lane = iota((8, LANES), 1)
    row = iota((8, LANES), 0)
    for plane in range(8):
        own, ends = total[plane, :8], total[plane, 8:]
        before = jnp.where(row == 0, ends[LEFT - 8 :, :], pltpu.roll(own, 1, 0))
        after = jnp.where(row == 7, ends[:1, :], pltpu.roll(own, 7, 0))
        own = own + 0.5 * (before + after)
        below = jnp.where(lane > 0, pltpu.roll(own, 1, 1), 0.0)
        above = jnp.where(lane < LANES - 1, pltpu.roll(own, LANES - 1, 1), 0.0)
        planes.append(own + 0.5 * (below + above))
    return jnp.stack(planes)


def position():
    return lax.axis_index(COARSE), lax.axis_index(FINE)


def put_faces(field_ref, pieces_ref, rows, row, member):
    before, after = jnp.maximum(member - 1, 0), jnp.minimum(member + 1, SIDE - 1)
    pieces_ref[pl.ds(before * rows + row, 8), :] = field_ref[pl.ds(0, 8, stride=8), :]
    pieces_ref[pl.ds(after * rows + row, 8), :] = field_ref[pl.ds(7, 8, stride=8), :]


def within(left, right, member, outside):
    left = jnp.where(member > 0, left, outside)
    right = jnp.where(member < SIDE - 1, right, outside)
    return left, right


def get_faces(pieces_ref, rows, row, member, outside):
    before, after = jnp.maximum(member - 1, 0), jnp.minimum(member + 1, SIDE - 1)
    left = pieces_ref[pl.ds(before * rows + row, 8), :]
    right = pieces_ref[pl.ds(after * rows + row, 8), :]
    return within(left, right, member, outside)


def fill_slabs(slabs_ref, field_ref, faces, ends, outside):
    owner, member = position()
    left, right = faces
    gap = jnp.full((8, LANES), outside, F32)
    for plane in range(8):
        slabs_ref[plane + 1, :8, :] = field_ref[8 * plane : 8 * plane + 8, :]
        slabs_ref[plane + 1, 8:, :] = gap
        slabs_ref[plane + 1, RIGHT : RIGHT + 1, :] = right[plane : plane + 1, :]
        slabs_ref[plane + 1, LEFT : LEFT + 1, :] = left[plane : plane + 1, :]
    for plane, inside, (own, *halos) in (
        (0, owner > 0, ends[0]),
        (9, owner < SIDE - 1, ends[1]),
    ):
        slabs_ref[plane, 8:, :] = gap
        slabs_ref[plane, :8, :] = jnp.where(inside, own, outside)
        for target, halo in zip((LEFT, RIGHT), halos):
            slabs_ref[plane, target : target + 1, :] = jnp.where(inside, halo, outside)


def add_prolonged(slabs_ref, numbers_ref, rows_ref):
    owner, member = position()
    for plane in range(10):
        if plane == 0:
            there = jnp.maximum(owner - 1, 0)
        elif plane == 9:
            there = jnp.minimum(owner + 1, SIDE - 1)
        else:
            there = owner
        row = jnp.broadcast_to(rows_ref[pl.ds(there, 1), :], (8, LANES))
        for part in (0, 8):
            number = numbers_ref[plane, part : part + 8, :]
            value = take_lanes(row, jnp.maximum(number, 0))
            slabs_ref[plane, part : part + 8, :] += jnp.where(number >= 0, value, 0.0)


def operate(field, kappa):
    own, own_kappa = field[1:9, :8], kappa[1:9, :8]
    return own_kappa * (8.0 * own - smooth(field)) + own * smooth(kappa) - smooth(
        kappa * field
    )


def offsets(aggregate):
    return aggregate - iota((ROWS, LANES), 1) // AGG


FIELD, KAPPA, MAP, FACE_ROWS, PLANE_ROWS = 0, 8, 16, 24, 32
OUTSIDE = (0.0, 0.0, -1.0)
F_SOURCE_2, F_SECOND = 8, 9
C_HALO_2, C_SOURCE_2, C_SECOND = 8, 10, 12


def begin(
    table_hbm, side_hbm, index_hbm, order_hbm, matrices_hbm, map_hbm, diagonal_hbm,
    pieces_ref, pair_ref, cross_ref, kappa_ref, smoothed_ref, numbers_ref,
    table_ref, side_ref, index_ref, order_ref, map_ref, diagonal_ref, picked_ref, product_ref,
    matrices_ref, arrived,
):
    owner, member = position()
    copies = [
        pltpu.make_async_copy(source, target, arrived.at[number])
        for number, (source, target) in enumerate(
            (
                (order_hbm, order_ref),
                (side_hbm, side_ref),
                (table_hbm, table_ref),
                (index_hbm, index_ref),
                (map_hbm, map_ref),
                (diagonal_hbm, diagonal_ref),
                (matrices_hbm, matrices_ref),
            )
        )
    ]
    for copy in copies:
        copy.start()
    copies[0].wait()
    for copy in copies[1:-1]:
        copy.wait()
    index = index_ref[...]
    kappa = jnp.zeros((ROWS, LANES), F32)
    for entry in range(table_ref.shape[0]):
        kappa = jnp.where(index == entry, table_ref[entry], kappa)
    kappa_ref[...] = kappa
    pick(side_ref, order_ref, picked_ref)
    copies[-1].wait()
    multiply_blocks(matrices_ref, picked_ref, product_ref)
    put_back(product_ref, order_ref, smoothed_ref)
    aggregate = map_ref[...]
    numbers_ref[...] = aggregate.astype(F32)
    source = restrict(side_ref[...], offsets(aggregate), member)
    spread = jnp.broadcast_to(jnp.concatenate([diagonal_ref[...]] * 8, axis=1), (8, LANES))
    beside = iota((8, LANES), 1) // SIDE == (member + 1) % 8
    message = jnp.where(beside, spread, source)
    for start in range(0, WIDE, 8):
        pieces_ref[start : start + 8, :] = message
    for row, field_ref in ((FIELD, smoothed_ref), (KAPPA, kappa_ref), (MAP, numbers_ref)):
        left = field_ref[pl.ds(0, 8, stride=8), :]
        right = field_ref[pl.ds(7, 8, stride=8), :]
        even = member % 2 == 0
        pair_ref[row : row + 8, :] = jnp.where(even, right, left)
        cross_ref[row : row + 8, :] = jnp.where(even, left, right)


def put_all(values, pieces_ref, rows, row):
    for piece in range(SIDE):
        pieces_ref[piece * rows + row : piece * rows + row + 1, :] = values[0:1, :]


def put_planes(field_ref, faces, pieces, outside):
    owner, member = position()
    left, right = get_faces(*faces, member, outside)
    pieces_ref, rows, plane_row, halo_row = pieces
    for there, plane in (
        (jnp.maximum(owner - 1, 0), 0),
        (jnp.minimum(owner + 1, SIDE - 1), 7),
    ):
        start = there * rows
        pieces_ref[pl.ds(start + plane_row, 8), :] = field_ref[8 * plane : 8 * plane + 8, :]
        for side, halo in enumerate((left, right)):
            pieces_ref[pl.ds(start + halo_row + side, 1), :] = halo[plane : plane + 1, :]


def gathered(rows):
    place = iota((SIDE, LANES), 0) % 8
    rows = jnp.where(iota((SIDE, LANES), 1) // SIDE == place, rows, 0.0)
    return [jnp.sum(rows[at : at + 8], axis=0, keepdims=True) for at in (0, 8)]


def coarse_rows(pieces_ref, step):
    pieces = pieces_ref[...].reshape(SIDE, SIDE, LANES)
    place = (iota((SIDE, LANES), 0) + step) % 8
    kept = jnp.where((iota((SIDE, LANES), 1) // SIDE == place)[None], pieces, 0.0)
    halves_of = [jnp.sum(kept[:, :8], axis=1), jnp.sum(kept[:, 8:], axis=1)]
    if step:
        halves_of = [pltpu.roll(half, LANES - SIDE * step, 1) for half in halves_of]
    return jnp.concatenate(halves_of, axis=1)


def first_faces(pair_ref, cross_ref, row, member, outside):
    pair, cross = pair_ref[row : row + 8, :], cross_ref[row : row + 8, :]
    even = member % 2 == 0
    left, right = jnp.where(even, cross, pair), jnp.where(even, pair, cross)
    return within(left, right, member, outside)


def relay_first(
    pair_ref, cross_ref, smoothed_ref, kappa_ref, numbers_ref, before_ref, after_ref
):
    owner, member = position()
    fields = (smoothed_ref, kappa_ref, numbers_ref)
    for target_ref, plane in ((before_ref, 0), (after_ref, 7)):
        target_ref[FACE_ROWS:, :] = jnp.zeros((8, LANES), F32)
        for number, field_ref in enumerate(fields):
            row = 8 * number
            faces = first_faces(pair_ref, cross_ref, row, member, OUTSIDE[number])
            target_ref[row : row + 8, :] = field_ref[8 * plane : 8 * plane + 8, :]
            for side, face in enumerate(faces):
                halo = FACE_ROWS + 2 * number + side
                target_ref[halo : halo + 1, :] = face[plane : plane + 1, :]


def fill_first(slabs_ref, field_ref, pair_ref, cross_ref, before_ref, after_ref, number):
    owner, member = position()
    row, outside = 8 * number, OUTSIDE[number]
    halo = FACE_ROWS + 2 * number
    ends = [
        (end[row : row + 8, :], end[halo : halo + 1, :], end[halo + 1 : halo + 2, :])
        for end in (before_ref, after_ref)
    ]
    faces = first_faces(pair_ref, cross_ref, row, member, outside)
    fill_slabs(slabs_ref, field_ref, faces, ends, outside)


def fill_second(slabs_ref, field_ref, faces_ref, pieces_ref):
    owner, member = position()
    ends = []
    for there in (jnp.maximum(owner - 1, 0), jnp.minimum(owner + 1, SIDE - 1)):
        start = there * C_SECOND
        ends.append(
            (
                pieces_ref[pl.ds(start, 8), :],
                pieces_ref[pl.ds(start + C_HALO_2, 1), :],
                pieces_ref[pl.ds(start + C_HALO_2 + 1, 1), :],
            )
        )
    faces = get_faces(faces_ref, F_SECOND, 0, member, 0.0)
    fill_slabs(slabs_ref, field_ref, faces, ends, 0.0)


def halves(pieces_ref, rows, row):
    return jnp.concatenate(
        [pieces_ref[pl.ds(row + half, SIDE, stride=rows), :] for half in range(2)], axis=1
    )


def first_image(
    rows_of_all_ref, pair_ref, cross_ref, before_ref, after_ref,
    own_ref, own_kappa_ref, numbers_ref, map_ref, order_ref, matrices_hbm,
    pieces_ref, field_ref, image_ref, smoothed_ref, kappa_ref, lanes_ref, diagonal_ref,
    matrices_ref,
    picked_ref, product_ref, slabs_ref, rows_ref, arrived,
):
    owner, member = position()
    copy = pltpu.make_async_copy(matrices_hbm, matrices_ref, arrived)
    copy.start()
    diagonal = coarse_rows(rows_of_all_ref, 1)
    diagonal_ref[...] = diagonal
    nearby(coarse_solve(coarse_rows(rows_of_all_ref, 0), diagonal), member, rows_ref)
    around = pair_ref, cross_ref, before_ref, after_ref
    fill_first(slabs_ref, numbers_ref, *around, 2)
    row = iota((10, SLAB, LANES), 1)
    shift = jnp.where(row < 8, SIDE, jnp.where(row == RIGHT, 2 * SIDE, 0))
    number = slabs_ref[...]
    lanes_ref[...] = jnp.where(number >= 0.0, number.astype(jnp.int32) + shift, -1)
    fill_first(kappa_ref, own_kappa_ref, *around, 1)
    fill_first(slabs_ref, own_ref, *around, 0)
    add_prolonged(slabs_ref, lanes_ref, rows_ref)
    field = slabs_ref[...]
    field_ref[...] = field[1:9, :8].reshape(ROWS, LANES)
    image_ref[...] = operate(field, kappa_ref[...]).reshape(ROWS, LANES)
    pick(image_ref, order_ref, picked_ref)
    copy.wait()
    multiply_blocks(matrices_ref, picked_ref, product_ref)
    put_back(product_ref, order_ref, smoothed_ref)
    source = restrict(image_ref[...], offsets(map_ref[...]), member)
    put_all(source, pieces_ref, F_SECOND, F_SOURCE_2)
    put_faces(smoothed_ref, pieces_ref, F_SECOND, 0, member)


def relay_second(faces_ref, smoothed_ref, pieces_ref):
    rows = faces_ref[pl.ds(F_SOURCE_2, SIDE, stride=F_SECOND), :]
    for half, values in enumerate(gathered(rows)):
        put_all(values, pieces_ref, C_SECOND, C_SOURCE_2 + half)
    faces, pieces = (faces_ref, F_SECOND, 0), (pieces_ref, C_SECOND, 0, C_HALO_2)
    put_planes(smoothed_ref, faces, pieces, 0.0)


def second_image(
    faces_ref, ends_ref, own_ref, kappa_ref, lanes_ref, map_ref, order_ref,
    diagonal_ref, side_ref, first_ref, image_ref, matrices_ref,
    pieces_ref, field_ref, second_ref, product_ref,
    picked_ref, slabs_ref, rows_ref,
):
    owner, member = position()
    source = halves(ends_ref, C_SECOND, C_SOURCE_2)
    nearby(coarse_solve(source, diagonal_ref[...]), member, rows_ref)
    fill_second(slabs_ref, own_ref, faces_ref, ends_ref)
    add_prolonged(slabs_ref, lanes_ref, rows_ref)
    slabs = slabs_ref[...]
    field = slabs[1:9, :8].reshape(ROWS, LANES)
    field_ref[...] = field
    second = operate(slabs, kappa_ref[...]).reshape(ROWS, LANES)
    second_ref[...] = second
    pick(second_ref, order_ref, picked_ref)
    multiply_blocks(matrices_ref, picked_ref, product_ref)
    first = first_ref[...]
    image = image_ref[...]
    pairs = (
        side_ref[...] * first,
        first * image,
        image * field,
        second * first,
        second * field,
        picked_ref[...] * product_ref[...],
    )
    lane = iota((8, LANES), 1)
    message = restrict(second, offsets(map_ref[...]), member)
    beside = lax.rem(member + 1, 8) * SIDE
    for number, pair in enumerate(pairs):
        total = jnp.sum(jnp.sum(pair, axis=0, keepdims=True), axis=1, keepdims=True)
        message = jnp.where(lane == beside + number, total, message)
    for start in range(0, WIDE, 8):
        pieces_ref[start : start + 8, :] = message


def finish(
    pieces_ref, diagonal_ref, map_ref, side_ref, first_ref, image_ref, field_ref, second_ref,
    smoothed_ref,
    solution_ref, residual_ref, search_ref,
):
    owner, member = position()
    pieces = pieces_ref[...].reshape(SIDE, SIDE, LANES)
    place = iota((SIDE, LANES), 0) % 8
    group = iota((SIDE, LANES), 1) // SIDE
    pieces_sum = jnp.sum(pieces, axis=0)
    sums = jnp.where(group == (place + 1) % 8, pieces_sum, 0.0)
    source = coarse_rows(pieces_ref, 0)
    coarse = coarse_solve(source, diagonal_ref[...])
    lane = iota((1, LANES), 1)
    sums = jnp.sum(sums, axis=0, keepdims=True)

    def total(number):
        picked = jnp.where(lane % SIDE == number, sums, 0.0)
        return jnp.sum(picked, axis=1, keepdims=True)

    def whole(array):
        return jnp.sum(jnp.sum(array, axis=0, keepdims=True), axis=1, keepdims=True)

    r_z, z_az, w_y, v_z, v_y, v_bv = (total(number) for number in range(6))
    v_u = v_bv + 4.0 * whole(source * coarse)
    alpha = r_z / z_az
    following = r_z - 2.0 * alpha * z_az + alpha * alpha * w_y
    grown = 1.0 + following / r_z
    product = grown * grown * z_az - grown * alpha * (v_z + w_y) + alpha * alpha * v_y
    again = following / product
    one = alpha + again * grown
    two = again * alpha
    last = (
        r_z - 2.0 * one * z_az + 2.0 * two * v_z + one * one * w_y
        - 2.0 * one * two * v_y + two * two * v_u
    )
    ratio = last / following
    lanes = iota((SIDE, WIDE), 1)
    rows = iota((SIDE, WIDE), 0)
    near = pltpu.roll(coarse, lax.rem((SIDE - member) * SIDE, WIDE), 1)[:, :LANES]
    row = jnp.sum(
        jnp.where(iota((SIDE, LANES), 0) == owner, near, 0.0), axis=0, keepdims=True
    )
    row = jnp.broadcast_to(row, (8, LANES))
    for g in range(8):
        at = slice(8 * g, 8 * g + 8)
        first, image, field, second = (
            ref[at, :] for ref in (first_ref, image_ref, field_ref, second_ref)
        )
        smoothed = smoothed_ref[at, :] + take_lanes(row, map_ref[at, :])
        solution_ref[at, :] = one * first - two * field
        residual_ref[at, :] = side_ref[at, :] - one * image + two * second
        search_ref[at, :] = (
            first - one * field + two * smoothed + ratio * (grown * first - alpha * field)
        )


def shards(
    right_side, coefficient_index, material_coefficients, block_cells, block_inverses,
    aggregate_map, coarse_diagonal,
):
    dims = right_side.shape
    side = right_side.reshape(ROWS, LANES)
    index = coefficient_index.reshape(ROWS, LANES)
    order = block_cells.reshape(ROWS, LANES)
    matrices = block_inverses.reshape(ROWS, LANES, LANES)
    aggregate = aggregate_map.reshape(ROWS, LANES)
    diagonal = coarse_diagonal.reshape(1, SIDE)
    local = shape(ROWS, LANES)
    cells = pltpu.VMEM((ROWS, LANES), F32)
    int_cells = pltpu.VMEM((ROWS, LANES), jnp.int32)
    scratch = [
        cells, cells, pltpu.VMEM((10, SLAB, LANES), F32), pltpu.VMEM((SIDE, LANES), F32),
    ]

    def call(kernel, outs, ins, scratch=(), specs=None):
        return pl.pallas_call(
            kernel,
            out_shape=outs,
            in_specs=specs or [vmem()] * ins,
            out_specs=[vmem()] * len(outs),
            scratch_shapes=list(scratch),
            compiler_params=params(),
            cost_estimate=pl.CostEstimate(
                flops=10**9, bytes_accessed=4 * 10**6, transcendentals=0
            ),
        )

    def exchange(pieces, axis):
        rows = pieces.shape
        pieces = lax.all_to_all(pieces.reshape(rows[0], 1, LANES), axis, 0, 0, tiled=True)
        return pieces.reshape(rows)

    def ring(rows, axis, step):
        return lax.ppermute(rows, axis, [(i, (i + step) % SIDE) for i in range(SIDE)])

    fixed = [
        pltpu.with_memory_space_constraint(array, pltpu.HBM)
        for array in (material_coefficients, side, index, order, matrices, aggregate, diagonal)
    ]
    pieces, pair, cross, kappa, smoothed, numbers = call(
        begin,
        [
            shape(WIDE, LANES), shape(FACE_ROWS, LANES), shape(FACE_ROWS, LANES), local, local,
            local,
        ],
        7,
        [
            pltpu.SMEM(material_coefficients.shape, F32), cells, int_cells, int_cells,
            int_cells, pltpu.VMEM((1, SIDE), F32), cells, cells,
            pltpu.VMEM(matrices.shape, F32), pltpu.SemaphoreType.DMA((7,)),
        ],
        [hbm()] * 7,
    )(*fixed)
    pair = lax.ppermute(pair, FINE, [(i, i ^ 1) for i in range(SIDE)])
    cross = lax.ppermute(
        cross, FINE, [(i, (i + (1 if i % 2 else -1)) % SIDE) for i in range(SIDE)]
    )
    rows = exchange(pieces, (COARSE, FINE))
    before, after = call(
        relay_first, [shape(PLANE_ROWS, LANES), shape(PLANE_ROWS, LANES)], 5
    )(pair, cross, smoothed, kappa, numbers)
    after, before = ring(before, COARSE, -1), ring(after, COARSE, 1)
    pieces, first, image, smoothed, kappa, lanes, diagonals, matrices = call(
        first_image,
        [
            shape(SIDE * F_SECOND, LANES), local, local, local, shape(10, SLAB, LANES),
            shape(10, SLAB, LANES, dtype=jnp.int32), shape(SIDE, WIDE),
            pltpu.VMEM(matrices.shape, F32),
        ],
        11,
        scratch + [pltpu.SemaphoreType.DMA],
        [vmem()] * 10 + [hbm()],
    )(
        rows, pair, cross, before, after, smoothed, kappa, numbers, aggregate, order, fixed[4]
    )
    matrices = pltpu.with_memory_space_constraint(matrices, pltpu.VMEM)
    faces = exchange(pieces, FINE)
    (pieces,) = call(relay_second, [shape(SIDE * C_SECOND, LANES)], 2)(faces, smoothed)
    ends = exchange(pieces, COARSE)
    pieces, field, second, product = call(
        second_image,
        [shape(WIDE, LANES), local, local, local],
        12,
        scratch[:1] + scratch[2:],
    )(
        faces, ends, smoothed, kappa, lanes, aggregate, order, diagonals, side, first,
        image, matrices,
    )
    pieces = exchange(pieces, (COARSE, FINE))
    (smoothed,) = call(put_back, [local], 2)(product, order)
    results = call(finish, [local, local, local], 9)(
        pieces, diagonals, aggregate, side, first, image, field, second, smoothed
    )
    return tuple(result.reshape(dims) for result in results)


def solution(mesh):
    cells = P(COARSE, FINE, None)
    in_specs = (
        cells,
        cells,
        P(),
        P(COARSE, FINE, None, None),
        P(COARSE, FINE, None, None, None),
        cells,
        cells,
    )
    return jax.shard_map(
        shards, mesh=mesh, in_specs=in_specs, out_specs=(cells,) * 3, check_vma=False
    )
```

```python
import functools

import jax
import jax.numpy as jnp
from jax import lax
from jax.experimental import pallas as pl
from jax.experimental.pallas import tpu as pltpu
from jax.sharding import PartitionSpec as P

AGG = 8
COARSE, FINE = "coarse", "fine"
SWEEPS = 4
OMEGA = 0.8
SIDE = 16
ROWS = 64
LANES = 128
WIDE = SIDE * SIDE
F32, BF16 = jnp.float32, jnp.bfloat16
GROUP = 8

SLAB = 16
RIGHT, LEFT = 8, 15


def vmem():
    return pl.BlockSpec(memory_space=pltpu.VMEM)


def smem():
    return pl.BlockSpec(memory_space=pltpu.SMEM)


def hbm():
    return pl.BlockSpec(memory_space=pltpu.HBM)


def params():
    return pltpu.CompilerParams(vmem_limit_bytes=24 * 1024 * 1024)


def shape(*dims, dtype=F32):
    return jax.ShapeDtypeStruct(dims, dtype)


def iota(dims, axis):
    return lax.broadcasted_iota(jnp.int32, dims, axis)


def take_lanes(values, lanes):
    numbers = lax.GatherDimensionNumbers(
        offset_dims=(),
        collapsed_slice_dims=(1,),
        start_index_map=(1,),
        operand_batching_dims=(0,),
        start_indices_batching_dims=(0,),
    )
    return lax.gather(
        values,
        lanes[..., None],
        numbers,
        slice_sizes=(1, 1),
        mode=lax.GatherScatterMode.PROMISE_IN_BOUNDS,
    )


def split(values):
    high = values.astype(BF16)
    return high, (values - high.astype(F32)).astype(BF16)


def matmul(left, right, left_dim, right_dim):
    dims = (((left_dim,), (right_dim,)), ((), ()))
    return lax.dot_general(left, right, dims, preferred_element_type=F32)


def lane_hits(order_ref, group):
    lane = iota((LANES, LANES), 0)
    return jnp.concatenate(
        [
            jnp.where(lane == order_ref[b : b + 1, :] % LANES, 1.0, 0.0).astype(BF16)
            for b in range(group * GROUP, group * GROUP + GROUP)
        ],
        axis=1,
    )


def row_hit(order_ref, block):
    return iota((ROWS, LANES), 0) == order_ref[block : block + 1, :] // LANES


def column_sum(values):
    total = jnp.sum(values.reshape(-1, 8, LANES), axis=0)
    return jnp.sum(total, axis=0, keepdims=True)


def pick(source_ref, order_ref, picked_ref):
    source = jnp.concatenate(split(source_ref[...]), axis=0)
    for group in range(ROWS // GROUP):
        start = group * GROUP
        found = matmul(source, lane_hits(order_ref, group), 1, 0)
        found = found[:ROWS] + found[ROWS:]
        rows = []
        for part in range(GROUP):
            column = found[:, LANES * part : LANES * (part + 1)]
            rows.append(column_sum(jnp.where(row_hit(order_ref, start + part), column, 0.0)))
        picked_ref[start : start + GROUP, :] = jnp.concatenate(rows, axis=0)


def multiply_blocks(matrices_ref, picked_ref, product_ref):
    wide = (2 * GROUP, GROUP * LANES)
    spread = jnp.where(iota(wide, 0) % GROUP == iota(wide, 1) // LANES, 1.0, 0.0).astype(BF16)
    for start in range(0, ROWS, GROUP):
        high, low = split(picked_ref[start : start + GROUP, :])
        both = jnp.concatenate([high.astype(F32), low.astype(F32)], axis=0)
        columns = matmul(jnp.transpose(both).astype(BF16), spread, 1, 0)
        rows = [
            column_sum(
                matrices_ref[start + part] * columns[:, LANES * part : LANES * (part + 1)]
            )
            for part in range(GROUP)
        ]
        product_ref[start : start + GROUP, :] = jnp.concatenate(rows, axis=0)


def put_back(product_ref, order_ref, target_ref):
    total = jnp.zeros((2 * ROWS, LANES), F32)
    for group in range(ROWS // GROUP):
        start = group * GROUP
        halves_of = [part.astype(F32) for part in split(product_ref[start : start + GROUP, :])]
        hits = [row_hit(order_ref, start + part) for part in range(GROUP)]
        values = [
            jnp.concatenate(
                [
                    jnp.where(hits[part], half[part : part + 1, :], 0.0).astype(BF16)
                    for part in range(GROUP)
                ],
                axis=1,
            )
            for half in halves_of
        ]
        total = total + matmul(
            jnp.concatenate(values, axis=0), lane_hits(order_ref, group), 1, 1
        )
    target_ref[...] = total[:ROWS] + total[ROWS:]


def restrict(field, offset, member):
    total = jnp.sum(jnp.where(offset == 0, field, 0.0), axis=0, keepdims=True)
    up = jnp.sum(jnp.where(offset == 1, field, 0.0), axis=0, keepdims=True)
    down = jnp.sum(jnp.where(offset == -1, field, 0.0), axis=0, keepdims=True)
    total, up, down = (jnp.broadcast_to(x, (8, LANES)) for x in (total, up, down))
    total = total + pltpu.roll(up, AGG, 1) + pltpu.roll(down, LANES - AGG, 1)
    for distance in (1, 2, 4):
        total = total + pltpu.roll(total, LANES - distance, 1)
    lane = iota((8, LANES), 1)
    total = 0.25 * take_lanes(total, (lane % SIDE) * AGG)
    return jnp.where(lane // SIDE == member % 8, total, 0.0)


def moved(values, distance, axis, keep):
    size = values.shape[axis]
    return jnp.where(keep, pltpu.roll(values, distance % size, axis), 0.0)


def coarse_solve(source, diagonal):
    owner, lane = iota((SIDE, WIDE), 0), iota((SIDE, WIDE), 1)
    cell = lane % SIDE
    weight = OMEGA / (6.0 + diagonal)
    guess = weight * source
    for sweep in range(SWEEPS - 1):
        beside = moved(guess, 1, 0, owner > 0) + moved(guess, -1, 0, owner < SIDE - 1)
        beside = beside + moved(guess, SIDE, 1, lane >= SIDE)
        beside = beside + moved(guess, -SIDE, 1, lane < WIDE - SIDE)
        beside = beside + moved(guess, 1, 1, cell > 0) + moved(guess, -1, 1, cell < SIDE - 1)
        guess = (1.0 - OMEGA) * guess + weight * (source + beside)
    return guess


def nearby(coarse, member, rows_ref):
    rows_ref[...] = pltpu.roll(coarse, lax.rem((SIDE + 1 - member) * SIDE, WIDE), 1)[:, :LANES]


def smooth(slabs):
    total = slabs[1:9] + 0.5 * (slabs[0:8] + slabs[2:10])
    planes = []
    lane = iota((8, LANES), 1)
    row = iota((8, LANES), 0)
    for plane in range(8):
        own, ends = total[plane, :8], total[plane, 8:]
        before = jnp.where(row == 0, ends[LEFT - 8 :, :], pltpu.roll(own, 1, 0))
        after = jnp.where(row == 7, ends[:1, :], pltpu.roll(own, 7, 0))
        own = own + 0.5 * (before + after)
        below = jnp.where(lane > 0, pltpu.roll(own, 1, 1), 0.0)
        above = jnp.where(lane < LANES - 1, pltpu.roll(own, LANES - 1, 1), 0.0)
        planes.append(own + 0.5 * (below + above))
    return jnp.stack(planes)


def position():
    return lax.axis_index(COARSE), lax.axis_index(FINE)


def put_faces(field_ref, pieces_ref, rows, row, member):
    before, after = jnp.maximum(member - 1, 0), jnp.minimum(member + 1, SIDE - 1)
    pieces_ref[pl.ds(before * rows + row, 8), :] = field_ref[pl.ds(0, 8, stride=8), :]
    pieces_ref[pl.ds(after * rows + row, 8), :] = field_ref[pl.ds(7, 8, stride=8), :]


def within(left, right, member, outside):
    left = jnp.where(member > 0, left, outside)
    right = jnp.where(member < SIDE - 1, right, outside)
    return left, right


def get_faces(pieces_ref, rows, row, member, outside):
    before, after = jnp.maximum(member - 1, 0), jnp.minimum(member + 1, SIDE - 1)
    left = pieces_ref[pl.ds(before * rows + row, 8), :]
    right = pieces_ref[pl.ds(after * rows + row, 8), :]
    return within(left, right, member, outside)


def fill_slabs(slabs_ref, field_ref, faces, ends, outside):
    owner, member = position()
    left, right = faces
    gap = jnp.full((8, LANES), outside, F32)
    for plane in range(8):
        slabs_ref[plane + 1, :8, :] = field_ref[8 * plane : 8 * plane + 8, :]
        slabs_ref[plane + 1, 8:, :] = gap
        slabs_ref[plane + 1, RIGHT : RIGHT + 1, :] = right[plane : plane + 1, :]
        slabs_ref[plane + 1, LEFT : LEFT + 1, :] = left[plane : plane + 1, :]
    for plane, inside, (own, *halos) in (
        (0, owner > 0, ends[0]),
        (9, owner < SIDE - 1, ends[1]),
    ):
        slabs_ref[plane, 8:, :] = gap
        slabs_ref[plane, :8, :] = jnp.where(inside, own, outside)
        for target, halo in zip((LEFT, RIGHT), halos):
            slabs_ref[plane, target : target + 1, :] = jnp.where(inside, halo, outside)


def add_prolonged(slabs_ref, numbers_ref, rows_ref):
    owner, member = position()
    for plane in range(10):
        if plane == 0:
            there = jnp.maximum(owner - 1, 0)
        elif plane == 9:
            there = jnp.minimum(owner + 1, SIDE - 1)
        else:
            there = owner
        row = jnp.broadcast_to(rows_ref[pl.ds(there, 1), :], (8, LANES))
        for part in (0, 8):
            number = numbers_ref[plane, part : part + 8, :]
            value = take_lanes(row, jnp.maximum(number, 0))
            slabs_ref[plane, part : part + 8, :] += jnp.where(number >= 0, value, 0.0)


def operate(field, kappa):
    own, own_kappa = field[1:9, :8], kappa[1:9, :8]
    return own_kappa * (8.0 * own - smooth(field)) + own * smooth(kappa) - smooth(
        kappa * field
    )


def offsets(aggregate):
    return aggregate - iota((ROWS, LANES), 1) // AGG


FIELD, KAPPA, MAP, FACE_ROWS, PLANE_ROWS = 0, 8, 16, 24, 32
OUTSIDE = (0.0, 0.0, -1.0)
F_SOURCE_2, F_SECOND = 8, 9
C_HALO_2, C_SOURCE_2, C_SECOND = 8, 10, 12


def fetch_matrices(matrices_hbm, matrices_ref, arrived):
    part = ROWS // 4
    copies = [
        pltpu.make_async_copy(
            matrices_hbm.at[pl.ds(part * number, part)],
            matrices_ref.at[pl.ds(part * number, part)],
            arrived.at[number],
        )
        for number in range(4)
    ]
    for copy in copies:
        copy.start()
    return copies


def begin(
    table_hbm, side_hbm, index_hbm, order_hbm, matrices_hbm, map_hbm, diagonal_hbm,
    pieces_ref, pair_ref, cross_ref, kappa_ref, smoothed_ref, numbers_ref,
    table_ref, side_ref, index_ref, order_ref, map_ref, diagonal_ref, picked_ref, product_ref,
    matrices_ref, arrived, quarter_arrived,
):
    owner, member = position()
    copies = [
        pltpu.make_async_copy(source, target, arrived.at[number])
        for number, (source, target) in enumerate(
            (
                (order_hbm, order_ref),
                (side_hbm, side_ref),
                (table_hbm, table_ref),
                (index_hbm, index_ref),
                (map_hbm, map_ref),
                (diagonal_hbm, diagonal_ref),
            )
        )
    ]
    for copy in copies:
        copy.start()
    quarters = fetch_matrices(matrices_hbm, matrices_ref, quarter_arrived)
    copies[0].wait()
    for copy in copies[1:]:
        copy.wait()
    index = index_ref[...]
    kappa = jnp.zeros((ROWS, LANES), F32)
    for entry in range(table_ref.shape[0]):
        kappa = jnp.where(index == entry, table_ref[entry], kappa)
    kappa_ref[...] = kappa
    pick(side_ref, order_ref, picked_ref)
    for copy in quarters:
        copy.wait()
    multiply_blocks(matrices_ref, picked_ref, product_ref)
    put_back(product_ref, order_ref, smoothed_ref)
    aggregate = map_ref[...]
    numbers_ref[...] = aggregate.astype(F32)
    source = restrict(side_ref[...], offsets(aggregate), member)
    spread = jnp.broadcast_to(jnp.concatenate([diagonal_ref[...]] * 8, axis=1), (8, LANES))
    beside = iota((8, LANES), 1) // SIDE == (member + 1) % 8
    message = jnp.where(beside, spread, source)
    for start in range(0, WIDE, 8):
        pieces_ref[start : start + 8, :] = message
    for row, field_ref in ((FIELD, smoothed_ref), (KAPPA, kappa_ref), (MAP, numbers_ref)):
        left = field_ref[pl.ds(0, 8, stride=8), :]
        right = field_ref[pl.ds(7, 8, stride=8), :]
        even = member % 2 == 0
        pair_ref[row : row + 8, :] = jnp.where(even, right, left)
        cross_ref[row : row + 8, :] = jnp.where(even, left, right)


def put_all(values, pieces_ref, rows, row):
    for piece in range(SIDE):
        pieces_ref[piece * rows + row : piece * rows + row + 1, :] = values[0:1, :]


def put_planes(field_ref, faces, pieces, outside):
    owner, member = position()
    left, right = get_faces(*faces, member, outside)
    pieces_ref, rows, plane_row, halo_row = pieces
    for there, plane in (
        (jnp.maximum(owner - 1, 0), 0),
        (jnp.minimum(owner + 1, SIDE - 1), 7),
    ):
        start = there * rows
        pieces_ref[pl.ds(start + plane_row, 8), :] = field_ref[8 * plane : 8 * plane + 8, :]
        for side, halo in enumerate((left, right)):
            pieces_ref[pl.ds(start + halo_row + side, 1), :] = halo[plane : plane + 1, :]


def gathered(rows):
    place = iota((SIDE, LANES), 0) % 8
    rows = jnp.where(iota((SIDE, LANES), 1) // SIDE == place, rows, 0.0)
    return [jnp.sum(rows[at : at + 8], axis=0, keepdims=True) for at in (0, 8)]


def coarse_rows(pieces_ref, step):
    pieces = pieces_ref[...].reshape(SIDE, SIDE, LANES)
    place = (iota((SIDE, LANES), 0) + step) % 8
    kept = jnp.where((iota((SIDE, LANES), 1) // SIDE == place)[None], pieces, 0.0)
    halves_of = [jnp.sum(kept[:, :8], axis=1), jnp.sum(kept[:, 8:], axis=1)]
    if step:
        halves_of = [pltpu.roll(half, LANES - SIDE * step, 1) for half in halves_of]
    return jnp.concatenate(halves_of, axis=1)


def first_faces(pair_ref, cross_ref, row, member, outside):
    pair, cross = pair_ref[row : row + 8, :], cross_ref[row : row + 8, :]
    even = member % 2 == 0
    left, right = jnp.where(even, cross, pair), jnp.where(even, pair, cross)
    return within(left, right, member, outside)


def relay_first(
    pair_ref, cross_ref, smoothed_ref, kappa_ref, numbers_ref, before_ref, after_ref
):
    owner, member = position()
    fields = (smoothed_ref, kappa_ref, numbers_ref)
    for target_ref, plane in ((before_ref, 0), (after_ref, 7)):
        target_ref[FACE_ROWS:, :] = jnp.zeros((8, LANES), F32)
        for number, field_ref in enumerate(fields):
            row = 8 * number
            faces = first_faces(pair_ref, cross_ref, row, member, OUTSIDE[number])
            target_ref[row : row + 8, :] = field_ref[8 * plane : 8 * plane + 8, :]
            for side, face in enumerate(faces):
                halo = FACE_ROWS + 2 * number + side
                target_ref[halo : halo + 1, :] = face[plane : plane + 1, :]


def fill_first(slabs_ref, field_ref, pair_ref, cross_ref, before_ref, after_ref, number):
    owner, member = position()
    row, outside = 8 * number, OUTSIDE[number]
    halo = FACE_ROWS + 2 * number
    ends = [
        (end[row : row + 8, :], end[halo : halo + 1, :], end[halo + 1 : halo + 2, :])
        for end in (before_ref, after_ref)
    ]
    faces = first_faces(pair_ref, cross_ref, row, member, outside)
    fill_slabs(slabs_ref, field_ref, faces, ends, outside)


def fill_second(slabs_ref, field_ref, faces_ref, pieces_ref):
    owner, member = position()
    ends = []
    for there in (jnp.maximum(owner - 1, 0), jnp.minimum(owner + 1, SIDE - 1)):
        start = there * C_SECOND
        ends.append(
            (
                pieces_ref[pl.ds(start, 8), :],
                pieces_ref[pl.ds(start + C_HALO_2, 1), :],
                pieces_ref[pl.ds(start + C_HALO_2 + 1, 1), :],
            )
        )
    faces = get_faces(faces_ref, F_SECOND, 0, member, 0.0)
    fill_slabs(slabs_ref, field_ref, faces, ends, 0.0)


def halves(pieces_ref, rows, row):
    return jnp.concatenate(
        [pieces_ref[pl.ds(row + half, SIDE, stride=rows), :] for half in range(2)], axis=1
    )


def first_image(
    rows_of_all_ref, pair_ref, cross_ref, before_ref, after_ref,
    own_ref, own_kappa_ref, numbers_ref, map_ref, order_ref, matrices_hbm,
    pieces_ref, field_ref, image_ref, smoothed_ref, kappa_ref, lanes_ref, diagonal_ref,
    matrices_ref,
    picked_ref, product_ref, slabs_ref, rows_ref, arrived,
):
    owner, member = position()
    copies = fetch_matrices(matrices_hbm, matrices_ref, arrived)
    diagonal = coarse_rows(rows_of_all_ref, 1)
    diagonal_ref[...] = diagonal
    nearby(coarse_solve(coarse_rows(rows_of_all_ref, 0), diagonal), member, rows_ref)
    around = pair_ref, cross_ref, before_ref, after_ref
    fill_first(slabs_ref, numbers_ref, *around, 2)
    row = iota((10, SLAB, LANES), 1)
    shift = jnp.where(row < 8, SIDE, jnp.where(row == RIGHT, 2 * SIDE, 0))
    number = slabs_ref[...]
    lanes_ref[...] = jnp.where(number >= 0.0, number.astype(jnp.int32) + shift, -1)
    fill_first(kappa_ref, own_kappa_ref, *around, 1)
    fill_first(slabs_ref, own_ref, *around, 0)
    add_prolonged(slabs_ref, lanes_ref, rows_ref)
    field = slabs_ref[...]
    field_ref[...] = field[1:9, :8].reshape(ROWS, LANES)
    image_ref[...] = operate(field, kappa_ref[...]).reshape(ROWS, LANES)
    pick(image_ref, order_ref, picked_ref)
    for copy in copies:
        copy.wait()
    multiply_blocks(matrices_ref, picked_ref, product_ref)
    put_back(product_ref, order_ref, smoothed_ref)
    source = restrict(image_ref[...], offsets(map_ref[...]), member)
    put_all(source, pieces_ref, F_SECOND, F_SOURCE_2)
    put_faces(smoothed_ref, pieces_ref, F_SECOND, 0, member)


def relay_second(faces_ref, smoothed_ref, pieces_ref):
    rows = faces_ref[pl.ds(F_SOURCE_2, SIDE, stride=F_SECOND), :]
    for half, values in enumerate(gathered(rows)):
        put_all(values, pieces_ref, C_SECOND, C_SOURCE_2 + half)
    faces, pieces = (faces_ref, F_SECOND, 0), (pieces_ref, C_SECOND, 0, C_HALO_2)
    put_planes(smoothed_ref, faces, pieces, 0.0)


def second_image(
    faces_ref, ends_ref, own_ref, kappa_ref, lanes_ref, map_ref, order_ref,
    diagonal_ref, side_ref, first_ref, image_ref, matrices_ref,
    pieces_ref, field_ref, second_ref, product_ref,
    picked_ref, slabs_ref, rows_ref,
):
    owner, member = position()
    source = halves(ends_ref, C_SECOND, C_SOURCE_2)
    nearby(coarse_solve(source, diagonal_ref[...]), member, rows_ref)
    fill_second(slabs_ref, own_ref, faces_ref, ends_ref)
    add_prolonged(slabs_ref, lanes_ref, rows_ref)
    slabs = slabs_ref[...]
    field = slabs[1:9, :8].reshape(ROWS, LANES)
    field_ref[...] = field
    second = operate(slabs, kappa_ref[...]).reshape(ROWS, LANES)
    second_ref[...] = second
    pick(second_ref, order_ref, picked_ref)
    multiply_blocks(matrices_ref, picked_ref, product_ref)
    first = first_ref[...]
    image = image_ref[...]
    pairs = (
        side_ref[...] * first,
        first * image,
        image * field,
        second * first,
        second * field,
        picked_ref[...] * product_ref[...],
    )
    lane = iota((8, LANES), 1)
    message = restrict(second, offsets(map_ref[...]), member)
    beside = lax.rem(member + 1, 8) * SIDE
    for number, pair in enumerate(pairs):
        total = jnp.sum(jnp.sum(pair, axis=0, keepdims=True), axis=1, keepdims=True)
        message = jnp.where(lane == beside + number, total, message)
    for start in range(0, WIDE, 8):
        pieces_ref[start : start + 8, :] = message


def finish(
    pieces_ref, diagonal_ref, map_ref, side_ref, first_ref, image_ref, field_ref, second_ref,
    smoothed_ref,
    solution_ref, residual_ref, search_ref,
):
    owner, member = position()
    pieces = pieces_ref[...].reshape(SIDE, SIDE, LANES)
    place = iota((SIDE, LANES), 0) % 8
    group = iota((SIDE, LANES), 1) // SIDE
    pieces_sum = jnp.sum(pieces, axis=0)
    sums = jnp.where(group == (place + 1) % 8, pieces_sum, 0.0)
    source = coarse_rows(pieces_ref, 0)
    coarse = coarse_solve(source, diagonal_ref[...])
    lane = iota((1, LANES), 1)
    sums = jnp.sum(sums, axis=0, keepdims=True)

    def total(number):
        picked = jnp.where(lane % SIDE == number, sums, 0.0)
        return jnp.sum(picked, axis=1, keepdims=True)

    def whole(array):
        return jnp.sum(jnp.sum(array, axis=0, keepdims=True), axis=1, keepdims=True)

    r_z, z_az, w_y, v_z, v_y, v_bv = (total(number) for number in range(6))
    v_u = v_bv + 4.0 * whole(source * coarse)
    alpha = r_z / z_az
    following = r_z - 2.0 * alpha * z_az + alpha * alpha * w_y
    grown = 1.0 + following / r_z
    product = grown * grown * z_az - grown * alpha * (v_z + w_y) + alpha * alpha * v_y
    again = following / product
    one = alpha + again * grown
    two = again * alpha
    last = (
        r_z - 2.0 * one * z_az + 2.0 * two * v_z + one * one * w_y
        - 2.0 * one * two * v_y + two * two * v_u
    )
    ratio = last / following
    lanes = iota((SIDE, WIDE), 1)
    rows = iota((SIDE, WIDE), 0)
    near = pltpu.roll(coarse, lax.rem((SIDE - member) * SIDE, WIDE), 1)[:, :LANES]
    row = jnp.sum(
        jnp.where(iota((SIDE, LANES), 0) == owner, near, 0.0), axis=0, keepdims=True
    )
    row = jnp.broadcast_to(row, (8, LANES))
    for g in range(8):
        at = slice(8 * g, 8 * g + 8)
        first, image, field, second = (
            ref[at, :] for ref in (first_ref, image_ref, field_ref, second_ref)
        )
        smoothed = smoothed_ref[at, :] + take_lanes(row, map_ref[at, :])
        solution_ref[at, :] = one * first - two * field
        residual_ref[at, :] = side_ref[at, :] - one * image + two * second
        search_ref[at, :] = (
            first - one * field + two * smoothed + ratio * (grown * first - alpha * field)
        )


def shards(
    right_side, coefficient_index, material_coefficients, block_cells, block_inverses,
    aggregate_map, coarse_diagonal,
):
    dims = right_side.shape
    side = right_side.reshape(ROWS, LANES)
    index = coefficient_index.reshape(ROWS, LANES)
    order = block_cells.reshape(ROWS, LANES)
    matrices = block_inverses.reshape(ROWS, LANES, LANES)
    aggregate = aggregate_map.reshape(ROWS, LANES)
    diagonal = coarse_diagonal.reshape(1, SIDE)
    local = shape(ROWS, LANES)
    cells = pltpu.VMEM((ROWS, LANES), F32)
    int_cells = pltpu.VMEM((ROWS, LANES), jnp.int32)
    scratch = [
        cells, cells, pltpu.VMEM((10, SLAB, LANES), F32), pltpu.VMEM((SIDE, LANES), F32),
    ]

    def call(kernel, outs, ins, scratch=(), specs=None):
        return pl.pallas_call(
            kernel,
            out_shape=outs,
            in_specs=specs or [vmem()] * ins,
            out_specs=[vmem()] * len(outs),
            scratch_shapes=list(scratch),
            compiler_params=params(),
            cost_estimate=pl.CostEstimate(
                flops=10**9, bytes_accessed=4 * 10**6, transcendentals=0
            ),
        )

    def exchange(pieces, axis):
        rows = pieces.shape
        pieces = lax.all_to_all(pieces.reshape(rows[0], 1, LANES), axis, 0, 0, tiled=True)
        return pieces.reshape(rows)

    def ring(rows, axis, step):
        return lax.ppermute(rows, axis, [(i, (i + step) % SIDE) for i in range(SIDE)])

    fixed = [
        pltpu.with_memory_space_constraint(array, pltpu.HBM)
        for array in (material_coefficients, side, index, order, matrices, aggregate, diagonal)
    ]
    pieces, pair, cross, kappa, smoothed, numbers = call(
        begin,
        [
            shape(WIDE, LANES), shape(FACE_ROWS, LANES), shape(FACE_ROWS, LANES), local, local,
            local,
        ],
        7,
        [
            pltpu.SMEM(material_coefficients.shape, F32), cells, int_cells, int_cells,
            int_cells, pltpu.VMEM((1, SIDE), F32), cells, cells,
            pltpu.VMEM(matrices.shape, F32), pltpu.SemaphoreType.DMA((6,)), pltpu.SemaphoreType.DMA((4,)),
        ],
        [hbm()] * 7,
    )(*fixed)
    pair = lax.ppermute(pair, FINE, [(i, i ^ 1) for i in range(SIDE)])
    cross = lax.ppermute(
        cross, FINE, [(i, (i + (1 if i % 2 else -1)) % SIDE) for i in range(SIDE)]
    )
    rows = exchange(pieces, (COARSE, FINE))
    before, after = call(
        relay_first, [shape(PLANE_ROWS, LANES), shape(PLANE_ROWS, LANES)], 5
    )(pair, cross, smoothed, kappa, numbers)
    after, before = ring(before, COARSE, -1), ring(after, COARSE, 1)
    pieces, first, image, smoothed, kappa, lanes, diagonals, matrices = call(
        first_image,
        [
            shape(SIDE * F_SECOND, LANES), local, local, local, shape(10, SLAB, LANES),
            shape(10, SLAB, LANES, dtype=jnp.int32), shape(SIDE, WIDE),
            pltpu.VMEM(matrices.shape, F32),
        ],
        11,
        scratch + [pltpu.SemaphoreType.DMA((4,))],
        [vmem()] * 10 + [hbm()],
    )(
        rows, pair, cross, before, after, smoothed, kappa, numbers, aggregate, order, fixed[4]
    )
    matrices = pltpu.with_memory_space_constraint(matrices, pltpu.VMEM)
    faces = exchange(pieces, FINE)
    (pieces,) = call(relay_second, [shape(SIDE * C_SECOND, LANES)], 2)(faces, smoothed)
    ends = exchange(pieces, COARSE)
    pieces, field, second, product = call(
        second_image,
        [shape(WIDE, LANES), local, local, local],
        12,
        scratch[:1] + scratch[2:],
    )(
        faces, ends, smoothed, kappa, lanes, aggregate, order, diagonals, side, first,
        image, matrices,
    )
    pieces = exchange(pieces, (COARSE, FINE))
    (smoothed,) = call(put_back, [local], 2)(product, order)
    results = call(finish, [local, local, local], 9)(
        pieces, diagonals, aggregate, side, first, image, field, second, smoothed
    )
    return tuple(result.reshape(dims) for result in results)


def solution(mesh):
    cells = P(COARSE, FINE, None)
    in_specs = (
        cells,
        cells,
        P(),
        P(COARSE, FINE, None, None),
        P(COARSE, FINE, None, None, None),
        cells,
        cells,
    )
    return jax.shard_map(
        shards, mesh=mesh, in_specs=in_specs, out_specs=(cells,) * 3, check_vma=False
    )
```
